256 devices in a mesh: seq: 64 (over x_hi, y, z), head: 4 (over x_lo, core).
Axes of the slice: x: 4 (x_hi: 2, x_lo: 2; x = x_hi * 2 + x_lo), y: 4, z: 8, core: 2. Of those that a mesh axis runs over, the one named last changes fastest.
Arguments:
- query_fine: bfloat16 [8192, 1024], P('seq', 'head'), may hold values from -6 to 6
- key_fine: bfloat16 [8192, 1024], P('seq', 'head'), may hold values from -6 to 6
- value_fine: bfloat16 [8192, 1024], P('seq', 'head'), may hold values from -6 to 6
- query_coarse: bfloat16 [256, 1024], P(None, 'head'), may hold values from -6 to 6
- key_coarse: bfloat16 [256, 1024], P(None, 'head'), may hold values from -6 to 6
- value_coarse: bfloat16 [256, 1024], P(None, 'head'), may hold values from -6 to 6
- out_weight: bfloat16 [1024, 1920], P('head'), may hold values from -0.1875 to 0.1875
- grad_fine: bfloat16 [8192, 1920], P('seq', 'head'), may hold values from -6 to 6
- grad_coarse: bfloat16 [256, 1920], P(None, 'head'), may hold values from -6 to 6
- fine_scale: int32 [8192], replicated, may hold values from 0 to 2, never falling along the last dimension, each value on 1 to 4096 neighbouring positions
- coarse_scale: int32 [256], replicated, may hold values from 0 to 3, never falling along the last dimension, each value on 1 to 128 neighbouring positions
Outputs:
- mixed_fine: bfloat16 [8192, 1920], P('seq', 'head')
- mixed_coarse: bfloat16 [256, 1920], P(None, 'head')
- query_grad_fine: bfloat16 [8192, 1024], P('seq', 'head')
- key_grad_fine: bfloat16 [8192, 1024], P('seq', 'head')
- value_grad_fine: bfloat16 [8192, 1024], P('seq', 'head')
- query_grad_coarse: bfloat16 [256, 1024], P(None, 'head')
- key_grad_coarse: bfloat16 [256, 1024], P(None, 'head')
- value_grad_coarse: bfloat16 [256, 1024], P(None, 'head')
The draws below stay inside these ranges and needn't reach their ends.
All inputs are finite; a program needn't handle non-finite values.
Results may differ from the reference program's by a relative error of at most 0.035.
Values may be sent and summed in bfloat16 or wider, within the bound.
No kernel may reach another device: no remote copies, remote signals or barrier semaphores. Data moves between devices by JAX's collectives and lax.ppermute only.
A program may use at most 128 MiB of HBM per device.

```python
import math
import jax
import jax.numpy as jnp
import numpy as np
from jax import lax

D = 1920
HEAD_SIZE = 64
HEADS = 16
HD = 1024
COARSE = 256
CSCALES = 4
FSCALES = 3
FINE = 8192


def normal_rows(key, row_total):
    return jnp.clip(1.6 * jax.random.normal(key, (row_total, HEADS * HEAD_SIZE), jnp.float32), -6.0, 6.0)


def draw_query_fine(key, part):
    key = jax.random.fold_in(key, 11)
    return normal_rows(key, FINE).astype(jnp.bfloat16)


def draw_query_coarse(key, part):
    key = jax.random.fold_in(key, 23)
    return normal_rows(key, COARSE).astype(jnp.bfloat16)


def draw_key_coarse(key, part):
    key = jax.random.fold_in(key, 31)
    return normal_rows(key, COARSE).astype(jnp.bfloat16)


def steps_of(key, dims, pieces, low, top_value):
    level, own = 1.0, jax.random.fold_in(key, 6)
    for position, parts in pieces:
        heights = jnp.exp(jax.random.uniform(jax.random.fold_in(own, position), (parts,), jnp.float32, low / len(pieces), top_value / len(pieces)))
        level = level * jnp.repeat(heights, dims[position] // parts).reshape([-1 if axis == position else 1 for axis in range(len(dims))])
    return level


def profile(count, total, bound, lean):
    portions = [(1 << 20) // math.isqrt(standing ** lean) + 1 for standing in range(2, count + 1)]
    spare, counts = total - bound - (count - 1), [1] * (count - 1)
    while spare > 0:
        movable = [i for i in range(count - 1) if counts[i] < bound]
        mass, remaining = sum([portions[i] for i in movable]), spare
        for i in movable:
            more = min(bound - counts[i], max(1, remaining * portions[i] // mass), spare)
            counts[i] = counts[i] + more
            spare = spare - more
    return np.array([bound] + counts)


def uneven(own_key, number_of, total, limit, skew):
    if number_of == 2:
        one = jax.random.randint(own_key, (), max(1, total - limit), min(limit, total - 1) + 1)
        return jnp.stack([one, total - one])
    sizes = jnp.asarray(profile(number_of, total, limit, skew), jnp.int32)
    twos = (number_of - 1) // 2
    giver, sink = sizes[1:1 + 2 * twos:2], sizes[2:2 + 2 * twos:2]
    room = jnp.minimum(giver - 1, limit - sink)
    moved = jax.random.randint(jax.random.fold_in(own_key, 1), (twos,), 0, 1 << 20) % (room + 1)
    sizes = sizes.at[1:1 + 2 * twos:2].set(giver - moved).at[2:2 + 2 * twos:2].set(sink + moved)
    return sizes[jax.random.permutation(jax.random.fold_in(own_key, 2), number_of)]


def noise(rng, shape, deviation, most, split=(), kind=jnp.bfloat16):
    array = deviation * jax.random.normal(rng, shape, jnp.float32)
    if split:
        array = array * steps_of(rng, shape, split, -0.22, 0.18)
    return jnp.clip(array, -most, most).astype(kind)


def setup_inputs(seed: int = 0) -> dict:
    arg_keys = jax.random.split(jax.random.key(seed), 12)
    query_fine = draw_query_fine(jax.random.fold_in(arg_keys[11], 71), 0)
    key_fine = noise(arg_keys[1], (FINE, HD), 1.6, 6.0, ((0, 64), (1, 4)))
    value_fine = noise(arg_keys[2], (FINE, HD), 1.0, 6.0, ((0, 64), (1, 4)))
    query_coarse = draw_query_coarse(jax.random.fold_in(arg_keys[11], 71), 0)
    key_coarse = draw_key_coarse(jax.random.fold_in(arg_keys[11], 71), 0)
    value_coarse = noise(arg_keys[5], (COARSE, HD), 1.0, 6.0, ((1, 4),))
    out_weight = noise(arg_keys[6], (HD, D), HD ** -0.5, 0.1875, ((0, 4),))
    grad_fine = noise(arg_keys[7], (FINE, D), 1.0, 6.0, ((0, 64), (1, 4)))
    grad_coarse = noise(arg_keys[8], (COARSE, D), 1.0, 6.0, ((1, 4),))
    fine_scale = jnp.searchsorted(jnp.cumsum(uneven(arg_keys[9], FSCALES, FINE, FINE // 2, 0)), jnp.arange(FINE), side="right").astype(jnp.int32)
    coarse_scale = jnp.searchsorted(jnp.cumsum(uneven(arg_keys[10], CSCALES, COARSE, COARSE // 2, 0)), jnp.arange(COARSE), side="right").astype(jnp.int32)
    return dict(query_fine=query_fine, key_fine=key_fine, value_fine=value_fine, query_coarse=query_coarse, key_coarse=key_coarse, value_coarse=value_coarse, out_weight=out_weight, grad_fine=grad_fine, grad_coarse=grad_coarse, fine_scale=fine_scale, coarse_scale=coarse_scale)


def head_major(matrix):
    return matrix.reshape(matrix.shape[0], HEADS, HEAD_SIZE).transpose(1, 0, 2)


def token_major(tensor):
    return tensor.transpose(1, 0, 2).reshape(tensor.shape[1], HEADS * HEAD_SIZE)


def head_probs(query_head, key_head, token_ids):
    raw_scores = jnp.dot(query_head, key_head.T, preferred_element_type=jnp.float32) * (HEAD_SIZE ** -0.5)
    visible = token_ids[None, :] <= token_ids[:, None]
    kept = jnp.where(visible, raw_scores, -jnp.inf)
    top_score = jnp.max(kept, axis=1, keepdims=True)
    log_total = top_score + jnp.log(jnp.sum(jnp.exp(kept - top_score), axis=1, keepdims=True))
    return jnp.where(visible, jnp.exp(raw_scores - log_total), 0.0)


def reference(query_fine, key_fine, value_fine, query_coarse, key_coarse, value_coarse, out_weight, grad_fine, grad_coarse, fine_scale, coarse_scale):
    token_ids = jnp.concatenate([coarse_scale.astype(jnp.int32), (fine_scale + CSCALES).astype(jnp.int32)])
    queries = head_major(jnp.concatenate([query_coarse, query_fine]))
    keys = head_major(jnp.concatenate([key_coarse, key_fine]))
    values = head_major(jnp.concatenate([value_coarse, value_fine]))

    def forward(operands):
        query_head, key_head, value_head = operands
        probs = head_probs(query_head, key_head, token_ids)
        return jnp.dot(probs.astype(jnp.bfloat16), value_head, preferred_element_type=jnp.float32).astype(jnp.bfloat16)

    attended = token_major(lax.map(forward, (queries, keys, values)))
    mixed = jnp.dot(attended, out_weight, preferred_element_type=jnp.float32).astype(jnp.bfloat16)
    grads = jnp.concatenate([grad_coarse, grad_fine])
    back = jnp.dot(grads, out_weight.T, preferred_element_type=jnp.float32).astype(jnp.bfloat16)

    def backward(operands):
        query_head, key_head, value_head, back_head, attended_head = operands
        probs = head_probs(query_head, key_head, token_ids)
        offset = jnp.sum(back_head.astype(jnp.float32) * attended_head.astype(jnp.float32), axis=1, keepdims=True)
        grad_probs = jnp.dot(back_head, value_head.T, preferred_element_type=jnp.float32)
        grad_scores = (probs * (grad_probs - offset)).astype(jnp.bfloat16)
        query_grad = jnp.dot(grad_scores, key_head, preferred_element_type=jnp.float32) * (HEAD_SIZE ** -0.5)
        key_grad = jnp.dot(grad_scores.T, query_head, preferred_element_type=jnp.float32) * (HEAD_SIZE ** -0.5)
        value_grad = jnp.dot(probs.astype(jnp.bfloat16).T, back_head, preferred_element_type=jnp.float32)
        return query_grad.astype(jnp.bfloat16), key_grad.astype(jnp.bfloat16), value_grad.astype(jnp.bfloat16)

    query_grad, key_grad, value_grad = lax.map(backward, (queries, keys, values, head_major(back), head_major(attended)))
    query_grad = token_major(query_grad)
    key_grad = token_major(key_grad)
    value_grad = token_major(value_grad)
    return (mixed[COARSE:], mixed[:COARSE], query_grad[COARSE:], key_grad[COARSE:], value_grad[COARSE:], query_grad[:COARSE], key_grad[:COARSE], value_grad[:COARSE])
```

```python
import jax
import jax.numpy as jnp
from jax import lax
from jax.experimental import pallas as pl
from jax.experimental.pallas import tpu as pltpu
from jax.sharding import Mesh
from jax.sharding import PartitionSpec as P

HEAD_SIZE = 64
SCALE = HEAD_SIZE ** (-0.5)
FSCALES = 3
HIDE = -30000.0
PIECE = 128
PIECES = 16
QUERY_BLOCKS = 4
QUERY_BLOCK = 512
STEP = 2
F32 = jnp.float32
BF16 = jnp.bfloat16

SEQ = ("xh", "yh", "yl", "zc", "zb", "za")
QUERY_GROUP = ("xh", "yh", "yl", "za")
KEY_GROUP = ("xh", "yh", "zc", "zb")
KEY_TILES = ("yl", "za")


def product(left, right):
    return jnp.dot(left, right, preferred_element_type=F32)


def product_nt(left, right):
    return lax.dot_general(left, right, (((1,), (1,)), ((), ())), preferred_element_type=F32)


def product_tn(left, right):
    return lax.dot_general(left, right, (((0,), (0,)), ((), ())), preferred_element_type=F32)


def call(kernel, outs, scratch=(), smem=0, flops=0, moved=0, exps=0):
    def run(*operands):
        return pl.pallas_call(
            kernel,
            out_shape=outs,
            in_specs=[pl.BlockSpec(memory_space=pltpu.SMEM)] * smem
            + [pl.BlockSpec(memory_space=pltpu.VMEM)] * (len(operands) - smem),
            out_specs=jax.tree.map(lambda _: pl.BlockSpec(memory_space=pltpu.VMEM), outs),
            scratch_shapes=list(scratch),
            compiler_params=pltpu.CompilerParams(vmem_limit_bytes=48 * 2**20),
            cost_estimate=pl.CostEstimate(
                flops=flops, bytes_accessed=moved, transcendentals=exps
            ),
        )(*operands)

    return run


def shape(*dims, dtype=BF16):
    return jax.ShapeDtypeStruct(dims, dtype)


def pack_keys_kernel(key_ref, value_ref, out_ref):
    for head in range(4):
        cols = slice(head * HEAD_SIZE, (head + 1) * HEAD_SIZE)
        both = jnp.concatenate([key_ref[:, cols], value_ref[:, cols]], axis=1)
        for other in range(4):
            out_ref[4 * head + other] = both


def pack_queries_kernel(query_ref, grad_ref, weight_ref, out_ref):
    back = product_nt(weight_ref[...], grad_ref[...]).astype(BF16)
    query = (query_ref[...].astype(F32) * SCALE).T.astype(BF16)
    for head in range(4):
        rows = slice(head * HEAD_SIZE, (head + 1) * HEAD_SIZE)
        both = jnp.concatenate([query[rows], back[rows]], axis=0)
        for other in range(4):
            out_ref[4 * head + other] = both


def prepare_keys(kv_ref, onehot_ref, masked_keys, turned):
    lane = lax.broadcasted_iota(jnp.int32, (PIECE, PIECE), 1)
    for piece in range(PIECES):
        both = kv_ref[piece]
        masked_keys[piece] = jnp.where(lane < HEAD_SIZE, both, onehot_ref[piece])
        turned[piece] = both.astype(F32).T.astype(BF16)


def query_side(qb_ref, ids_ref, block):
    both = jnp.concatenate([qb_ref[4 * block + part] for part in range(4)], axis=1)
    row = lax.broadcasted_iota(jnp.int32, (HEAD_SIZE, QUERY_BLOCK), 0)
    hidden = (row > ids_ref[block]) & (row < FSCALES)
    penalty = jnp.where(hidden, HIDE, 0.0).astype(BF16)
    return both, jnp.concatenate([both[:HEAD_SIZE], penalty], axis=0)


def rows_of(ref, step):
    return ref[pl.ds(STEP * step, STEP)].reshape(STEP * PIECE, PIECE)


def turned_of(ref, step, first):
    return jnp.concatenate(
        [ref[STEP * step + part, first:first + HEAD_SIZE, :] for part in range(STEP)], axis=1
    )


def coarse_side(kvc_ref):
    both = kvc_ref[...]
    lane = lax.broadcasted_iota(jnp.int32, both.shape, 1)
    only_keys = jnp.where(lane < HEAD_SIZE, both, jnp.zeros_like(both))
    return both, only_keys, both.astype(F32).T.astype(BF16)


def forward_kernel(steps_ref, kv_ref, onehot_ref, kvc_ref, qb_ref, ids_ref, out_ref, stats_ref, masked_keys, turned):
    prepare_keys(kv_ref, onehot_ref, masked_keys, turned)
    _, coarse_keys, coarse_turned = coarse_side(kvc_ref)

    def one_block(block, _):
        both, queries = query_side(qb_ref, ids_ref, block)
        scores = product(coarse_keys, queries)
        top = jnp.max(scores, axis=0, keepdims=True)
        probs = jnp.exp(scores - top)
        total = jnp.sum(probs, axis=0, keepdims=True)
        accum = product(coarse_turned[HEAD_SIZE:], probs.astype(BF16))

        def one_step(step, carried):
            top, total, accum = carried
            scores = product(rows_of(masked_keys, step), queries)
            new_top = jnp.maximum(top, jnp.max(scores, axis=0, keepdims=True))
            fade = jnp.exp(top - new_top)
            probs = jnp.exp(scores - new_top)
            total = total * fade + jnp.sum(probs, axis=0, keepdims=True)
            accum = accum * fade + product(turned_of(turned, step, HEAD_SIZE), probs.astype(BF16))
            return new_top, total, accum

        top, total, accum = lax.fori_loop(0, steps_ref[block], one_step, (top, total, accum))
        offset = jnp.sum(both[HEAD_SIZE:].astype(F32) * accum, axis=0, keepdims=True)
        out_ref[block] = accum
        stats_ref[block] = jnp.concatenate(
            [top, total, offset, jnp.zeros((5, QUERY_BLOCK), F32)], axis=0
        )
        return 0

    lax.fori_loop(0, QUERY_BLOCKS, one_block, 0)


def backward_kernel(
    steps_ref, kv_ref, onehot_ref, kvc_ref, qb_ref, ids_ref, accum_ref, own_ref, stats_ref, od_ref, dkv_ref,
    masked_keys, turned, key_sums, coarse_sums,
):
    prepare_keys(kv_ref, onehot_ref, masked_keys, turned)
    coarse_both, coarse_keys, coarse_turned = coarse_side(kvc_ref)
    key_sums[...] = jnp.zeros_like(key_sums)
    coarse_sums[...] = jnp.zeros_like(coarse_sums)

    def one_block(block, _):
        both, queries = query_side(qb_ref, ids_ref, block)
        stats = [stats_ref[source, block] for source in range(4)]
        top = stats[0][0:1]
        for other in stats[1:]:
            top = jnp.maximum(top, other[0:1])
        total = jnp.zeros_like(top)
        offset = jnp.zeros_like(top)
        for other in stats:
            fade = jnp.exp(other[0:1] - top)
            total = total + fade * other[1:2]
            offset = offset + fade * other[2:3]
        offset = offset / total
        log_total = top + jnp.log(total)
        attended = accum_ref[block] * (jnp.exp(own_ref[block][0:1] - top) / total)
        back = jnp.concatenate(
            [jnp.zeros((HEAD_SIZE, QUERY_BLOCK), BF16), both[HEAD_SIZE:]], axis=0
        )
        token_rows = both.astype(F32).T
        lane = lax.broadcasted_iota(jnp.int32, token_rows.shape, 1)
        query_rows = jnp.where(lane < HEAD_SIZE, token_rows, 0.0).astype(BF16)
        back_rows = jnp.where(lane < HEAD_SIZE, 0.0, token_rows).astype(BF16)

        def terms(only_keys, key_value, key_turned):
            probs = jnp.exp(product(only_keys, queries) - log_total)
            grad_probs = product(key_value, back)
            grad_scores = (probs * (grad_probs - offset)).astype(BF16)
            key_side = product(grad_scores, query_rows) + product(probs.astype(BF16), back_rows)
            return product(key_turned, grad_scores), key_side

        query_grad, coarse_term = terms(coarse_keys, coarse_both, coarse_turned[:HEAD_SIZE])
        coarse_sums[...] += coarse_term

        def one_step(step, query_grad):
            query_term, key_side = terms(
                rows_of(masked_keys, step), rows_of(kv_ref, step), turned_of(turned, step, 0)
            )
            key_sums[pl.ds(STEP * step, STEP)] += key_side.reshape(STEP, PIECE, PIECE)
            return query_grad + query_term

        query_grad = lax.fori_loop(0, steps_ref[block], one_step, query_grad)
        both_out = jnp.concatenate([attended, query_grad * SCALE], axis=0).astype(BF16)
        for part in range(4):
            od_ref[4 * block + part] = both_out[:, part * PIECE:(part + 1) * PIECE]
        return 0

    lax.fori_loop(0, QUERY_BLOCKS, one_block, 0)
    dkv_ref[:, :PIECE, :] = key_sums[...].astype(BF16)
    coarse = coarse_sums[...].astype(BF16)
    for piece in range(PIECES):
        dkv_ref[piece, PIECE:, :] = coarse


def coarse_kernel(
    query_ref, key_ref, value_ref, grad_ref, weight_ref, bias_ref, att_ref, dq_ref, dk_ref, dv_ref
):
    back_all = product_nt(weight_ref[...], grad_ref[...]).astype(BF16)
    query_grads, attended_all, key_grads, value_grads = [], [], [], []
    for head in range(4):
        cols = slice(head * HEAD_SIZE, (head + 1) * HEAD_SIZE)
        query = (query_ref[:, cols].astype(F32) * SCALE).astype(BF16)
        key, value, back = key_ref[:, cols], value_ref[:, cols], back_all[cols]
        scores = product_nt(key, query) + bias_ref[...]
        top = jnp.max(scores, axis=0, keepdims=True)
        total = jnp.sum(jnp.exp(scores - top), axis=0, keepdims=True)
        probs = jnp.exp(scores - (top + jnp.log(total)))
        rounded = probs.astype(BF16)
        attended = product_tn(value, rounded).astype(BF16)
        offset = jnp.sum(back.astype(F32) * attended.astype(F32), axis=0, keepdims=True)
        grad_scores = (probs * (product(value, back) - offset)).astype(BF16)
        query_grads.append(product_tn(key, grad_scores) * SCALE)
        key_grads.append(product(grad_scores, query))
        value_grads.append(product_nt(rounded, back))
        attended_all.append(attended)
    att_ref[...] = jnp.concatenate(attended_all, axis=0)
    dq_ref[...] = jnp.concatenate(query_grads, axis=0).T.astype(BF16)
    dk_ref[...] = jnp.concatenate(key_grads, axis=1)
    dv_ref[...] = jnp.concatenate(value_grads, axis=1)


def query_sums_kernel(parts_ref, att_ref, dq_ref):
    grads = []
    for head in range(4):
        summed = sum(parts_ref[4 * head + part].astype(F32) for part in range(4))
        att_ref[head * HEAD_SIZE:(head + 1) * HEAD_SIZE, :] = summed[:HEAD_SIZE].astype(BF16)
        grads.append(summed[HEAD_SIZE:])
    dq_ref[...] = jnp.concatenate(grads, axis=0).T.astype(BF16)


def key_sums_kernel(parts_ref, dk_ref, dv_ref, coarse_ref):
    keys, values = [], []
    for head in range(4):
        summed = sum(parts_ref[4 * head + part].astype(F32) for part in range(4))
        keys.append(summed[:PIECE, :HEAD_SIZE])
        values.append(summed[:PIECE, HEAD_SIZE:])
        coarse_ref[head] = summed[PIECE:].astype(BF16)
    dk_ref[...] = jnp.concatenate(keys, axis=1).astype(BF16)
    dv_ref[...] = jnp.concatenate(values, axis=1).astype(BF16)


def coarse_sums_kernel(parts_ref, dk_ref, dv_ref, dk_out, dv_out):
    for tile in range(4):
        rows = slice(tile * 64, (tile + 1) * 64)
        parts = [parts_ref[tile, head].astype(F32) for head in range(4)]
        keys = jnp.concatenate([part[:, :HEAD_SIZE] for part in parts], axis=1)
        values = jnp.concatenate([part[:, HEAD_SIZE:] for part in parts], axis=1)
        dk_out[rows, :] = (dk_ref[rows, :] + keys).astype(BF16)
        dv_out[rows, :] = (dv_ref[rows, :] + values).astype(BF16)


def exchange(array, group):
    return lax.all_to_all(array, group, 0, 0, tiled=True)


def on_device(
    query_fine, key_fine, value_fine, query_coarse, key_coarse, value_coarse,
    out_weight, grad_fine, grad_coarse, fine_scale, coarse_scale,
):
    place = {name: lax.axis_index(name) for name in SEQ}
    head_of = place["xh"] * 2 + place["yh"]
    tile_of = place["yl"] * 2 + place["za"]

    packed_kv = call(pack_keys_kernel, shape(PIECES, PIECE, PIECE), moved=2**20)(key_fine, value_fine)
    kv = exchange(packed_kv, KEY_GROUP)

    wide = jnp.concatenate([out_weight, grad_coarse], axis=1)
    wide_all = lax.all_gather(wide, "head", axis=0, tiled=False)
    full_grad = lax.all_gather(grad_fine, "head", axis=1, tiled=True)
    packed_q = call(pack_queries_kernel, shape(PIECES, PIECE, PIECE), flops=2 * 128 * 256 * 1920, moved=2**21)(
        query_fine, full_grad, out_weight
    )
    qb = exchange(packed_q, QUERY_GROUP)

    ids = fine_scale.reshape(2, 2, 2, 2, 2, 2, PIECE)
    query_ids = lax.dynamic_index_in_dim(ids, place["zc"], 3, keepdims=False)
    query_ids = lax.dynamic_index_in_dim(query_ids, place["zb"], 3, keepdims=False)
    query_ids = query_ids.reshape(QUERY_BLOCKS, 1, QUERY_BLOCK)
    key_ids = lax.dynamic_index_in_dim(ids, place["yl"], 2, keepdims=False)
    key_ids = lax.dynamic_index_in_dim(key_ids, place["za"], 4, keepdims=False)
    key_ids = key_ids.reshape(PIECES, PIECE)
    lane = lax.broadcasted_iota(jnp.int32, (PIECES, PIECE, PIECE), 2)
    onehot = (lane - HEAD_SIZE == key_ids[:, :, None]).astype(BF16)
    seen = jnp.sum(key_ids[None, :, 0] <= query_ids[:, 0, -1:], axis=1)
    steps = ((seen + STEP - 1) // STEP).astype(jnp.int32)

    coarse_rows = [
        lax.dynamic_slice(array, (tile_of * 64, 0), (64, 256)).reshape(64, 4, HEAD_SIZE)
        for array in (key_coarse, value_coarse)
    ]
    kvc = jnp.concatenate(
        [lax.dynamic_index_in_dim(rows, head_of, 1, keepdims=False) for rows in coarse_rows], axis=1
    )

    half = [pltpu.VMEM((PIECES, PIECE, PIECE), BF16)] * 2
    accum, stats = call(
        forward_kernel,
        (shape(QUERY_BLOCKS, HEAD_SIZE, QUERY_BLOCK, dtype=F32), shape(QUERY_BLOCKS, 8, QUERY_BLOCK, dtype=F32)),
        half, 1, 4 * 2048 * 2112 * 64, 2**21, 2048 * 2112,
    )(steps, kv, onehot, kvc, qb, query_ids)
    stats_all = lax.all_gather(stats, KEY_TILES, axis=0, tiled=False)
    od, dkv = call(
        backward_kernel,
        (shape(PIECES, PIECE, PIECE), shape(PIECES, PIECE + 64, PIECE)),
        half + [pltpu.VMEM((PIECES, PIECE, PIECE), F32), pltpu.VMEM((64, PIECE), F32)],
        1, 10 * 2048 * 2112 * 64, 2**22, 2048 * 2112,
    )(steps, kv, onehot, kvc, qb, query_ids, accum, stats, stats_all)

    dkv_parts = exchange(dkv, KEY_GROUP)
    od_parts = exchange(od, QUERY_GROUP)

    full_coarse = jnp.concatenate([wide_all[part, :, 1920:] for part in range(4)], axis=1)
    own_head = lax.axis_index("head")
    columns = lax.dynamic_slice(wide_all, (0, 0, own_head * 480), (4, 256, 480)).reshape(1024, 480)
    bias = jnp.where(coarse_scale[:, None] <= coarse_scale[None, :], 0.0, -1e9).astype(F32)
    att_coarse, dq_coarse, dk_coarse, dv_coarse = call(
        coarse_kernel,
        (shape(256, 256), shape(256, 256), shape(256, 256, dtype=F32), shape(256, 256, dtype=F32)),
        flops=2**29, moved=2**22, exps=2**19,
    )(query_coarse, key_coarse, value_coarse, full_coarse, out_weight, bias)

    att_fine, dq_fine = call(query_sums_kernel, (shape(256, PIECE), shape(PIECE, 256)), moved=2**20)(od_parts)
    attended = jnp.concatenate([att_coarse, att_fine], axis=1)
    attended = lax.all_gather(attended, "head", axis=0, tiled=True)
    mixed = product_tn(attended, columns).astype(BF16)

    dk_fine, dv_fine, coarse_part = call(
        key_sums_kernel, (shape(PIECE, 256), shape(PIECE, 256), shape(4, 64, PIECE)), moved=2**20
    )(dkv_parts)
    coarse_parts = lax.all_gather(coarse_part, KEY_TILES, axis=0, tiled=False)
    dk_coarse, dv_coarse = call(coarse_sums_kernel, (shape(256, 256), shape(256, 256)), moved=2**20)(
        coarse_parts, dk_coarse, dv_coarse
    )
    return (
        mixed[256:], mixed[:256], dq_fine, dk_fine, dv_fine, dq_coarse, dk_coarse, dv_coarse,
    )


def solution(mesh):
    fine_mesh = Mesh(mesh.devices.reshape(2, 2, 2, 2, 2, 2, 4), SEQ + ("head",))
    in_specs = (
        P(SEQ, "head"), P(SEQ, "head"), P(SEQ, "head"),
        P(None, "head"), P(None, "head"), P(None, "head"),
        P("head", None), P(SEQ, "head"), P(None, "head"), P(), P(),
    )
    out_specs = (
        P(SEQ, "head"), P(None, "head"),
        P(SEQ, "head"), P(SEQ, "head"), P(SEQ, "head"),
        P(None, "head"), P(None, "head"), P(None, "head"),
    )
    return jax.shard_map(
        on_device, mesh=fine_mesh, in_specs=in_specs, out_specs=out_specs, check_vma=False
    )
```

```python
import jax
import jax.numpy as jnp
from jax import lax
from jax.experimental import pallas as pl
from jax.experimental.pallas import tpu as pltpu
from jax.sharding import Mesh
from jax.sharding import PartitionSpec as P

HEAD_SIZE = 64
SCALE = HEAD_SIZE ** (-0.5)
FSCALES = 3
HIDE = -30000.0
PIECE = 128
PIECES = 16
QUERY_BLOCKS = 4
QUERY_BLOCK = 512
STEP = 2
F32 = jnp.float32
BF16 = jnp.bfloat16

SEQ = ("xh", "yh", "yl", "zc", "zb", "za")
HEADS = ("xh", "yh")
KEY_GROUP = ("xh", "yh", "zc", "zb")
KEY_TILES = ("yl", "za")


def product(left, right):
    return jnp.dot(left, right, preferred_element_type=F32)


def product_nt(left, right):
    return lax.dot_general(left, right, (((1,), (1,)), ((), ())), preferred_element_type=F32)


def product_tn(left, right):
    return lax.dot_general(left, right, (((0,), (0,)), ((), ())), preferred_element_type=F32)


def call(kernel, outs, scratch=(), smem=0, flops=0, moved=0, exps=0):
    def run(*operands):
        return pl.pallas_call(
            kernel,
            out_shape=outs,
            in_specs=[pl.BlockSpec(memory_space=pltpu.SMEM)] * smem
            + [pl.BlockSpec(memory_space=pltpu.VMEM)] * (len(operands) - smem),
            out_specs=jax.tree.map(lambda _: pl.BlockSpec(memory_space=pltpu.VMEM), outs),
            scratch_shapes=list(scratch),
            compiler_params=pltpu.CompilerParams(vmem_limit_bytes=48 * 2**20),
            cost_estimate=pl.CostEstimate(
                flops=flops, bytes_accessed=moved, transcendentals=exps
            ),
        )(*operands)

    return run


def shape(*dims, dtype=BF16):
    return jax.ShapeDtypeStruct(dims, dtype)


def pack_keys_kernel(key_ref, value_ref, out_ref):
    for head in range(4):
        cols = slice(head * HEAD_SIZE, (head + 1) * HEAD_SIZE)
        both = jnp.concatenate([key_ref[:, cols], value_ref[:, cols]], axis=1)
        for other in range(4):
            out_ref[4 * head + other] = both


def weight_blocks_kernel(place_ref, weight_ref, *refs):
    outs, held = refs[:4], refs[4]
    for part in range(4):
        held[part] = weight_ref[:, part * 480:(part + 1) * 480]
    for partner in range(4):
        outs[partner][...] = held[place_ref[2] ^ partner]


def pack_queries_kernel(place_ref, query_ref, *refs):
    grads, weights, outs, held = refs[:4], refs[4:8], refs[8:12], refs[12]
    back = sum(product(weight[...], grad[...]) for weight, grad in zip(weights, grads)).astype(BF16)
    query = (query_ref[...].astype(F32) * SCALE).T.astype(BF16)
    for head in range(4):
        rows = slice(head * HEAD_SIZE, (head + 1) * HEAD_SIZE)
        held[head] = jnp.concatenate([query[rows], back[rows]], axis=0)
    for partner in range(4):
        outs[partner][...] = held[place_ref[0] ^ partner]


def prepare_keys(kv_ref, onehot_ref, masked_keys, turned):
    lane = lax.broadcasted_iota(jnp.int32, (PIECE, PIECE), 1)
    for piece in range(PIECES):
        both = kv_ref[piece]
        masked_keys[piece] = jnp.where(lane < HEAD_SIZE, both, onehot_ref[piece])
        turned[piece] = both.astype(F32).T.astype(BF16)


def query_side(place_ref, qb_refs, ids_ref, block):
    source = place_ref[0] ^ block
    both = jnp.concatenate([ref[source] for ref in qb_refs], axis=1)
    ids = jnp.concatenate([ids_ref[4 * block + (place_ref[1] ^ part)] for part in range(4)], axis=1)
    row = lax.broadcasted_iota(jnp.int32, (HEAD_SIZE, QUERY_BLOCK), 0)
    hidden = (row > ids) & (row < FSCALES)
    penalty = jnp.where(hidden, HIDE, 0.0).astype(BF16)
    return both, jnp.concatenate([both[:HEAD_SIZE], penalty], axis=0)


def rows_of(ref, step):
    return ref[pl.ds(STEP * step, STEP)].reshape(STEP * PIECE, PIECE)


def turned_of(ref, step, first):
    return jnp.concatenate(
        [ref[STEP * step + part, first:first + HEAD_SIZE, :] for part in range(STEP)], axis=1
    )


def coarse_side(kvc_ref):
    both = kvc_ref[...]
    lane = lax.broadcasted_iota(jnp.int32, both.shape, 1)
    only_keys = jnp.where(lane < HEAD_SIZE, both, jnp.zeros_like(both))
    return both, only_keys, both.astype(F32).T.astype(BF16)


def forward_kernel(
    place_ref, steps_ref, kv_ref, onehot_ref, kvc_ref, qb0, qb1, qb2, qb3, ids_ref, out_ref, stats_ref, masked_keys, turned
):
    prepare_keys(kv_ref, onehot_ref, masked_keys, turned)
    _, coarse_keys, coarse_turned = coarse_side(kvc_ref)

    def one_block(block, _):
        both, queries = query_side(place_ref, (qb0, qb1, qb2, qb3), ids_ref, block)
        scores = product(coarse_keys, queries)
        top = jnp.max(scores, axis=0, keepdims=True)
        probs = jnp.exp(scores - top)
        total = jnp.sum(probs, axis=0, keepdims=True)
        accum = product(coarse_turned[HEAD_SIZE:], probs.astype(BF16))

        def one_step(step, carried):
            top, total, accum = carried
            scores = product(rows_of(masked_keys, step), queries)
            new_top = jnp.maximum(top, jnp.max(scores, axis=0, keepdims=True))
            fade = jnp.exp(top - new_top)
            probs = jnp.exp(scores - new_top)
            total = total * fade + jnp.sum(probs, axis=0, keepdims=True)
            accum = accum * fade + product(turned_of(turned, step, HEAD_SIZE), probs.astype(BF16))
            return new_top, total, accum

        top, total, accum = lax.fori_loop(0, steps_ref[block], one_step, (top, total, accum))
        offset = jnp.sum(both[HEAD_SIZE:].astype(F32) * accum, axis=0, keepdims=True)
        out_ref[block] = accum
        stats_ref[block] = jnp.concatenate(
            [top, total, offset, jnp.zeros((5, QUERY_BLOCK), F32)], axis=0
        )
        return 0

    lax.fori_loop(0, QUERY_BLOCKS, one_block, 0)


def backward_kernel(
    place_ref, steps_ref, kv_ref, onehot_ref, kvc_ref, qb0, qb1, qb2, qb3, ids_ref, accum_ref, own_ref,
    stats1, stats2, stats3, od0, od1, od2, od3, dkv_ref, masked_keys, turned, key_sums, coarse_sums,
):
    prepare_keys(kv_ref, onehot_ref, masked_keys, turned)
    coarse_both, coarse_keys, coarse_turned = coarse_side(kvc_ref)
    key_sums[...] = jnp.zeros_like(key_sums)
    coarse_sums[...] = jnp.zeros_like(coarse_sums)

    def one_block(block, _):
        both, queries = query_side(place_ref, (qb0, qb1, qb2, qb3), ids_ref, block)
        stats = [own_ref[block]]
        for partner, ref in enumerate((stats1, stats2, stats3), 1):
            theirs = ref[block]
            parts = [theirs[:, (part ^ partner) * PIECE:((part ^ partner) + 1) * PIECE] for part in range(4)]
            stats.append(jnp.concatenate(parts, axis=1))
        top = stats[0][0:1]
        for other in stats[1:]:
            top = jnp.maximum(top, other[0:1])
        total = jnp.zeros_like(top)
        offset = jnp.zeros_like(top)
        for other in stats:
            fade = jnp.exp(other[0:1] - top)
            total = total + fade * other[1:2]
            offset = offset + fade * other[2:3]
        offset = offset / total
        log_total = top + jnp.log(total)
        attended = accum_ref[block] * (jnp.exp(own_ref[block][0:1] - top) / total)
        back = jnp.concatenate(
            [jnp.zeros((HEAD_SIZE, QUERY_BLOCK), BF16), both[HEAD_SIZE:]], axis=0
        )
        token_rows = both.astype(F32).T
        lane = lax.broadcasted_iota(jnp.int32, token_rows.shape, 1)
        query_rows = jnp.where(lane < HEAD_SIZE, token_rows, 0.0).astype(BF16)
        back_rows = jnp.where(lane < HEAD_SIZE, 0.0, token_rows).astype(BF16)

        def terms(only_keys, key_value, key_turned):
            probs = jnp.exp(product(only_keys, queries) - log_total)
            grad_probs = product(key_value, back)
            grad_scores = (probs * (grad_probs - offset)).astype(BF16)
            key_side = product(grad_scores, query_rows) + product(probs.astype(BF16), back_rows)
            return product(key_turned, grad_scores), key_side

        query_grad, coarse_term = terms(coarse_keys, coarse_both, coarse_turned[:HEAD_SIZE])
        coarse_sums[...] += coarse_term

        def one_step(step, query_grad):
            query_term, key_side = terms(
                rows_of(masked_keys, step), rows_of(kv_ref, step), turned_of(turned, step, 0)
            )
            key_sums[pl.ds(STEP * step, STEP)] += key_side.reshape(STEP, PIECE, PIECE)
            return query_grad + query_term

        query_grad = lax.fori_loop(0, steps_ref[block], one_step, query_grad)
        both_out = jnp.concatenate([attended, query_grad * SCALE], axis=0).astype(BF16)
        for part, ref in enumerate((od0, od1, od2, od3)):
            ref[block] = both_out[:, part * PIECE:(part + 1) * PIECE]
        return 0

    lax.fori_loop(0, QUERY_BLOCKS, one_block, 0)
    dkv_ref[:, :PIECE, :] = key_sums[...].astype(BF16)
    coarse = coarse_sums[...].astype(BF16)
    for piece in range(PIECES):
        dkv_ref[piece, PIECE:, :] = coarse


def coarse_kernel(query_ref, key_ref, value_ref, bias_ref, *refs):
    grads, weights, (att_ref, dq_ref, dk_ref, dv_ref) = refs[:4], refs[4:8], refs[8:]
    back_all = sum(product(weight[...], grad[...]) for weight, grad in zip(weights, grads)).astype(BF16)
    query_grads, attended_all, key_grads, value_grads = [], [], [], []
    for head in range(4):
        cols = slice(head * HEAD_SIZE, (head + 1) * HEAD_SIZE)
        query = (query_ref[:, cols].astype(F32) * SCALE).astype(BF16)
        key, value, back = key_ref[:, cols], value_ref[:, cols], back_all[cols]
        scores = product_nt(key, query) + bias_ref[...]
        top = jnp.max(scores, axis=0, keepdims=True)
        total = jnp.sum(jnp.exp(scores - top), axis=0, keepdims=True)
        probs = jnp.exp(scores - (top + jnp.log(total)))
        rounded = probs.astype(BF16)
        attended = product_tn(value, rounded).astype(BF16)
        offset = jnp.sum(back.astype(F32) * attended.astype(F32), axis=0, keepdims=True)
        grad_scores = (probs * (product(value, back) - offset)).astype(BF16)
        query_grads.append(product_tn(key, grad_scores) * SCALE)
        key_grads.append(product(grad_scores, query))
        value_grads.append(product_nt(rounded, back))
        attended_all.append(attended)
    att_ref[...] = jnp.concatenate(attended_all, axis=0)
    dq_ref[...] = jnp.concatenate(query_grads, axis=0).T.astype(BF16)
    dk_ref[...] = jnp.concatenate(key_grads, axis=1)
    dv_ref[...] = jnp.concatenate(value_grads, axis=1)


def mix_kernel(*refs):
    attended, weights, out_ref = refs[:4], refs[4:8], refs[8]
    out_ref[...] = sum(
        product_tn(weight[...], att[...]) for weight, att in zip(weights, attended)
    ).astype(BF16)


def query_sums_kernel(place_ref, *refs):
    parts, outs, held = refs[:4], refs[4:8], refs[8]
    for block in range(4):
        held[block] = sum(part[block].astype(F32) for part in parts).astype(BF16)
    for partner in range(4):
        outs[partner][...] = held[place_ref[0] ^ partner]


def query_heads_kernel(place_ref, *refs):
    parts, (att_ref, dq_ref, held) = refs[:4], refs[4:]
    for partner, part in enumerate(parts):
        rows = pl.ds(pl.multiple_of((place_ref[0] ^ partner) * HEAD_SIZE, HEAD_SIZE), HEAD_SIZE)
        att_ref[rows, :] = part[:HEAD_SIZE, :]
        held[rows, :] = part[HEAD_SIZE:, :].astype(F32)
    dq_ref[...] = held[...].T.astype(BF16)


def key_sums_kernel(parts_ref, dk_ref, dv_ref, coarse_ref):
    keys, values = [], []
    for head in range(4):
        summed = sum(parts_ref[4 * head + part].astype(F32) for part in range(4))
        keys.append(summed[:PIECE, :HEAD_SIZE])
        values.append(summed[:PIECE, HEAD_SIZE:])
        coarse_ref[head] = summed[PIECE:].astype(BF16)
    dk_ref[...] = jnp.concatenate(keys, axis=1).astype(BF16)
    dv_ref[...] = jnp.concatenate(values, axis=1).astype(BF16)


def coarse_sums_kernel(place_ref, *refs):
    received, (dk_ref, dv_ref, dk_out, dv_out) = refs[:4], refs[4:]
    for partner, ref in enumerate(received):
        rows = pl.ds(pl.multiple_of((place_ref[1] ^ partner) * 64, 64), 64)
        parts = [ref[head].astype(F32) for head in range(4)]
        keys = jnp.concatenate([part[:, :HEAD_SIZE] for part in parts], axis=1)
        values = jnp.concatenate([part[:, HEAD_SIZE:] for part in parts], axis=1)
        dk_out[rows, :] = (dk_ref[rows, :] + keys).astype(BF16)
        dv_out[rows, :] = (dv_ref[rows, :] + values).astype(BF16)


def exchange(array, group):
    return lax.all_to_all(array, group, 0, 0, tiled=True)


def swap(arrays, axes):
    out = [arrays[0]]
    for partner in (1, 2, 3):
        out.append(lax.ppermute(arrays[partner], axes, [(i, i ^ partner) for i in range(4)]))
    return out


def on_device(
    query_fine, key_fine, value_fine, query_coarse, key_coarse, value_coarse,
    out_weight, grad_fine, grad_coarse, fine_scale, coarse_scale,
):
    place = {name: lax.axis_index(name) for name in SEQ}
    head_of = place["xh"] * 2 + place["yh"]
    tile_of = place["yl"] * 2 + place["za"]
    placed = jnp.stack([head_of, tile_of, lax.axis_index("head")]).astype(jnp.int32)

    grads = swap([grad_fine.T] * 4, "head")
    packed_kv = call(pack_keys_kernel, shape(PIECES, PIECE, PIECE), moved=2**20)(key_fine, value_fine)
    kv = exchange(packed_kv, KEY_GROUP)
    weights = call(
        weight_blocks_kernel, (shape(256, 480),) * 4, [pltpu.VMEM((4, 256, 480), BF16)], 1, moved=2**21
    )(placed, out_weight)
    packed_q = call(
        pack_queries_kernel, (shape(PIECE, PIECE),) * 4, [pltpu.VMEM((4, PIECE, PIECE), BF16)], 1,
        flops=2 * 128 * 256 * 1920, moved=2**21,
    )(placed, query_fine, *grads, *weights)
    own_head = jnp.stack(swap(packed_q, HEADS))
    qb = swap([own_head] * 4, KEY_TILES)

    coarse_grads = swap([grad_coarse.T] * 4, "head")
    columns = swap(weights, "head")

    ids = fine_scale.reshape(2, 2, 2, 2, 2, 2, PIECE)
    query_ids = lax.dynamic_index_in_dim(ids, place["zc"], 3, keepdims=False)
    query_ids = lax.dynamic_index_in_dim(query_ids, place["zb"], 3, keepdims=False)
    query_ids = query_ids.reshape(PIECES, 1, PIECE)
    key_ids = lax.dynamic_index_in_dim(ids, place["yl"], 2, keepdims=False)
    key_ids = lax.dynamic_index_in_dim(key_ids, place["za"], 4, keepdims=False)
    key_ids = key_ids.reshape(PIECES, PIECE)
    lane = lax.broadcasted_iota(jnp.int32, (PIECES, PIECE, PIECE), 2)
    onehot = (lane - HEAD_SIZE == key_ids[:, :, None]).astype(BF16)
    seen = jnp.sum(key_ids[None, :, 0] <= query_ids[3::4, 0, -1:], axis=1)
    steps = ((seen + STEP - 1) // STEP).astype(jnp.int32)

    coarse_rows = [
        lax.dynamic_slice(array, (tile_of * 64, 0), (64, 256)).reshape(64, 4, HEAD_SIZE)
        for array in (key_coarse, value_coarse)
    ]
    kvc = jnp.concatenate(
        [lax.dynamic_index_in_dim(rows, head_of, 1, keepdims=False) for rows in coarse_rows], axis=1
    )

    half = [pltpu.VMEM((PIECES, PIECE, PIECE), BF16)] * 2
    accum, stats = call(
        forward_kernel,
        (shape(QUERY_BLOCKS, HEAD_SIZE, QUERY_BLOCK, dtype=F32), shape(QUERY_BLOCKS, 8, QUERY_BLOCK, dtype=F32)),
        half, 2, 4 * 2048 * 2112 * 64, 2**21, 2048 * 2112,
    )(placed, steps, kv, onehot, kvc, *qb, query_ids)
    all_stats = swap([stats] * 4, KEY_TILES)
    *od, dkv = call(
        backward_kernel,
        (shape(4, PIECE, PIECE),) * 4 + (shape(PIECES, PIECE + 64, PIECE),),
        half + [pltpu.VMEM((PIECES, PIECE, PIECE), F32), pltpu.VMEM((64, PIECE), F32)],
        2, 10 * 2048 * 2112 * 64, 2**22, 2048 * 2112,
    )(placed, steps, kv, onehot, kvc, *qb, query_ids, accum, *all_stats)

    dkv_parts = exchange(dkv, KEY_GROUP)
    od_sums = call(
        query_sums_kernel, (shape(PIECE, PIECE),) * 4, [pltpu.VMEM((4, PIECE, PIECE), BF16)], 1, moved=2**20
    )(placed, *swap(od, KEY_TILES))
    att_fine, dq_fine = call(
        query_heads_kernel, (shape(256, PIECE), shape(PIECE, 256)), [pltpu.VMEM((256, PIECE), F32)], 1, moved=2**20
    )(placed, *swap(od_sums, HEADS))
    mixed_fine = call(mix_kernel, shape(480, PIECE), flops=2**27, moved=2**20)(
        *swap([att_fine] * 4, "head"), *columns
    )

    bias = jnp.where(coarse_scale[:, None] <= coarse_scale[None, :], 0.0, -1e9).astype(F32)
    att_coarse, dq_coarse, dk_coarse, dv_coarse = call(
        coarse_kernel,
        (shape(256, 256), shape(256, 256), shape(256, 256, dtype=F32), shape(256, 256, dtype=F32)),
        flops=2**29, moved=2**22, exps=2**19,
    )(query_coarse, key_coarse, value_coarse, bias, *coarse_grads, *weights)
    mixed_coarse = call(mix_kernel, shape(480, 256), flops=2**28, moved=2**20)(
        *swap([att_coarse] * 4, "head"), *columns
    )

    dkv_parts, mixed_fine, mixed_coarse, dq_fine, dq_coarse, dk_coarse, dv_coarse = lax.optimization_barrier(
        (dkv_parts, mixed_fine, mixed_coarse, dq_fine, dq_coarse, dk_coarse, dv_coarse)
    )
    dk_fine, dv_fine, coarse_part = call(
        key_sums_kernel, (shape(PIECE, 256), shape(PIECE, 256), shape(4, 64, PIECE)), moved=2**20
    )(dkv_parts)
    dk_coarse, dv_coarse = call(coarse_sums_kernel, (shape(256, 256), shape(256, 256)), (), 1, moved=2**20)(
        placed, *swap([coarse_part] * 4, KEY_TILES), dk_coarse, dv_coarse
    )
    return (
        mixed_fine.T, mixed_coarse.T, dq_fine, dk_fine, dv_fine, dq_coarse, dk_coarse, dv_coarse,
    )


def solution(mesh):
    fine_mesh = Mesh(mesh.devices.reshape(2, 2, 2, 2, 2, 2, 4), SEQ + ("head",))
    in_specs = (
        P(SEQ, "head"), P(SEQ, "head"), P(SEQ, "head"),
        P(None, "head"), P(None, "head"), P(None, "head"),
        P("head", None), P(SEQ, "head"), P(None, "head"), P(), P(),
    )
    out_specs = (
        P(SEQ, "head"), P(None, "head"),
        P(SEQ, "head"), P(SEQ, "head"), P(SEQ, "head"),
        P(None, "head"), P(None, "head"), P(None, "head"),
    )
    return jax.shard_map(
        on_device, mesh=fine_mesh, in_specs=in_specs, out_specs=out_specs, check_vma=False
    )
```

```python
import jax
import jax.numpy as jnp
from jax import lax
from jax.experimental import pallas as pl
from jax.experimental.pallas import tpu as pltpu
from jax.sharding import Mesh
from jax.sharding import PartitionSpec as P

HEAD_SIZE = 64
SCALE = HEAD_SIZE ** (-0.5)
FSCALES = 3
HIDE = -30000.0
PIECE = 128
PIECES = 16
QUERY_BLOCKS = 4
QUERY_BLOCK = 512
STEP = 2
F32 = jnp.float32
BF16 = jnp.bfloat16

SEQ = ("xh", "yh", "yl", "zc", "zb", "za")
HEADS = ("xh", "yh")
QUERY_TILES = ("zc", "zb")
KEY_TILES = ("yl", "za")


def product(left, right):
    return jnp.dot(left, right, preferred_element_type=F32)


def product_nt(left, right):
    return lax.dot_general(left, right, (((1,), (1,)), ((), ())), preferred_element_type=F32)


def product_tn(left, right):
    return lax.dot_general(left, right, (((0,), (0,)), ((), ())), preferred_element_type=F32)


def call(kernel, outs, scratch=(), smem=0, flops=0, moved=0, exps=0):
    def run(*operands):
        return pl.pallas_call(
            kernel,
            out_shape=outs,
            in_specs=[pl.BlockSpec(memory_space=pltpu.SMEM)] * smem
            + [pl.BlockSpec(memory_space=pltpu.VMEM)] * (len(operands) - smem),
            out_specs=jax.tree.map(lambda _: pl.BlockSpec(memory_space=pltpu.VMEM), outs),
            scratch_shapes=list(scratch),
            compiler_params=pltpu.CompilerParams(vmem_limit_bytes=48 * 2**20),
            cost_estimate=pl.CostEstimate(
                flops=flops, bytes_accessed=moved, transcendentals=exps
            ),
        )(*operands)

    return run


def shape(*dims, dtype=BF16):
    return jax.ShapeDtypeStruct(dims, dtype)


def weight_blocks_kernel(place_ref, weight_ref, *refs):
    outs, held = refs[:4], refs[4]
    for part in range(4):
        held[part] = weight_ref[:, part * 480:(part + 1) * 480]
    for partner in range(4):
        outs[partner][...] = held[place_ref[2] ^ partner]


def pack_kernel(place_ref, query_ref, key_ref, value_ref, *refs):
    grads, weights, outs, held = refs[:4], refs[4:8], refs[8:12], refs[12]
    back = sum(product(weight[...], grad[...]) for weight, grad in zip(weights, grads)).astype(BF16)
    query = (query_ref[...].astype(F32) * SCALE).T.astype(BF16)
    for head in range(4):
        part = slice(head * HEAD_SIZE, (head + 1) * HEAD_SIZE)
        held[head, :HEAD_SIZE] = query[part]
        held[head, HEAD_SIZE:PIECE] = back[part]
        held[head, PIECE:] = jnp.concatenate([key_ref[:, part], value_ref[:, part]], axis=1)
    for partner in range(4):
        outs[partner][...] = held[place_ref[0] ^ partner]


def own_head_kernel(place_ref, *refs):
    parts, (qb_ref, kv_ref) = refs[:4], refs[4:]
    for partner, part in enumerate(parts):
        source = place_ref[0] ^ partner
        qb_ref[source] = part[:PIECE, :]
        kv_ref[source] = part[PIECE:, :]


def prepare_keys(place_ref, kv_refs, onehot_ref, masked_keys, plain, turned):
    lane = lax.broadcasted_iota(jnp.int32, (PIECE, PIECE), 1)
    for partner, ref in enumerate(kv_refs):
        for source in range(4):
            piece = 4 * source + (place_ref[3] ^ partner)
            both = ref[source]
            masked_keys[piece] = jnp.where(lane < HEAD_SIZE, both, onehot_ref[piece])
            turned[piece] = both.astype(F32).T.astype(BF16)
            if plain is not None:
                plain[piece] = both


def query_side(place_ref, qb_refs, ids_ref, block):
    both = jnp.concatenate([ref[block] for ref in qb_refs], axis=1)
    ids = jnp.concatenate([ids_ref[4 * block + (place_ref[1] ^ part)] for part in range(4)], axis=1)
    row = lax.broadcasted_iota(jnp.int32, (HEAD_SIZE, QUERY_BLOCK), 0)
    hidden = (row > ids) & (row < FSCALES)
    penalty = jnp.where(hidden, HIDE, 0.0).astype(BF16)
    return both, jnp.concatenate([both[:HEAD_SIZE], penalty], axis=0)


def rows_of(ref, step):
    return ref[pl.ds(STEP * step, STEP)].reshape(STEP * PIECE, PIECE)


def turned_of(ref, step, first):
    return jnp.concatenate(
        [ref[STEP * step + part, first:first + HEAD_SIZE, :] for part in range(STEP)], axis=1
    )


def coarse_side(kvc_ref):
    both = kvc_ref[...]
    lane = lax.broadcasted_iota(jnp.int32, both.shape, 1)
    only_keys = jnp.where(lane < HEAD_SIZE, both, jnp.zeros_like(both))
    return both, only_keys, both.astype(F32).T.astype(BF16)


def forward_kernel(
    place_ref, steps_ref, kv0, kv1, kv2, kv3, onehot_ref, kvc_ref, qb0, qb1, qb2, qb3, ids_ref,
    out_ref, stats_ref, masked_keys, turned,
):
    prepare_keys(place_ref, (kv0, kv1, kv2, kv3), onehot_ref, masked_keys, None, turned)
    _, coarse_keys, coarse_turned = coarse_side(kvc_ref)

    def one_block(block, _):
        both, queries = query_side(place_ref, (qb0, qb1, qb2, qb3), ids_ref, block)
        scores = product(coarse_keys, queries)
        top = jnp.max(scores, axis=0, keepdims=True)
        probs = jnp.exp(scores - top)
        total = jnp.sum(probs, axis=0, keepdims=True)
        accum = product(coarse_turned[HEAD_SIZE:], probs.astype(BF16))

        def one_step(step, carried):
            top, total, accum = carried
            scores = product(rows_of(masked_keys, step), queries)
            new_top = jnp.maximum(top, jnp.max(scores, axis=0, keepdims=True))
            fade = jnp.exp(top - new_top)
            probs = jnp.exp(scores - new_top)
            total = total * fade + jnp.sum(probs, axis=0, keepdims=True)
            accum = accum * fade + product(turned_of(turned, step, HEAD_SIZE), probs.astype(BF16))
            return new_top, total, accum

        top, total, accum = lax.fori_loop(0, steps_ref[block], one_step, (top, total, accum))
        offset = jnp.sum(both[HEAD_SIZE:].astype(F32) * accum, axis=0, keepdims=True)
        out_ref[block] = accum
        stats_ref[block] = jnp.concatenate(
            [top, total, offset, jnp.zeros((5, QUERY_BLOCK), F32)], axis=0
        )
        return 0

    lax.fori_loop(0, QUERY_BLOCKS, one_block, 0)


def backward_kernel(
    place_ref, steps_ref, kv0, kv1, kv2, kv3, onehot_ref, kvc_ref, qb0, qb1, qb2, qb3, ids_ref, accum_ref, own_ref,
    stats1, stats2, stats3, od0, od1, od2, od3, dkv0, dkv1, dkv2, dkv3,
    masked_keys, plain, turned, key_sums, coarse_sums,
):
    prepare_keys(place_ref, (kv0, kv1, kv2, kv3), onehot_ref, masked_keys, plain, turned)
    coarse_both, coarse_keys, coarse_turned = coarse_side(kvc_ref)
    key_sums[...] = jnp.zeros_like(key_sums)
    coarse_sums[...] = jnp.zeros_like(coarse_sums)

    def one_block(block, _):
        both, queries = query_side(place_ref, (qb0, qb1, qb2, qb3), ids_ref, block)
        stats = [own_ref[block]]
        for partner, ref in enumerate((stats1, stats2, stats3), 1):
            theirs = ref[block]
            parts = [theirs[:, (part ^ partner) * PIECE:((part ^ partner) + 1) * PIECE] for part in range(4)]
            stats.append(jnp.concatenate(parts, axis=1))
        top = stats[0][0:1]
        for other in stats[1:]:
            top = jnp.maximum(top, other[0:1])
        total = jnp.zeros_like(top)
        offset = jnp.zeros_like(top)
        for other in stats:
            fade = jnp.exp(other[0:1] - top)
            total = total + fade * other[1:2]
            offset = offset + fade * other[2:3]
        offset = offset / total
        log_total = top + jnp.log(total)
        attended = accum_ref[block] * (jnp.exp(own_ref[block][0:1] - top) / total)
        back = jnp.concatenate(
            [jnp.zeros((HEAD_SIZE, QUERY_BLOCK), BF16), both[HEAD_SIZE:]], axis=0
        )
        token_rows = both.astype(F32).T
        lane = lax.broadcasted_iota(jnp.int32, token_rows.shape, 1)
        query_rows = jnp.where(lane < HEAD_SIZE, token_rows, 0.0).astype(BF16)
        back_rows = jnp.where(lane < HEAD_SIZE, 0.0, token_rows).astype(BF16)

        def terms(only_keys, key_value, key_turned):
            probs = jnp.exp(product(only_keys, queries) - log_total)
            grad_probs = product(key_value, back)
            grad_scores = (probs * (grad_probs - offset)).astype(BF16)
            key_side = product(grad_scores, query_rows) + product(probs.astype(BF16), back_rows)
            return product(key_turned, grad_scores), key_side

        query_grad, coarse_term = terms(coarse_keys, coarse_both, coarse_turned[:HEAD_SIZE])
        coarse_sums[...] += coarse_term

        def one_step(step, query_grad):
            query_term, key_side = terms(
                rows_of(masked_keys, step), rows_of(plain, step), turned_of(turned, step, 0)
            )
            key_sums[pl.ds(STEP * step, STEP)] += key_side.reshape(STEP, PIECE, PIECE)
            return query_grad + query_term

        query_grad = lax.fori_loop(0, steps_ref[block], one_step, query_grad)
        both_out = jnp.concatenate([attended, query_grad * SCALE], axis=0).astype(BF16)
        for part, ref in enumerate((od0, od1, od2, od3)):
            ref[block] = both_out[:, part * PIECE:(part + 1) * PIECE]
        return 0

    lax.fori_loop(0, QUERY_BLOCKS, one_block, 0)
    coarse = coarse_sums[...].astype(BF16)
    for partner, ref in enumerate((dkv0, dkv1, dkv2, dkv3)):
        for source in range(4):
            piece = key_sums[4 * source + (place_ref[3] ^ partner)]
            ref[source * PIECE:(source + 1) * PIECE, :] = piece.astype(BF16)
        ref[4 * PIECE:, :] = coarse


def coarse_kernel(query_ref, key_ref, value_ref, bias_ref, *refs):
    grads, weights, (att_ref, dq_ref, dk_ref, dv_ref) = refs[:4], refs[4:8], refs[8:]
    back_all = sum(product(weight[...], grad[...]) for weight, grad in zip(weights, grads)).astype(BF16)
    query_grads, attended_all, key_grads, value_grads = [], [], [], []
    for head in range(4):
        cols = slice(head * HEAD_SIZE, (head + 1) * HEAD_SIZE)
        query = (query_ref[:, cols].astype(F32) * SCALE).astype(BF16)
        key, value, back = key_ref[:, cols], value_ref[:, cols], back_all[cols]
        scores = product_nt(key, query) + bias_ref[...]
        top = jnp.max(scores, axis=0, keepdims=True)
        total = jnp.sum(jnp.exp(scores - top), axis=0, keepdims=True)
        probs = jnp.exp(scores - (top + jnp.log(total)))
        rounded = probs.astype(BF16)
        attended = product_tn(value, rounded).astype(BF16)
        offset = jnp.sum(back.astype(F32) * attended.astype(F32), axis=0, keepdims=True)
        grad_scores = (probs * (product(value, back) - offset)).astype(BF16)
        query_grads.append(product_tn(key, grad_scores) * SCALE)
        key_grads.append(product(grad_scores, query))
        value_grads.append(product_nt(rounded, back))
        attended_all.append(attended)
    att_ref[...] = jnp.concatenate(attended_all, axis=0)
    dq_ref[...] = jnp.concatenate(query_grads, axis=0).T.astype(BF16)
    dk_ref[...] = jnp.concatenate(key_grads, axis=1)
    dv_ref[...] = jnp.concatenate(value_grads, axis=1)


def mixed_of(attended, weights):
    return sum(product_tn(weight[...], att[...]) for weight, att in zip(weights, attended)).astype(BF16)


def mix_kernel(*refs):
    refs[8][...] = mixed_of(refs[:4], refs[4:8])


def sums_kernel(place_ref, *refs):
    od, dkv, outs, held = refs[:4], refs[4:8], refs[8:12], refs[12]
    for source in range(4):
        rows = slice(source * PIECE, (source + 1) * PIECE)
        held[source, :PIECE] = sum(part[source].astype(F32) for part in od).astype(BF16)
        held[source, PIECE:] = sum(part[rows, :].astype(F32) for part in dkv).astype(BF16)
    coarse = sum(part[4 * PIECE:, :].astype(F32) for part in dkv).astype(BF16)
    for partner in range(4):
        outs[partner][:2 * PIECE, :] = held[place_ref[0] ^ partner]
        outs[partner][2 * PIECE:, :] = coarse


def heads_kernel(place_ref, *refs):
    parts, (att_ref, dq_ref, dk_ref, dv_ref, coarse_ref, query_held, key_held) = refs[:4], refs[4:]
    for partner, part in enumerate(parts):
        head = place_ref[0] ^ partner
        rows = pl.ds(pl.multiple_of(head * HEAD_SIZE, HEAD_SIZE), HEAD_SIZE)
        att_ref[rows, :] = part[:HEAD_SIZE, :]
        query_held[rows, :] = part[HEAD_SIZE:PIECE, :].astype(F32)
        key_held[head] = part[PIECE:2 * PIECE, :]
        coarse_ref[head] = part[2 * PIECE:, :]
    dq_ref[...] = query_held[...].T.astype(BF16)
    dk_ref[...] = jnp.concatenate([key_held[head, :, :HEAD_SIZE] for head in range(4)], axis=1)
    dv_ref[...] = jnp.concatenate([key_held[head, :, HEAD_SIZE:] for head in range(4)], axis=1)


def last_kernel(place_ref, *refs):
    attended, weights, received = refs[:4], refs[4:8], refs[8:12]
    dk_ref, dv_ref, mixed_ref, dk_out, dv_out = refs[12:]
    mixed_ref[...] = mixed_of(attended, weights)
    for partner, ref in enumerate(received):
        rows = pl.ds(pl.multiple_of((place_ref[1] ^ partner) * 64, 64), 64)
        parts = [ref[head].astype(F32) for head in range(4)]
        keys = jnp.concatenate([part[:, :HEAD_SIZE] for part in parts], axis=1)
        values = jnp.concatenate([part[:, HEAD_SIZE:] for part in parts], axis=1)
        dk_out[rows, :] = (dk_ref[rows, :] + keys).astype(BF16)
        dv_out[rows, :] = (dv_ref[rows, :] + values).astype(BF16)


def swap(arrays, axes):
    out = [arrays[0]]
    for partner in (1, 2, 3):
        out.append(lax.ppermute(arrays[partner], axes, [(i, i ^ partner) for i in range(4)]))
    return out


def on_device(
    query_fine, key_fine, value_fine, query_coarse, key_coarse, value_coarse,
    out_weight, grad_fine, grad_coarse, fine_scale, coarse_scale,
):
    place = {name: lax.axis_index(name) for name in SEQ}
    head_of = place["xh"] * 2 + place["yh"]
    tile_of = place["yl"] * 2 + place["za"]
    placed = jnp.stack(
        [head_of, tile_of, lax.axis_index("head"), place["zc"] * 2 + place["zb"]]
    ).astype(jnp.int32)

    grads = swap([grad_fine.T] * 4, "head")
    weights = call(
        weight_blocks_kernel, (shape(256, 480),) * 4, [pltpu.VMEM((4, 256, 480), BF16)], 1, moved=2**21
    )(placed, out_weight)
    packed = call(
        pack_kernel, (shape(2 * PIECE, PIECE),) * 4, [pltpu.VMEM((4, 2 * PIECE, PIECE), BF16)], 1,
        flops=2 * 128 * 256 * 1920, moved=2**21,
    )(placed, query_fine, key_fine, value_fine, *grads, *weights)
    own_qb, own_kv = call(own_head_kernel, (shape(4, PIECE, PIECE),) * 2, (), 1, moved=2**19)(
        placed, *swap(packed, HEADS)
    )
    kv = swap([own_kv] * 4, QUERY_TILES)
    qb = swap([own_qb] * 4, KEY_TILES)

    coarse_grads = swap([grad_coarse.T] * 4, "head")
    columns = swap(weights, "head")

    ids = fine_scale.reshape(2, 2, 2, 2, 2, 2, PIECE)
    query_ids = lax.dynamic_index_in_dim(ids, place["zc"], 3, keepdims=False)
    query_ids = lax.dynamic_index_in_dim(query_ids, place["zb"], 3, keepdims=False)
    query_ids = query_ids.reshape(PIECES, 1, PIECE)
    key_ids = lax.dynamic_index_in_dim(ids, place["yl"], 2, keepdims=False)
    key_ids = lax.dynamic_index_in_dim(key_ids, place["za"], 4, keepdims=False)
    key_ids = key_ids.reshape(PIECES, PIECE)
    lane = lax.broadcasted_iota(jnp.int32, (PIECES, PIECE, PIECE), 2)
    onehot = (lane - HEAD_SIZE == key_ids[:, :, None]).astype(BF16)
    seen = jnp.sum(key_ids[None, :, 0] <= query_ids[3::4, 0, -1:], axis=1)
    steps = ((seen + STEP - 1) // STEP).astype(jnp.int32)

    coarse_rows = [
        lax.dynamic_slice(array, (tile_of * 64, 0), (64, 256)).reshape(64, 4, HEAD_SIZE)
        for array in (key_coarse, value_coarse)
    ]
    kvc = jnp.concatenate(
        [lax.dynamic_index_in_dim(rows, head_of, 1, keepdims=False) for rows in coarse_rows], axis=1
    )

    bias = jnp.where(coarse_scale[:, None] <= coarse_scale[None, :], 0.0, -1e9).astype(F32)
    att_coarse, dq_coarse, dk_coarse, dv_coarse = call(
        coarse_kernel,
        (shape(256, 256), shape(256, 256), shape(256, 256, dtype=F32), shape(256, 256, dtype=F32)),
        flops=2**29, moved=2**22, exps=2**19,
    )(query_coarse, key_coarse, value_coarse, bias, *coarse_grads, *weights)
    kv, dk_coarse = lax.optimization_barrier((kv, dk_coarse))

    half = [pltpu.VMEM((PIECES, PIECE, PIECE), BF16)]
    accum, stats = call(
        forward_kernel,
        (shape(QUERY_BLOCKS, HEAD_SIZE, QUERY_BLOCK, dtype=F32), shape(QUERY_BLOCKS, 8, QUERY_BLOCK, dtype=F32)),
        half * 2, 2, 4 * 2048 * 2112 * 64, 2**21, 2048 * 2112,
    )(placed, steps, *kv, onehot, kvc, *qb, query_ids)
    all_stats = swap([stats] * 4, KEY_TILES)
    parts = call(
        backward_kernel,
        (shape(4, PIECE, PIECE),) * 4 + (shape(4 * PIECE + 64, PIECE),) * 4,
        half * 3 + [pltpu.VMEM((PIECES, PIECE, PIECE), F32), pltpu.VMEM((64, PIECE), F32)],
        2, 10 * 2048 * 2112 * 64, 2**22, 2048 * 2112,
    )(placed, steps, *kv, onehot, kvc, *qb, query_ids, accum, *all_stats)

    dkv = swap(parts[4:], QUERY_TILES)
    od = swap(parts[:4], KEY_TILES)
    mixed_coarse = call(mix_kernel, shape(480, 256), flops=2**28, moved=2**20)(
        *swap([att_coarse] * 4, "head"), *columns
    )
    dkv, mixed_coarse = lax.optimization_barrier((dkv, mixed_coarse))
    sums = call(
        sums_kernel, (shape(2 * PIECE + 64, PIECE),) * 4, [pltpu.VMEM((4, 2 * PIECE, PIECE), BF16)], 1, moved=2**21
    )(placed, *od, *dkv)
    att_fine, dq_fine, dk_fine, dv_fine, coarse_part = call(
        heads_kernel,
        (shape(256, PIECE),) + (shape(PIECE, 256),) * 3 + (shape(4, 64, PIECE),),
        [pltpu.VMEM((256, PIECE), F32), pltpu.VMEM((4, PIECE, PIECE), BF16)], 1, moved=2**20,
    )(placed, *swap(sums, HEADS))
    coarse_parts = swap([coarse_part] * 4, KEY_TILES)
    attended = swap([att_fine] * 4, "head")
    mixed_fine, dk_coarse, dv_coarse = call(
        last_kernel, (shape(480, PIECE), shape(256, 256), shape(256, 256)), (), 1, flops=2**27, moved=2**20
    )(placed, *attended, *columns, *coarse_parts, dk_coarse, dv_coarse)
    return (
        mixed_fine.T, mixed_coarse.T, dq_fine, dk_fine, dv_fine, dq_coarse, dk_coarse, dv_coarse,
    )


def solution(mesh):
    fine_mesh = Mesh(mesh.devices.reshape(2, 2, 2, 2, 2, 2, 4), SEQ + ("head",))
    in_specs = (
        P(SEQ, "head"), P(SEQ, "head"), P(SEQ, "head"),
        P(None, "head"), P(None, "head"), P(None, "head"),
        P("head", None), P(SEQ, "head"), P(None, "head"), P(), P(),
    )
    out_specs = (
        P(SEQ, "head"), P(None, "head"),
        P(SEQ, "head"), P(SEQ, "head"), P(SEQ, "head"),
        P(None, "head"), P(None, "head"), P(None, "head"),
    )
    return jax.shard_map(
        on_device, mesh=fine_mesh, in_specs=in_specs, out_specs=out_specs, check_vma=False
    )
```

```python
import jax
import jax.numpy as jnp
from jax import lax
from jax.experimental import pallas as pl
from jax.experimental.pallas import tpu as pltpu
from jax.sharding import Mesh
from jax.sharding import PartitionSpec as P

HEAD_SIZE = 64
SCALE = HEAD_SIZE ** (-0.5)
FSCALES = 3
HIDE = -30000.0
PIECE = 128
PIECES = 16
QUERY_BLOCKS = 4
QUERY_BLOCK = 512
STEP = 2
F32 = jnp.float32
BF16 = jnp.bfloat16

SEQ = ("xh", "yh", "yl", "zc", "zb", "za")
HEADS = ("xh", "yh")
QUERY_TILES = ("zc", "zb")
KEY_TILES = ("yl", "za")


def product(left, right):
    return jnp.dot(left, right, preferred_element_type=F32)


def product_nt(left, right):
    return lax.dot_general(left, right, (((1,), (1,)), ((), ())), preferred_element_type=F32)


def product_tn(left, right):
    return lax.dot_general(left, right, (((0,), (0,)), ((), ())), preferred_element_type=F32)


def call(kernel, outs, scratch=(), smem=0, flops=0, moved=0, exps=0):
    def run(*operands):
        return pl.pallas_call(
            kernel,
            out_shape=outs,
            in_specs=[pl.BlockSpec(memory_space=pltpu.SMEM)] * smem
            + [pl.BlockSpec(memory_space=pltpu.VMEM)] * (len(operands) - smem),
            out_specs=jax.tree.map(lambda _: pl.BlockSpec(memory_space=pltpu.VMEM), outs),
            scratch_shapes=list(scratch),
            compiler_params=pltpu.CompilerParams(vmem_limit_bytes=48 * 2**20),
            cost_estimate=pl.CostEstimate(
                flops=flops, bytes_accessed=moved, transcendentals=exps
            ),
        )(*operands)

    return run


def shape(*dims, dtype=BF16):
    return jax.ShapeDtypeStruct(dims, dtype)


def weight_blocks_kernel(place_ref, weight_ref, *refs):
    outs, held = refs[:4], refs[4]
    for part in range(4):
        held[part] = weight_ref[:, part * 480:(part + 1) * 480]
    for partner in range(4):
        outs[partner][...] = held[place_ref[2] ^ partner]


def pack_kernel(place_ref, query_ref, key_ref, value_ref, *refs):
    grads, weights, outs, held = refs[:4], refs[4:8], refs[8:12], refs[12]
    back = sum(product(weight[...], grad[...]) for weight, grad in zip(weights, grads)).astype(BF16)
    query = (query_ref[...].astype(F32) * SCALE).T.astype(BF16)
    for head in range(4):
        part = slice(head * HEAD_SIZE, (head + 1) * HEAD_SIZE)
        held[head, :HEAD_SIZE] = query[part]
        held[head, HEAD_SIZE:PIECE] = back[part]
        held[head, PIECE:] = jnp.concatenate([key_ref[:, part], value_ref[:, part]], axis=1)
    for partner in range(4):
        outs[partner][...] = held[place_ref[0] ^ partner]


def own_head_kernel(place_ref, *refs):
    parts, (qb_ref, kv_ref) = refs[:4], refs[4:]
    for partner, part in enumerate(parts):
        source = place_ref[0] ^ partner
        qb_ref[source] = part[:PIECE, :]
        kv_ref[source] = part[PIECE:, :]


def prepare_keys(place_ref, kv_refs, onehot_ref, masked_keys, plain, turned):
    lane = lax.broadcasted_iota(jnp.int32, (PIECE, PIECE), 1)
    for partner, ref in enumerate(kv_refs):
        for source in range(4):
            piece = 4 * source + (place_ref[3] ^ partner)
            both = ref[source]
            masked_keys[piece] = jnp.where(lane < HEAD_SIZE, both, onehot_ref[piece])
            turned[piece] = both.astype(F32).T.astype(BF16)
            if plain is not None:
                plain[piece] = both


def query_side(place_ref, qb_refs, ids_ref, block):
    both = jnp.concatenate([ref[block] for ref in qb_refs], axis=1)
    ids = jnp.concatenate([ids_ref[4 * block + (place_ref[1] ^ part)] for part in range(4)], axis=1)
    row = lax.broadcasted_iota(jnp.int32, (HEAD_SIZE, QUERY_BLOCK), 0)
    hidden = (row > ids) & (row < FSCALES)
    penalty = jnp.where(hidden, HIDE, 0.0).astype(BF16)
    return both, jnp.concatenate([both[:HEAD_SIZE], penalty], axis=0)


def rows_of(ref, step):
    return ref[pl.ds(STEP * step, STEP)].reshape(STEP * PIECE, PIECE)


def turned_of(ref, step, first):
    return jnp.concatenate(
        [ref[STEP * step + part, first:first + HEAD_SIZE, :] for part in range(STEP)], axis=1
    )


def coarse_side(kvc_ref):
    both = kvc_ref[...]
    lane = lax.broadcasted_iota(jnp.int32, both.shape, 1)
    only_keys = jnp.where(lane < HEAD_SIZE, both, jnp.zeros_like(both))
    return both, only_keys, both.astype(F32).T.astype(BF16)


def forward_kernel(
    place_ref, steps_ref, kv0, kv1, kv2, kv3, onehot_ref, kvc_ref, qb0, qb1, qb2, qb3, ids_ref,
    out_ref, stats_ref, masked_keys, turned,
):
    prepare_keys(place_ref, (kv0, kv1, kv2, kv3), onehot_ref, masked_keys, None, turned)
    _, coarse_keys, coarse_turned = coarse_side(kvc_ref)

    def one_block(block, _):
        both, queries = query_side(place_ref, (qb0, qb1, qb2, qb3), ids_ref, block)
        scores = product(coarse_keys, queries)
        top = jnp.max(scores, axis=0, keepdims=True)
        probs = jnp.exp(scores - top)
        total = jnp.sum(probs, axis=0, keepdims=True)
        accum = product(coarse_turned[HEAD_SIZE:], probs.astype(BF16))

        def one_step(step, carried):
            top, total, accum = carried
            scores = product(rows_of(masked_keys, step), queries)
            new_top = jnp.maximum(top, jnp.max(scores, axis=0, keepdims=True))
            fade = jnp.exp(top - new_top)
            probs = jnp.exp(scores - new_top)
            total = total * fade + jnp.sum(probs, axis=0, keepdims=True)
            accum = accum * fade + product(turned_of(turned, step, HEAD_SIZE), probs.astype(BF16))
            return new_top, total, accum

        top, total, accum = lax.fori_loop(0, steps_ref[block], one_step, (top, total, accum))
        offset = jnp.sum(both[HEAD_SIZE:].astype(F32) * accum, axis=0, keepdims=True)
        out_ref[block] = accum
        stats_ref[block] = jnp.concatenate(
            [top, total, offset, jnp.zeros((5, QUERY_BLOCK), F32)], axis=0
        )
        return 0

    lax.fori_loop(0, QUERY_BLOCKS, one_block, 0)


def backward_kernel(
    place_ref, steps_ref, kv0, kv1, kv2, kv3, onehot_ref, kvc_ref, qb0, qb1, qb2, qb3, ids_ref, accum_ref, own_ref,
    stats1, stats2, stats3, od0, od1, od2, od3, dkv0, dkv1, dkv2, dkv3,
    masked_keys, plain, turned, key_sums, coarse_sums,
):
    prepare_keys(place_ref, (kv0, kv1, kv2, kv3), onehot_ref, masked_keys, plain, turned)
    coarse_both, coarse_keys, coarse_turned = coarse_side(kvc_ref)
    key_sums[...] = jnp.zeros_like(key_sums)
    coarse_sums[...] = jnp.zeros_like(coarse_sums)

    def one_block(block, _):
        both, queries = query_side(place_ref, (qb0, qb1, qb2, qb3), ids_ref, block)
        stats = [own_ref[block]]
        for partner, ref in enumerate((stats1, stats2, stats3), 1):
            theirs = ref[block]
            parts = [theirs[:, (part ^ partner) * PIECE:((part ^ partner) + 1) * PIECE] for part in range(4)]
            stats.append(jnp.concatenate(parts, axis=1))
        top = stats[0][0:1]
        for other in stats[1:]:
            top = jnp.maximum(top, other[0:1])
        total = jnp.zeros_like(top)
        offset = jnp.zeros_like(top)
        for other in stats:
            fade = jnp.exp(other[0:1] - top)
            total = total + fade * other[1:2]
            offset = offset + fade * other[2:3]
        offset = offset / total
        log_total = top + jnp.log(total)
        attended = accum_ref[block] * (jnp.exp(own_ref[block][0:1] - top) / total)
        back = jnp.concatenate(
            [jnp.zeros((HEAD_SIZE, QUERY_BLOCK), BF16), both[HEAD_SIZE:]], axis=0
        )
        token_rows = both.astype(F32).T
        lane = lax.broadcasted_iota(jnp.int32, token_rows.shape, 1)
        query_rows = jnp.where(lane < HEAD_SIZE, token_rows, 0.0).astype(BF16)
        back_rows = jnp.where(lane < HEAD_SIZE, 0.0, token_rows).astype(BF16)

        def terms(only_keys, key_value, key_turned):
            probs = jnp.exp(product(only_keys, queries) - log_total)
            grad_probs = product(key_value, back)
            grad_scores = (probs * (grad_probs - offset)).astype(BF16)
            key_side = product(grad_scores, query_rows) + product(probs.astype(BF16), back_rows)
            return product(key_turned, grad_scores), key_side

        query_grad, coarse_term = terms(coarse_keys, coarse_both, coarse_turned[:HEAD_SIZE])
        coarse_sums[...] += coarse_term

        def one_step(step, query_grad):
            query_term, key_side = terms(
                rows_of(masked_keys, step), rows_of(plain, step), turned_of(turned, step, 0)
            )
            key_sums[pl.ds(STEP * step, STEP)] += key_side.reshape(STEP, PIECE, PIECE)
            return query_grad + query_term

        query_grad = lax.fori_loop(0, steps_ref[block], one_step, query_grad)
        both_out = jnp.concatenate([attended, query_grad * SCALE], axis=0).astype(BF16)
        for part, ref in enumerate((od0, od1, od2, od3)):
            ref[block] = both_out[:, part * PIECE:(part + 1) * PIECE]
        return 0

    lax.fori_loop(0, QUERY_BLOCKS, one_block, 0)
    coarse = coarse_sums[...].astype(BF16)
    for partner, ref in enumerate((dkv0, dkv1, dkv2, dkv3)):
        for source in range(4):
            piece = key_sums[4 * source + (place_ref[3] ^ partner)]
            ref[source * PIECE:(source + 1) * PIECE, :] = piece.astype(BF16)
        ref[4 * PIECE:, :] = coarse


def coarse_probs(query, key, bias):
    scores = product_nt(key, query) + bias
    top = jnp.max(scores, axis=0, keepdims=True)
    total = jnp.sum(jnp.exp(scores - top), axis=0, keepdims=True)
    return jnp.exp(scores - (top + jnp.log(total)))


def head_columns(ref, head):
    return ref[:, head * HEAD_SIZE:(head + 1) * HEAD_SIZE]


def packet_kernel(place_ref, query_ref, key_ref, value_ref, bias_ref, weight_ref, grad_ref, *refs):
    outs, held = refs[:4], refs[4]
    for part in range(4):
        held[part] = weight_ref[:, part * 480:(part + 1) * 480].astype(F32).T.astype(BF16)
    attended = []
    for head in range(4):
        query = (head_columns(query_ref, head).astype(F32) * SCALE).astype(BF16)
        probs = coarse_probs(query, head_columns(key_ref, head), bias_ref[...])
        attended.append(product_tn(head_columns(value_ref, head), probs.astype(BF16)).astype(BF16))
    attended = jnp.concatenate(attended, axis=0)
    for partner in range(4):
        outs[partner][:480, :] = held[place_ref[2] ^ partner]
        outs[partner][480:960, :] = grad_ref[...]
        outs[partner][960:, :] = attended


def coarse_kernel(query_ref, key_ref, value_ref, bias_ref, *refs):
    packets, weights, (mixed_ref, dq_ref, dk_ref, dv_ref) = refs[:4], refs[4:8], refs[8:]
    back_all = sum(
        product(weight[...], packet[480:960, :]) for weight, packet in zip(weights, packets)
    ).astype(BF16)
    mixed_ref[...] = sum(product(packet[:480, :], packet[960:, :]) for packet in packets).astype(BF16)
    query_grads, key_grads, value_grads = [], [], []
    for head in range(4):
        part = slice(head * HEAD_SIZE, (head + 1) * HEAD_SIZE)
        query = (query_ref[:, part].astype(F32) * SCALE).astype(BF16)
        key, value, back = key_ref[:, part], value_ref[:, part], back_all[part]
        probs = coarse_probs(query, key, bias_ref[...])
        rounded = probs.astype(BF16)
        attended = packets[0][960 + part.start:960 + part.stop, :]
        offset = jnp.sum(back.astype(F32) * attended.astype(F32), axis=0, keepdims=True)
        grad_scores = (probs * (product(value, back) - offset)).astype(BF16)
        query_grads.append(product_tn(key, grad_scores) * SCALE)
        key_grads.append(product(grad_scores, query))
        value_grads.append(product_nt(rounded, back))
    dq_ref[...] = jnp.concatenate(query_grads, axis=0).T.astype(BF16)
    dk_ref[...] = jnp.concatenate(key_grads, axis=1)
    dv_ref[...] = jnp.concatenate(value_grads, axis=1)


def sums_kernel(place_ref, *refs):
    od, dkv, outs, held = refs[:4], refs[4:8], refs[8:12], refs[12]
    for source in range(4):
        rows = slice(source * PIECE, (source + 1) * PIECE)
        held[source, :PIECE] = sum(part[source].astype(F32) for part in od).astype(BF16)
        held[source, PIECE:] = sum(part[rows, :].astype(F32) for part in dkv).astype(BF16)
    coarse = sum(part[4 * PIECE:, :].astype(F32) for part in dkv).astype(BF16)
    for partner in range(4):
        outs[partner][:2 * PIECE, :] = held[place_ref[0] ^ partner]
        outs[partner][2 * PIECE:, :] = coarse


def heads_kernel(place_ref, *refs):
    parts, (att_ref, dq_ref, dk_ref, dv_ref, coarse_ref, query_held, key_held) = refs[:4], refs[4:]
    for partner, part in enumerate(parts):
        head = place_ref[0] ^ partner
        rows = pl.ds(pl.multiple_of(head * HEAD_SIZE, HEAD_SIZE), HEAD_SIZE)
        att_ref[rows, :] = part[:HEAD_SIZE, :]
        query_held[rows, :] = part[HEAD_SIZE:PIECE, :].astype(F32)
        key_held[head] = part[PIECE:2 * PIECE, :]
        coarse_ref[head] = part[2 * PIECE:, :]
    dq_ref[...] = query_held[...].T.astype(BF16)
    dk_ref[...] = jnp.concatenate([key_held[head, :, :HEAD_SIZE] for head in range(4)], axis=1)
    dv_ref[...] = jnp.concatenate([key_held[head, :, HEAD_SIZE:] for head in range(4)], axis=1)


def last_kernel(place_ref, *refs):
    attended, packets, received = refs[:4], refs[4:8], refs[8:12]
    dk_ref, dv_ref, mixed_ref, dk_out, dv_out = refs[12:]
    mixed_ref[...] = sum(
        product(packet[:480, :], att[...]) for packet, att in zip(packets, attended)
    ).astype(BF16)
    for partner, ref in enumerate(received):
        rows = pl.ds(pl.multiple_of((place_ref[1] ^ partner) * 64, 64), 64)
        parts = [ref[head].astype(F32) for head in range(4)]
        keys = jnp.concatenate([part[:, :HEAD_SIZE] for part in parts], axis=1)
        values = jnp.concatenate([part[:, HEAD_SIZE:] for part in parts], axis=1)
        dk_out[rows, :] = (dk_ref[rows, :] + keys).astype(BF16)
        dv_out[rows, :] = (dv_ref[rows, :] + values).astype(BF16)


def swap(arrays, axes):
    out = [arrays[0]]
    for partner in (1, 2, 3):
        out.append(lax.ppermute(arrays[partner], axes, [(i, i ^ partner) for i in range(4)]))
    return out


def on_device(
    query_fine, key_fine, value_fine, query_coarse, key_coarse, value_coarse,
    out_weight, grad_fine, grad_coarse, fine_scale, coarse_scale,
):
    place = {name: lax.axis_index(name) for name in SEQ}
    head_of = place["xh"] * 2 + place["yh"]
    tile_of = place["yl"] * 2 + place["za"]
    placed = jnp.stack(
        [head_of, tile_of, lax.axis_index("head"), place["zc"] * 2 + place["zb"]]
    ).astype(jnp.int32)

    grads = swap([grad_fine.T] * 4, "head")
    weights = call(
        weight_blocks_kernel, (shape(256, 480),) * 4, [pltpu.VMEM((4, 256, 480), BF16)], 1, moved=2**21
    )(placed, out_weight)
    packed = call(
        pack_kernel, (shape(2 * PIECE, PIECE),) * 4, [pltpu.VMEM((4, 2 * PIECE, PIECE), BF16)], 1,
        flops=2 * 128 * 256 * 1920, moved=2**21,
    )(placed, query_fine, key_fine, value_fine, *grads, *weights)
    own_qb, own_kv = call(own_head_kernel, (shape(4, PIECE, PIECE),) * 2, (), 1, moved=2**19)(
        placed, *swap(packed, HEADS)
    )
    kv = swap([own_kv] * 4, QUERY_TILES)
    qb = swap([own_qb] * 4, KEY_TILES)

    ids = fine_scale.reshape(2, 2, 2, 2, 2, 2, PIECE)
    query_ids = lax.dynamic_index_in_dim(ids, place["zc"], 3, keepdims=False)
    query_ids = lax.dynamic_index_in_dim(query_ids, place["zb"], 3, keepdims=False)
    query_ids = query_ids.reshape(PIECES, 1, PIECE)
    key_ids = lax.dynamic_index_in_dim(ids, place["yl"], 2, keepdims=False)
    key_ids = lax.dynamic_index_in_dim(key_ids, place["za"], 4, keepdims=False)
    key_ids = key_ids.reshape(PIECES, PIECE)
    lane = lax.broadcasted_iota(jnp.int32, (PIECES, PIECE, PIECE), 2)
    onehot = (lane - HEAD_SIZE == key_ids[:, :, None]).astype(BF16)
    seen = jnp.sum(key_ids[None, :, 0] <= query_ids[3::4, 0, -1:], axis=1)
    steps = ((seen + STEP - 1) // STEP).astype(jnp.int32)

    coarse_rows = [
        lax.dynamic_slice(array, (tile_of * 64, 0), (64, 256)).reshape(64, 4, HEAD_SIZE)
        for array in (key_coarse, value_coarse)
    ]
    kvc = jnp.concatenate(
        [lax.dynamic_index_in_dim(rows, head_of, 1, keepdims=False) for rows in coarse_rows], axis=1
    )

    bias = jnp.where(coarse_scale[:, None] <= coarse_scale[None, :], 0.0, -1e9).astype(F32)
    packed = call(
        packet_kernel, (shape(1216, 256),) * 4, [pltpu.VMEM((4, 480, 256), BF16)], 1,
        flops=2**28, moved=2**22, exps=2**18,
    )(placed, query_coarse, key_coarse, value_coarse, bias, out_weight, grad_coarse.T)
    kv, packed = lax.optimization_barrier((kv, packed))

    half = [pltpu.VMEM((PIECES, PIECE, PIECE), BF16)]
    accum, stats = call(
        forward_kernel,
        (shape(QUERY_BLOCKS, HEAD_SIZE, QUERY_BLOCK, dtype=F32), shape(QUERY_BLOCKS, 8, QUERY_BLOCK, dtype=F32)),
        half * 2, 2, 4 * 2048 * 2112 * 64, 2**21, 2048 * 2112,
    )(placed, steps, *kv, onehot, kvc, *qb, query_ids)
    all_stats = swap([stats] * 4, KEY_TILES)
    packed, stats = lax.optimization_barrier((packed, stats))
    packets = swap(packed, "head")
    parts = call(
        backward_kernel,
        (shape(4, PIECE, PIECE),) * 4 + (shape(4 * PIECE + 64, PIECE),) * 4,
        half * 3 + [pltpu.VMEM((PIECES, PIECE, PIECE), F32), pltpu.VMEM((64, PIECE), F32)],
        2, 10 * 2048 * 2112 * 64, 2**22, 2048 * 2112,
    )(placed, steps, *kv, onehot, kvc, *qb, query_ids, accum, *all_stats)

    dkv = swap(parts[4:], QUERY_TILES)
    od = swap(parts[:4], KEY_TILES)
    mixed_coarse, dq_coarse, dk_coarse, dv_coarse = call(
        coarse_kernel,
        (shape(480, 256), shape(256, 256), shape(256, 256, dtype=F32), shape(256, 256, dtype=F32)),
        flops=2**29, moved=2**22, exps=2**19,
    )(query_coarse, key_coarse, value_coarse, bias, *packets, *weights)
    dkv, dk_coarse = lax.optimization_barrier((dkv, dk_coarse))
    sums = call(
        sums_kernel, (shape(2 * PIECE + 64, PIECE),) * 4, [pltpu.VMEM((4, 2 * PIECE, PIECE), BF16)], 1, moved=2**21
    )(placed, *od, *dkv)
    att_fine, dq_fine, dk_fine, dv_fine, coarse_part = call(
        heads_kernel,
        (shape(256, PIECE),) + (shape(PIECE, 256),) * 3 + (shape(4, 64, PIECE),),
        [pltpu.VMEM((256, PIECE), F32), pltpu.VMEM((4, PIECE, PIECE), BF16)], 1, moved=2**20,
    )(placed, *swap(sums, HEADS))
    coarse_parts = swap([coarse_part] * 4, KEY_TILES)
    attended = swap([att_fine] * 4, "head")
    mixed_fine, dk_coarse, dv_coarse = call(
        last_kernel, (shape(480, PIECE), shape(256, 256), shape(256, 256)), (), 1, flops=2**27, moved=2**20
    )(placed, *attended, *packets, *coarse_parts, dk_coarse, dv_coarse)
    return (
        mixed_fine.T, mixed_coarse.T, dq_fine, dk_fine, dv_fine, dq_coarse, dk_coarse, dv_coarse,
    )


def solution(mesh):
    fine_mesh = Mesh(mesh.devices.reshape(2, 2, 2, 2, 2, 2, 4), SEQ + ("head",))
    in_specs = (
        P(SEQ, "head"), P(SEQ, "head"), P(SEQ, "head"),
        P(None, "head"), P(None, "head"), P(None, "head"),
        P("head", None), P(SEQ, "head"), P(None, "head"), P(), P(),
    )
    out_specs = (
        P(SEQ, "head"), P(None, "head"),
        P(SEQ, "head"), P(SEQ, "head"), P(SEQ, "head"),
        P(None, "head"), P(None, "head"), P(None, "head"),
    )
    return jax.shard_map(
        on_device, mesh=fine_mesh, in_specs=in_specs, out_specs=out_specs, check_vma=False
    )
```

```python
import jax
import jax.numpy as jnp
from jax import lax
from jax.experimental import pallas as pl
from jax.experimental.pallas import tpu as pltpu
from jax.sharding import Mesh
from jax.sharding import PartitionSpec as P

HEAD_SIZE = 64
SCALE = HEAD_SIZE ** (-0.5)
FSCALES = 3
HIDE = -30000.0
PIECE = 128
PIECES = 16
QUERY_BLOCKS = 4
QUERY_BLOCK = 512
STEP = 2
F32 = jnp.float32
BF16 = jnp.bfloat16

SEQ = ("xh", "yh", "yl", "zc", "zb", "za")
HEADS = ("xh", "yh")
QUERY_TILES = ("zc", "zb")
KEY_TILES = ("yl", "za")


def product(left, right):
    return jnp.dot(left, right, preferred_element_type=F32)


def product_nt(left, right):
    return lax.dot_general(left, right, (((1,), (1,)), ((), ())), preferred_element_type=F32)


def product_tn(left, right):
    return lax.dot_general(left, right, (((0,), (0,)), ((), ())), preferred_element_type=F32)


def call(kernel, outs, scratch=(), smem=0, flops=0, moved=0, exps=0):
    def run(*operands):
        return pl.pallas_call(
            kernel,
            out_shape=outs,
            in_specs=[pl.BlockSpec(memory_space=pltpu.SMEM)] * smem
            + [pl.BlockSpec(memory_space=pltpu.VMEM)] * (len(operands) - smem),
            out_specs=jax.tree.map(lambda _: pl.BlockSpec(memory_space=pltpu.VMEM), outs),
            scratch_shapes=list(scratch),
            compiler_params=pltpu.CompilerParams(vmem_limit_bytes=48 * 2**20),
            cost_estimate=pl.CostEstimate(
                flops=flops, bytes_accessed=moved, transcendentals=exps
            ),
        )(*operands)

    return run


def shape(*dims, dtype=BF16):
    return jax.ShapeDtypeStruct(dims, dtype)


def weight_blocks_kernel(place_ref, weight_ref, *refs):
    outs, held = refs[:4], refs[4]
    for part in range(4):
        held[part] = weight_ref[:, part * 480:(part + 1) * 480]
    for partner in range(4):
        outs[partner][...] = held[place_ref[2] ^ partner]


def pack_kernel(place_ref, query_ref, key_ref, value_ref, *refs):
    grads, weights, outs, held = refs[:4], refs[4:8], refs[8:12], refs[12]
    back = sum(product(weight[...], grad[...]) for weight, grad in zip(weights, grads)).astype(BF16)
    query = (query_ref[...].astype(F32) * SCALE).T.astype(BF16)
    for head in range(4):
        part = slice(head * HEAD_SIZE, (head + 1) * HEAD_SIZE)
        held[head, :HEAD_SIZE] = query[part]
        held[head, HEAD_SIZE:PIECE] = back[part]
        held[head, PIECE:] = jnp.concatenate([key_ref[:, part], value_ref[:, part]], axis=1)
    for partner in range(4):
        outs[partner][...] = held[place_ref[0] ^ partner]


def own_head_kernel(place_ref, *refs):
    parts, (qb_ref, kv_ref) = refs[:4], refs[4:]
    for partner, part in enumerate(parts):
        source = place_ref[0] ^ partner
        qb_ref[source] = part[:PIECE, :]
        kv_ref[source] = part[PIECE:, :]


def prepare_keys(place_ref, kv_refs, onehot_ref, masked_keys, plain, turned):
    lane = lax.broadcasted_iota(jnp.int32, (PIECE, PIECE), 1)
    for partner, ref in enumerate(kv_refs):
        for source in range(4):
            piece = 4 * source + (place_ref[3] ^ partner)
            both = ref[source]
            masked_keys[piece] = jnp.where(lane < HEAD_SIZE, both, onehot_ref[piece])
            turned[piece] = both.astype(F32).T.astype(BF16)
            if plain is not None:
                plain[piece] = both


def query_side(place_ref, qb_refs, ids_ref, block):
    both = jnp.concatenate([ref[block] for ref in qb_refs], axis=1)
    ids = jnp.concatenate([ids_ref[4 * block + (place_ref[1] ^ part)] for part in range(4)], axis=1)
    row = lax.broadcasted_iota(jnp.int32, (HEAD_SIZE, QUERY_BLOCK), 0)
    hidden = (row > ids) & (row < FSCALES)
    penalty = jnp.where(hidden, HIDE, 0.0).astype(BF16)
    return both, jnp.concatenate([both[:HEAD_SIZE], penalty], axis=0)


def rows_of(ref, step):
    return ref[pl.ds(STEP * step, STEP)].reshape(STEP * PIECE, PIECE)


def turned_of(ref, step, first):
    return jnp.concatenate(
        [ref[STEP * step + part, first:first + HEAD_SIZE, :] for part in range(STEP)], axis=1
    )


def coarse_side(kvc_ref):
    both = kvc_ref[...]
    lane = lax.broadcasted_iota(jnp.int32, both.shape, 1)
    only_keys = jnp.where(lane < HEAD_SIZE, both, jnp.zeros_like(both))
    return both, only_keys, both.astype(F32).T.astype(BF16)


def forward_kernel(
    place_ref, steps_ref, kv0, kv1, kv2, kv3, onehot_ref, kvc_ref, qb0, qb1, qb2, qb3, ids_ref,
    out_ref, stats_ref, masked_keys, turned, queries_held, scores_held,
):
    prepare_keys(place_ref, (kv0, kv1, kv2, kv3), onehot_ref, masked_keys, None, turned)
    _, coarse_keys, coarse_turned = coarse_side(kvc_ref)
    for block in range(QUERY_BLOCKS):
        _, queries = query_side(place_ref, (qb0, qb1, qb2, qb3), ids_ref, block)
        queries_held[block] = queries
        scores = product(coarse_keys, queries)
        top = jnp.max(scores, axis=0, keepdims=True)
        probs = jnp.exp(scores - top)
        total = jnp.sum(probs, axis=0, keepdims=True)
        out_ref[block] = product(coarse_turned[HEAD_SIZE:], probs.astype(BF16))
        stats_ref[block] = jnp.concatenate([top, total, jnp.zeros((6, QUERY_BLOCK), F32)], axis=0)

    def one_block(block, _):
        queries = queries_held[block]
        last = steps_ref[block] - 1
        scores_held[0] = product(rows_of(masked_keys, 0), queries)

        def one_step(step, carried):
            top, total, accum = carried
            slot = step & 1
            scores = scores_held[slot]
            scores_held[1 - slot] = product(rows_of(masked_keys, jnp.minimum(step + 1, last)), queries)
            new_top = jnp.maximum(top, jnp.max(scores, axis=0, keepdims=True))
            fade = jnp.exp(top - new_top)
            probs = jnp.exp(scores - new_top)
            total = total * fade + jnp.sum(probs, axis=0, keepdims=True)
            accum = accum * fade + product(turned_of(turned, step, HEAD_SIZE), probs.astype(BF16))
            return new_top, total, accum

        start = stats_ref[block]
        top, total, accum = lax.fori_loop(
            0, steps_ref[block], one_step, (start[0:1], start[1:2], out_ref[block])
        )
        back = jnp.concatenate([ref[block, HEAD_SIZE:, :] for ref in (qb0, qb1, qb2, qb3)], axis=1)
        offset = jnp.sum(back.astype(F32) * accum, axis=0, keepdims=True)
        out_ref[block] = accum
        stats_ref[block] = jnp.concatenate(
            [top, total, offset, jnp.zeros((5, QUERY_BLOCK), F32)], axis=0
        )
        return 0

    lax.fori_loop(0, QUERY_BLOCKS, one_block, 0)


def backward_kernel(
    place_ref, steps_ref, kv0, kv1, kv2, kv3, onehot_ref, kvc_ref, qb0, qb1, qb2, qb3, ids_ref, accum_ref, own_ref,
    stats1, stats2, stats3, od0, od1, od2, od3, dkv0, dkv1, dkv2, dkv3,
    masked_keys, plain, turned, key_sums, coarse_sums,
):
    prepare_keys(place_ref, (kv0, kv1, kv2, kv3), onehot_ref, masked_keys, plain, turned)
    coarse_both, coarse_keys, coarse_turned = coarse_side(kvc_ref)
    key_sums[...] = jnp.zeros_like(key_sums)
    coarse_sums[...] = jnp.zeros_like(coarse_sums)

    def one_block(block, _):
        both, queries = query_side(place_ref, (qb0, qb1, qb2, qb3), ids_ref, block)
        stats = [own_ref[block]]
        for partner, ref in enumerate((stats1, stats2, stats3), 1):
            theirs = ref[block]
            parts = [theirs[:, (part ^ partner) * PIECE:((part ^ partner) + 1) * PIECE] for part in range(4)]
            stats.append(jnp.concatenate(parts, axis=1))
        top = stats[0][0:1]
        for other in stats[1:]:
            top = jnp.maximum(top, other[0:1])
        total = jnp.zeros_like(top)
        offset = jnp.zeros_like(top)
        for other in stats:
            fade = jnp.exp(other[0:1] - top)
            total = total + fade * other[1:2]
            offset = offset + fade * other[2:3]
        offset = offset / total
        log_total = top + jnp.log(total)
        attended = accum_ref[block] * (jnp.exp(own_ref[block][0:1] - top) / total)
        back = jnp.concatenate(
            [jnp.zeros((HEAD_SIZE, QUERY_BLOCK), BF16), both[HEAD_SIZE:]], axis=0
        )
        token_rows = both.astype(F32).T
        lane = lax.broadcasted_iota(jnp.int32, token_rows.shape, 1)
        query_rows = jnp.where(lane < HEAD_SIZE, token_rows, 0.0).astype(BF16)
        back_rows = jnp.where(lane < HEAD_SIZE, 0.0, token_rows).astype(BF16)

        def terms(only_keys, key_value, key_turned):
            probs = jnp.exp(product(only_keys, queries) - log_total)
            grad_probs = product(key_value, back)
            grad_scores = (probs * (grad_probs - offset)).astype(BF16)
            key_side = product(grad_scores, query_rows) + product(probs.astype(BF16), back_rows)
            return product(key_turned, grad_scores), key_side

        query_grad, coarse_term = terms(coarse_keys, coarse_both, coarse_turned[:HEAD_SIZE])
        coarse_sums[...] += coarse_term

        def one_step(step, query_grad):
            query_term, key_side = terms(
                rows_of(masked_keys, step), rows_of(plain, step), turned_of(turned, step, 0)
            )
            key_sums[pl.ds(STEP * step, STEP)] += key_side.reshape(STEP, PIECE, PIECE)
            return query_grad + query_term

        query_grad = lax.fori_loop(0, steps_ref[block], one_step, query_grad)
        both_out = jnp.concatenate([attended, query_grad * SCALE], axis=0).astype(BF16)
        for part, ref in enumerate((od0, od1, od2, od3)):
            ref[block] = both_out[:, part * PIECE:(part + 1) * PIECE]
        return 0

    lax.fori_loop(0, QUERY_BLOCKS, one_block, 0)
    coarse = coarse_sums[...].astype(BF16)
    for partner, ref in enumerate((dkv0, dkv1, dkv2, dkv3)):
        for source in range(4):
            piece = key_sums[4 * source + (place_ref[3] ^ partner)]
            ref[source * PIECE:(source + 1) * PIECE, :] = piece.astype(BF16)
        ref[4 * PIECE:, :] = coarse


def coarse_probs(query, key, bias):
    scores = product_nt(key, query) + bias
    top = jnp.max(scores, axis=0, keepdims=True)
    total = jnp.sum(jnp.exp(scores - top), axis=0, keepdims=True)
    return jnp.exp(scores - (top + jnp.log(total)))


def head_columns(ref, head):
    return ref[:, head * HEAD_SIZE:(head + 1) * HEAD_SIZE]


def packet_kernel(place_ref, query_ref, key_ref, value_ref, bias_ref, weight_ref, grad_ref, *refs):
    outs, held = refs[:4], refs[4]
    for part in range(4):
        held[part] = weight_ref[:, part * 480:(part + 1) * 480].astype(F32).T.astype(BF16)
    attended = []
    for head in range(4):
        query = (head_columns(query_ref, head).astype(F32) * SCALE).astype(BF16)
        probs = coarse_probs(query, head_columns(key_ref, head), bias_ref[...])
        attended.append(product_tn(head_columns(value_ref, head), probs.astype(BF16)).astype(BF16))
    attended = jnp.concatenate(attended, axis=0)
    for partner in range(4):
        outs[partner][:480, :] = held[place_ref[2] ^ partner]
        outs[partner][480:960, :] = grad_ref[...]
        outs[partner][960:, :] = attended


def coarse_kernel(query_ref, key_ref, value_ref, bias_ref, *refs):
    packets, weights, (mixed_ref, dq_ref, dk_ref, dv_ref) = refs[:4], refs[4:8], refs[8:]
    back_all = sum(
        product(weight[...], packet[480:960, :]) for weight, packet in zip(weights, packets)
    ).astype(BF16)
    mixed_ref[...] = sum(product(packet[:480, :], packet[960:, :]) for packet in packets).astype(BF16)
    query_grads, key_grads, value_grads = [], [], []
    for head in range(4):
        part = slice(head * HEAD_SIZE, (head + 1) * HEAD_SIZE)
        query = (query_ref[:, part].astype(F32) * SCALE).astype(BF16)
        key, value, back = key_ref[:, part], value_ref[:, part], back_all[part]
        probs = coarse_probs(query, key, bias_ref[...])
        rounded = probs.astype(BF16)
        attended = packets[0][960 + part.start:960 + part.stop, :]
        offset = jnp.sum(back.astype(F32) * attended.astype(F32), axis=0, keepdims=True)
        grad_scores = (probs * (product(value, back) - offset)).astype(BF16)
        query_grads.append(product_tn(key, grad_scores) * SCALE)
        key_grads.append(product(grad_scores, query))
        value_grads.append(product_nt(rounded, back))
    dq_ref[...] = jnp.concatenate(query_grads, axis=0).T.astype(BF16)
    dk_ref[...] = jnp.concatenate(key_grads, axis=1)
    dv_ref[...] = jnp.concatenate(value_grads, axis=1)


def sums_kernel(place_ref, *refs):
    od, dkv, outs, held = refs[:4], refs[4:8], refs[8:12], refs[12]
    for source in range(4):
        rows = slice(source * PIECE, (source + 1) * PIECE)
        held[source, :PIECE] = sum(part[source].astype(F32) for part in od).astype(BF16)
        held[source, PIECE:] = sum(part[rows, :].astype(F32) for part in dkv).astype(BF16)
    coarse = sum(part[4 * PIECE:, :].astype(F32) for part in dkv).astype(BF16)
    for partner in range(4):
        outs[partner][:2 * PIECE, :] = held[place_ref[0] ^ partner]
        outs[partner][2 * PIECE:, :] = coarse


def heads_kernel(place_ref, *refs):
    parts, (att_ref, dq_ref, dk_ref, dv_ref, coarse_ref, query_held, key_held) = refs[:4], refs[4:]
    for partner, part in enumerate(parts):
        head = place_ref[0] ^ partner
        rows = pl.ds(pl.multiple_of(head * HEAD_SIZE, HEAD_SIZE), HEAD_SIZE)
        att_ref[rows, :] = part[:HEAD_SIZE, :]
        query_held[rows, :] = part[HEAD_SIZE:PIECE, :].astype(F32)
        key_held[head] = part[PIECE:2 * PIECE, :]
        coarse_ref[head] = part[2 * PIECE:, :]
    dq_ref[...] = query_held[...].T.astype(BF16)
    dk_ref[...] = jnp.concatenate([key_held[head, :, :HEAD_SIZE] for head in range(4)], axis=1)
    dv_ref[...] = jnp.concatenate([key_held[head, :, HEAD_SIZE:] for head in range(4)], axis=1)


def last_kernel(place_ref, *refs):
    attended, packets, received = refs[:4], refs[4:8], refs[8:12]
    dk_ref, dv_ref, mixed_ref, dk_out, dv_out = refs[12:]
    mixed_ref[...] = sum(
        product(packet[:480, :], att[...]) for packet, att in zip(packets, attended)
    ).astype(BF16)
    for partner, ref in enumerate(received):
        rows = pl.ds(pl.multiple_of((place_ref[1] ^ partner) * 64, 64), 64)
        parts = [ref[head].astype(F32) for head in range(4)]
        keys = jnp.concatenate([part[:, :HEAD_SIZE] for part in parts], axis=1)
        values = jnp.concatenate([part[:, HEAD_SIZE:] for part in parts], axis=1)
        dk_out[rows, :] = (dk_ref[rows, :] + keys).astype(BF16)
        dv_out[rows, :] = (dv_ref[rows, :] + values).astype(BF16)


def swap(arrays, axes):
    out = [arrays[0]]
    for partner in (1, 2, 3):
        out.append(lax.ppermute(arrays[partner], axes, [(i, i ^ partner) for i in range(4)]))
    return out


def on_device(
    query_fine, key_fine, value_fine, query_coarse, key_coarse, value_coarse,
    out_weight, grad_fine, grad_coarse, fine_scale, coarse_scale,
):
    place = {name: lax.axis_index(name) for name in SEQ}
    head_of = place["xh"] * 2 + place["yh"]
    tile_of = place["yl"] * 2 + place["za"]
    placed = jnp.stack(
        [head_of, tile_of, lax.axis_index("head"), place["zc"] * 2 + place["zb"]]
    ).astype(jnp.int32)

    grads = swap([grad_fine.T] * 4, "head")
    weights = call(
        weight_blocks_kernel, (shape(256, 480),) * 4, [pltpu.VMEM((4, 256, 480), BF16)], 1, moved=2**21
    )(placed, out_weight)
    packed = call(
        pack_kernel, (shape(2 * PIECE, PIECE),) * 4, [pltpu.VMEM((4, 2 * PIECE, PIECE), BF16)], 1,
        flops=2 * 128 * 256 * 1920, moved=2**21,
    )(placed, query_fine, key_fine, value_fine, *grads, *weights)
    own_qb, own_kv = call(own_head_kernel, (shape(4, PIECE, PIECE),) * 2, (), 1, moved=2**19)(
        placed, *swap(packed, HEADS)
    )
    kv = swap([own_kv] * 4, QUERY_TILES)
    qb = swap([own_qb] * 4, KEY_TILES)

    ids = fine_scale.reshape(2, 2, 2, 2, 2, 2, PIECE)
    query_ids = lax.dynamic_index_in_dim(ids, place["zc"], 3, keepdims=False)
    query_ids = lax.dynamic_index_in_dim(query_ids, place["zb"], 3, keepdims=False)
    query_ids = query_ids.reshape(PIECES, 1, PIECE)
    key_ids = lax.dynamic_index_in_dim(ids, place["yl"], 2, keepdims=False)
    key_ids = lax.dynamic_index_in_dim(key_ids, place["za"], 4, keepdims=False)
    key_ids = key_ids.reshape(PIECES, PIECE)
    lane = lax.broadcasted_iota(jnp.int32, (PIECES, PIECE, PIECE), 2)
    onehot = (lane - HEAD_SIZE == key_ids[:, :, None]).astype(BF16)
    seen = jnp.sum(key_ids[None, :, 0] <= query_ids[3::4, 0, -1:], axis=1)
    steps = ((seen + STEP - 1) // STEP).astype(jnp.int32)

    coarse_rows = [
        lax.dynamic_slice(array, (tile_of * 64, 0), (64, 256)).reshape(64, 4, HEAD_SIZE)
        for array in (key_coarse, value_coarse)
    ]
    kvc = jnp.concatenate(
        [lax.dynamic_index_in_dim(rows, head_of, 1, keepdims=False) for rows in coarse_rows], axis=1
    )

    bias = jnp.where(coarse_scale[:, None] <= coarse_scale[None, :], 0.0, -1e9).astype(F32)
    packed = call(
        packet_kernel, (shape(1216, 256),) * 4, [pltpu.VMEM((4, 480, 256), BF16)], 1,
        flops=2**28, moved=2**22, exps=2**18,
    )(placed, query_coarse, key_coarse, value_coarse, bias, out_weight, grad_coarse.T)
    kv, qb, packed = lax.optimization_barrier((kv, qb, packed))

    half = [pltpu.VMEM((PIECES, PIECE, PIECE), BF16)]
    accum, stats = call(
        forward_kernel,
        (shape(QUERY_BLOCKS, HEAD_SIZE, QUERY_BLOCK, dtype=F32), shape(QUERY_BLOCKS, 8, QUERY_BLOCK, dtype=F32)),
        half * 2 + [
            pltpu.VMEM((QUERY_BLOCKS, PIECE, QUERY_BLOCK), BF16),
            pltpu.VMEM((2, STEP * PIECE, QUERY_BLOCK), F32),
        ],
        2,
    )(placed, steps, *kv, onehot, kvc, *qb, query_ids)
    all_stats = swap([stats] * 4, KEY_TILES)
    packets = swap(packed, "head")
    all_stats, packets = lax.optimization_barrier((all_stats, packets))
    parts = call(
        backward_kernel,
        (shape(4, PIECE, PIECE),) * 4 + (shape(4 * PIECE + 64, PIECE),) * 4,
        half * 3 + [pltpu.VMEM((PIECES, PIECE, PIECE), F32), pltpu.VMEM((64, PIECE), F32)],
        2, 10 * 2048 * 2112 * 64, 2**22, 2048 * 2112,
    )(placed, steps, *kv, onehot, kvc, *qb, query_ids, accum, *all_stats)

    dkv = swap(parts[4:], QUERY_TILES)
    od = swap(parts[:4], KEY_TILES)
    mixed_coarse, dq_coarse, dk_coarse, dv_coarse = call(
        coarse_kernel,
        (shape(480, 256), shape(256, 256), shape(256, 256, dtype=F32), shape(256, 256, dtype=F32)),
        flops=2**29, moved=2**22, exps=2**19,
    )(query_coarse, key_coarse, value_coarse, bias, *packets, *weights)
    dkv, dk_coarse = lax.optimization_barrier((dkv, dk_coarse))
    sums = call(
        sums_kernel, (shape(2 * PIECE + 64, PIECE),) * 4, [pltpu.VMEM((4, 2 * PIECE, PIECE), BF16)], 1, moved=2**21
    )(placed, *od, *dkv)
    att_fine, dq_fine, dk_fine, dv_fine, coarse_part = call(
        heads_kernel,
        (shape(256, PIECE),) + (shape(PIECE, 256),) * 3 + (shape(4, 64, PIECE),),
        [pltpu.VMEM((256, PIECE), F32), pltpu.VMEM((4, PIECE, PIECE), BF16)], 1, moved=2**20,
    )(placed, *swap(sums, HEADS))
    coarse_parts = swap([coarse_part] * 4, KEY_TILES)
    attended = swap([att_fine] * 4, "head")
    mixed_fine, dk_coarse, dv_coarse = call(
        last_kernel, (shape(480, PIECE), shape(256, 256), shape(256, 256)), (), 1, flops=2**27, moved=2**20
    )(placed, *attended, *packets, *coarse_parts, dk_coarse, dv_coarse)
    return (
        mixed_fine.T, mixed_coarse.T, dq_fine, dk_fine, dv_fine, dq_coarse, dk_coarse, dv_coarse,
    )


def solution(mesh):
    fine_mesh = Mesh(mesh.devices.reshape(2, 2, 2, 2, 2, 2, 4), SEQ + ("head",))
    in_specs = (
        P(SEQ, "head"), P(SEQ, "head"), P(SEQ, "head"),
        P(None, "head"), P(None, "head"), P(None, "head"),
        P("head", None), P(SEQ, "head"), P(None, "head"), P(), P(),
    )
    out_specs = (
        P(SEQ, "head"), P(None, "head"),
        P(SEQ, "head"), P(SEQ, "head"), P(SEQ, "head"),
        P(None, "head"), P(None, "head"), P(None, "head"),
    )
    return jax.shard_map(
        on_device, mesh=fine_mesh, in_specs=in_specs, out_specs=out_specs, check_vma=False
    )
```

```python
import jax
import jax.numpy as jnp
from jax import lax
from jax.experimental import pallas as pl
from jax.experimental.pallas import tpu as pltpu
from jax.sharding import Mesh
from jax.sharding import PartitionSpec as P

HEAD_SIZE = 64
SCALE = HEAD_SIZE ** (-0.5)
FSCALES = 3
HIDE = -30000.0
PIECE = 128
PIECES = 16
QUERY_BLOCKS = 4
QUERY_BLOCK = 512
STEP = 2
F32 = jnp.float32
BF16 = jnp.bfloat16

SEQ = ("xh", "yh", "yl", "zc", "zb", "za")
HEADS = ("xh", "yh")
QUERY_TILES = ("zc", "zb")
KEY_TILES = ("yl", "za")


def product(left, right):
    return jnp.dot(left, right, preferred_element_type=F32)


def product_nt(left, right):
    return lax.dot_general(left, right, (((1,), (1,)), ((), ())), preferred_element_type=F32)


def product_tn(left, right):
    return lax.dot_general(left, right, (((0,), (0,)), ((), ())), preferred_element_type=F32)


def call(kernel, outs, scratch=(), smem=0, flops=0, moved=0, exps=0):
    def run(*operands):
        return pl.pallas_call(
            kernel,
            out_shape=outs,
            in_specs=[pl.BlockSpec(memory_space=pltpu.SMEM)] * smem
            + [pl.BlockSpec(memory_space=pltpu.VMEM)] * (len(operands) - smem),
            out_specs=jax.tree.map(lambda _: pl.BlockSpec(memory_space=pltpu.VMEM), outs),
            scratch_shapes=list(scratch),
            compiler_params=pltpu.CompilerParams(vmem_limit_bytes=48 * 2**20),
            cost_estimate=pl.CostEstimate(
                flops=flops, bytes_accessed=moved, transcendentals=exps
            ),
        )(*operands)

    return run


def shape(*dims, dtype=BF16):
    return jax.ShapeDtypeStruct(dims, dtype)


def weight_blocks_kernel(place_ref, weight_ref, *refs):
    outs, held = refs[:4], refs[4]
    for part in range(4):
        held[part] = weight_ref[:, part * 480:(part + 1) * 480]
    for partner in range(4):
        outs[partner][...] = held[place_ref[2] ^ partner]


def pack_kernel(place_ref, query_ref, key_ref, value_ref, *refs):
    grads, weights, outs, held = refs[:4], refs[4:8], refs[8:12], refs[12]
    back = sum(product(weight[...], grad[...]) for weight, grad in zip(weights, grads)).astype(BF16)
    query = (query_ref[...].astype(F32) * SCALE).T.astype(BF16)
    for head in range(4):
        part = slice(head * HEAD_SIZE, (head + 1) * HEAD_SIZE)
        held[head, :HEAD_SIZE] = query[part]
        held[head, HEAD_SIZE:PIECE] = back[part]
        held[head, PIECE:] = jnp.concatenate([key_ref[:, part], value_ref[:, part]], axis=1)
    for partner in range(4):
        outs[partner][...] = held[place_ref[0] ^ partner]


def own_head_kernel(place_ref, *refs):
    parts, (qb_ref, kv_ref) = refs[:4], refs[4:]
    for partner, part in enumerate(parts):
        source = place_ref[0] ^ partner
        qb_ref[source] = part[:PIECE, :]
        kv_ref[source] = part[PIECE:, :]


def prepare_keys(place_ref, kv_refs, onehot_ref, masked_keys, plain, turned):
    lane = lax.broadcasted_iota(jnp.int32, (PIECE, PIECE), 1)
    for partner, ref in enumerate(kv_refs):
        for source in range(4):
            piece = 4 * source + (place_ref[3] ^ partner)
            both = ref[source]
            masked_keys[piece] = jnp.where(lane < HEAD_SIZE, both, onehot_ref[piece])
            turned[piece] = both.astype(F32).T.astype(BF16)
            if plain is not None:
                plain[piece] = both


def query_side(place_ref, qb_refs, ids_ref, block):
    both = jnp.concatenate([ref[block] for ref in qb_refs], axis=1)
    ids = jnp.concatenate([ids_ref[4 * block + (place_ref[1] ^ part)] for part in range(4)], axis=1)
    row = lax.broadcasted_iota(jnp.int32, (HEAD_SIZE, QUERY_BLOCK), 0)
    hidden = (row > ids) & (row < FSCALES)
    penalty = jnp.where(hidden, HIDE, 0.0).astype(BF16)
    return both, jnp.concatenate([both[:HEAD_SIZE], penalty], axis=0)


def rows_of(ref, step):
    return ref[pl.ds(STEP * step, STEP)].reshape(STEP * PIECE, PIECE)


def turned_of(ref, step, first):
    return jnp.concatenate(
        [ref[STEP * step + part, first:first + HEAD_SIZE, :] for part in range(STEP)], axis=1
    )


def coarse_side(kvc_ref):
    both = kvc_ref[...]
    lane = lax.broadcasted_iota(jnp.int32, both.shape, 1)
    only_keys = jnp.where(lane < HEAD_SIZE, both, jnp.zeros_like(both))
    return both, only_keys, both.astype(F32).T.astype(BF16)


def forward_kernel(
    place_ref, steps_ref, kv0, kv1, kv2, kv3, onehot_ref, kvc_ref, qb0, qb1, qb2, qb3, ids_ref,
    out_ref, stats_ref, masked_keys, turned, queries_held, scores_held,
):
    prepare_keys(place_ref, (kv0, kv1, kv2, kv3), onehot_ref, masked_keys, None, turned)
    _, coarse_keys, coarse_turned = coarse_side(kvc_ref)
    for block in range(QUERY_BLOCKS):
        _, queries = query_side(place_ref, (qb0, qb1, qb2, qb3), ids_ref, block)
        queries_held[block] = queries
        scores = product(coarse_keys, queries)
        top = jnp.max(scores, axis=0, keepdims=True)
        probs = jnp.exp(scores - top)
        total = jnp.sum(probs, axis=0, keepdims=True)
        out_ref[block] = product(coarse_turned[HEAD_SIZE:], probs.astype(BF16))
        stats_ref[block] = jnp.concatenate([top, total, jnp.zeros((6, QUERY_BLOCK), F32)], axis=0)

    def one_block(block, _):
        queries = queries_held[block]
        last = steps_ref[block] - 1
        scores_held[0] = product(rows_of(masked_keys, 0), queries)

        def one_step(step, carried):
            top, total, accum = carried
            slot = step & 1
            scores = scores_held[slot]
            scores_held[1 - slot] = product(rows_of(masked_keys, jnp.minimum(step + 1, last)), queries)
            new_top = jnp.maximum(top, jnp.max(scores, axis=0, keepdims=True))
            fade = jnp.exp(top - new_top)
            probs = jnp.exp(scores - new_top)
            total = total * fade + jnp.sum(probs, axis=0, keepdims=True)
            accum = accum * fade + product(turned_of(turned, step, HEAD_SIZE), probs.astype(BF16))
            return new_top, total, accum

        start = stats_ref[block]
        top, total, accum = lax.fori_loop(
            0, steps_ref[block], one_step, (start[0:1], start[1:2], out_ref[block])
        )
        back = jnp.concatenate([ref[block, HEAD_SIZE:, :] for ref in (qb0, qb1, qb2, qb3)], axis=1)
        offset = jnp.sum(back.astype(F32) * accum, axis=0, keepdims=True)
        out_ref[block] = accum
        stats_ref[block] = jnp.concatenate(
            [top, total, offset, jnp.zeros((5, QUERY_BLOCK), F32)], axis=0
        )
        return 0

    lax.fori_loop(0, QUERY_BLOCKS, one_block, 0)


def backward_kernel(
    place_ref, steps_ref, kv0, kv1, kv2, kv3, onehot_ref, kvc_ref, qb0, qb1, qb2, qb3, ids_ref, accum_ref, own_ref,
    stats1, stats2, stats3, od0, od1, od2, od3, dkv0, dkv1, dkv2, dkv3,
    masked_keys, plain, turned, key_sums, coarse_sums,
):
    prepare_keys(place_ref, (kv0, kv1, kv2, kv3), onehot_ref, masked_keys, plain, turned)
    coarse_both, coarse_keys, coarse_turned = coarse_side(kvc_ref)
    key_sums[...] = jnp.zeros_like(key_sums)
    coarse_sums[...] = jnp.zeros_like(coarse_sums)

    def one_block(block, _):
        both, queries = query_side(place_ref, (qb0, qb1, qb2, qb3), ids_ref, block)
        stats = [own_ref[block]]
        for partner, ref in enumerate((stats1, stats2, stats3), 1):
            theirs = ref[block]
            parts = [theirs[:, (part ^ partner) * PIECE:((part ^ partner) + 1) * PIECE] for part in range(4)]
            stats.append(jnp.concatenate(parts, axis=1))
        top = stats[0][0:1]
        for other in stats[1:]:
            top = jnp.maximum(top, other[0:1])
        total = jnp.zeros_like(top)
        offset = jnp.zeros_like(top)
        for other in stats:
            fade = jnp.exp(other[0:1] - top)
            total = total + fade * other[1:2]
            offset = offset + fade * other[2:3]
        offset = offset / total
        log_total = top + jnp.log(total)
        attended = accum_ref[block] * (jnp.exp(own_ref[block][0:1] - top) / total)
        back = jnp.concatenate(
            [jnp.zeros((HEAD_SIZE, QUERY_BLOCK), BF16), both[HEAD_SIZE:]], axis=0
        )
        token_rows = both.astype(F32).T
        lane = lax.broadcasted_iota(jnp.int32, token_rows.shape, 1)
        query_rows = jnp.where(lane < HEAD_SIZE, token_rows, 0.0).astype(BF16)
        back_rows = jnp.where(lane < HEAD_SIZE, 0.0, token_rows).astype(BF16)

        def terms(only_keys, key_value, key_turned):
            probs = jnp.exp(product(only_keys, queries) - log_total)
            grad_probs = product(key_value, back)
            grad_scores = (probs * (grad_probs - offset)).astype(BF16)
            key_side = product(grad_scores, query_rows) + product(probs.astype(BF16), back_rows)
            return product(key_turned, grad_scores), key_side

        query_grad, coarse_term = terms(coarse_keys, coarse_both, coarse_turned[:HEAD_SIZE])
        coarse_sums[...] += coarse_term

        def one_step(step, query_grad):
            query_term, key_side = terms(
                rows_of(masked_keys, step), rows_of(plain, step), turned_of(turned, step, 0)
            )
            key_sums[pl.ds(STEP * step, STEP)] += key_side.reshape(STEP, PIECE, PIECE)
            return query_grad + query_term

        query_grad = lax.fori_loop(0, steps_ref[block], one_step, query_grad)
        both_out = jnp.concatenate([attended, query_grad * SCALE], axis=0).astype(BF16)
        for part, ref in enumerate((od0, od1, od2, od3)):
            ref[block] = both_out[:, part * PIECE:(part + 1) * PIECE]
        return 0

    lax.fori_loop(0, QUERY_BLOCKS, one_block, 0)
    coarse = coarse_sums[...].astype(BF16)
    for partner, ref in enumerate((dkv0, dkv1, dkv2, dkv3)):
        for source in range(4):
            piece = key_sums[4 * source + (place_ref[3] ^ partner)]
            ref[source * PIECE:(source + 1) * PIECE, :] = piece.astype(BF16)
        ref[4 * PIECE:, :] = coarse


def coarse_probs(query, key, bias):
    scores = product_nt(key, query) + bias
    top = jnp.max(scores, axis=0, keepdims=True)
    total = jnp.sum(jnp.exp(scores - top), axis=0, keepdims=True)
    return jnp.exp(scores - (top + jnp.log(total)))


def head_columns(ref, head):
    return ref[:, head * HEAD_SIZE:(head + 1) * HEAD_SIZE]


def coarse_packet_kernel(query_ref, key_ref, value_ref, bias_ref, grad_ref, out_ref):
    out_ref[:480, :] = grad_ref[...]
    for head in range(4):
        query = (head_columns(query_ref, head).astype(F32) * SCALE).astype(BF16)
        probs = coarse_probs(query, head_columns(key_ref, head), bias_ref[...])
        attended = product_tn(head_columns(value_ref, head), probs.astype(BF16))
        out_ref[480 + head * HEAD_SIZE:480 + (head + 1) * HEAD_SIZE, :] = attended.astype(BF16)


def coarse_kernel(query_ref, key_ref, value_ref, bias_ref, *refs):
    packets, weights, columns, (mixed_ref, dq_ref, dk_ref, dv_ref) = refs[:4], refs[4:8], refs[8:12], refs[12:]
    back_all = sum(
        product(weight[...], packet[:480, :]) for weight, packet in zip(weights, packets)
    ).astype(BF16)
    mixed_ref[...] = sum(
        product_tn(column[...], packet[480:, :]) for column, packet in zip(columns, packets)
    ).astype(BF16)
    query_grads, key_grads, value_grads = [], [], []
    for head in range(4):
        part = slice(head * HEAD_SIZE, (head + 1) * HEAD_SIZE)
        query = (query_ref[:, part].astype(F32) * SCALE).astype(BF16)
        key, value, back = key_ref[:, part], value_ref[:, part], back_all[part]
        probs = coarse_probs(query, key, bias_ref[...])
        rounded = probs.astype(BF16)
        attended = packets[0][480 + part.start:480 + part.stop, :]
        offset = jnp.sum(back.astype(F32) * attended.astype(F32), axis=0, keepdims=True)
        grad_scores = (probs * (product(value, back) - offset)).astype(BF16)
        query_grads.append(product_tn(key, grad_scores) * SCALE)
        key_grads.append(product(grad_scores, query))
        value_grads.append(product_nt(rounded, back))
    dq_ref[...] = jnp.concatenate(query_grads, axis=0).T.astype(BF16)
    dk_ref[...] = jnp.concatenate(key_grads, axis=1)
    dv_ref[...] = jnp.concatenate(value_grads, axis=1)


def sums_kernel(place_ref, *refs):
    od, dkv, outs, held = refs[:4], refs[4:8], refs[8:12], refs[12]
    for source in range(4):
        rows = slice(source * PIECE, (source + 1) * PIECE)
        held[source, :PIECE] = sum(part[source].astype(F32) for part in od).astype(BF16)
        held[source, PIECE:] = sum(part[rows, :].astype(F32) for part in dkv).astype(BF16)
    coarse = sum(part[4 * PIECE:, :].astype(F32) for part in dkv).astype(BF16)
    for partner in range(4):
        outs[partner][:2 * PIECE, :] = held[place_ref[0] ^ partner]
        outs[partner][2 * PIECE:, :] = coarse


def heads_kernel(place_ref, *refs):
    parts, (att_ref, dq_ref, dk_ref, dv_ref, coarse_ref, query_held, key_held) = refs[:4], refs[4:]
    for partner, part in enumerate(parts):
        head = place_ref[0] ^ partner
        rows = pl.ds(pl.multiple_of(head * HEAD_SIZE, HEAD_SIZE), HEAD_SIZE)
        att_ref[rows, :] = part[:HEAD_SIZE, :]
        query_held[rows, :] = part[HEAD_SIZE:PIECE, :].astype(F32)
        key_held[head] = part[PIECE:2 * PIECE, :]
        coarse_ref[head] = part[2 * PIECE:, :]
    dq_ref[...] = query_held[...].T.astype(BF16)
    dk_ref[...] = jnp.concatenate([key_held[head, :, :HEAD_SIZE] for head in range(4)], axis=1)
    dv_ref[...] = jnp.concatenate([key_held[head, :, HEAD_SIZE:] for head in range(4)], axis=1)


def last_kernel(place_ref, *refs):
    attended, columns, received = refs[:4], refs[4:8], refs[8:12]
    dk_ref, dv_ref, mixed_ref, dk_out, dv_out = refs[12:]
    mixed_ref[...] = sum(
        product_tn(column[...], att[...]) for column, att in zip(columns, attended)
    ).astype(BF16)
    for partner, ref in enumerate(received):
        rows = pl.ds(pl.multiple_of((place_ref[1] ^ partner) * 64, 64), 64)
        parts = [ref[head].astype(F32) for head in range(4)]
        keys = jnp.concatenate([part[:, :HEAD_SIZE] for part in parts], axis=1)
        values = jnp.concatenate([part[:, HEAD_SIZE:] for part in parts], axis=1)
        dk_out[rows, :] = (dk_ref[rows, :] + keys).astype(BF16)
        dv_out[rows, :] = (dv_ref[rows, :] + values).astype(BF16)


def swap(arrays, axes):
    out = [arrays[0]]
    for partner in (1, 2, 3):
        out.append(lax.ppermute(arrays[partner], axes, [(i, i ^ partner) for i in range(4)]))
    return out


def on_device(
    query_fine, key_fine, value_fine, query_coarse, key_coarse, value_coarse,
    out_weight, grad_fine, grad_coarse, fine_scale, coarse_scale,
):
    place = {name: lax.axis_index(name) for name in SEQ}
    head_of = place["xh"] * 2 + place["yh"]
    tile_of = place["yl"] * 2 + place["za"]
    placed = jnp.stack(
        [head_of, tile_of, lax.axis_index("head"), place["zc"] * 2 + place["zb"]]
    ).astype(jnp.int32)

    grads = swap([grad_fine.T] * 4, "head")
    weights = call(
        weight_blocks_kernel, (shape(256, 480),) * 4, [pltpu.VMEM((4, 256, 480), BF16)], 1, moved=2**21
    )(placed, out_weight)
    packed = call(
        pack_kernel, (shape(2 * PIECE, PIECE),) * 4, [pltpu.VMEM((4, 2 * PIECE, PIECE), BF16)], 1,
        flops=2 * 128 * 256 * 1920, moved=2**21,
    )(placed, query_fine, key_fine, value_fine, *grads, *weights)
    own_qb, own_kv = call(own_head_kernel, (shape(4, PIECE, PIECE),) * 2, (), 1, moved=2**19)(
        placed, *swap(packed, HEADS)
    )
    kv = swap([own_kv] * 4, QUERY_TILES)
    qb = swap([own_qb] * 4, KEY_TILES)

    ids = fine_scale.reshape(2, 2, 2, 2, 2, 2, PIECE)
    query_ids = lax.dynamic_index_in_dim(ids, place["zc"], 3, keepdims=False)
    query_ids = lax.dynamic_index_in_dim(query_ids, place["zb"], 3, keepdims=False)
    query_ids = query_ids.reshape(PIECES, 1, PIECE)
    key_ids = lax.dynamic_index_in_dim(ids, place["yl"], 2, keepdims=False)
    key_ids = lax.dynamic_index_in_dim(key_ids, place["za"], 4, keepdims=False)
    key_ids = key_ids.reshape(PIECES, PIECE)
    lane = lax.broadcasted_iota(jnp.int32, (PIECES, PIECE, PIECE), 2)
    onehot = (lane - HEAD_SIZE == key_ids[:, :, None]).astype(BF16)
    seen = jnp.sum(key_ids[None, :, 0] <= query_ids[3::4, 0, -1:], axis=1)
    steps = ((seen + STEP - 1) // STEP).astype(jnp.int32)

    coarse_rows = [
        lax.dynamic_slice(array, (tile_of * 64, 0), (64, 256)).reshape(64, 4, HEAD_SIZE)
        for array in (key_coarse, value_coarse)
    ]
    kvc = jnp.concatenate(
        [lax.dynamic_index_in_dim(rows, head_of, 1, keepdims=False) for rows in coarse_rows], axis=1
    )

    bias = jnp.where(coarse_scale[:, None] <= coarse_scale[None, :], 0.0, -1e9).astype(F32)
    packet = call(coarse_packet_kernel, shape(736, 256), flops=2**28, moved=2**22, exps=2**18)(
        query_coarse, key_coarse, value_coarse, bias, grad_coarse.T
    )
    kv, qb, packet = lax.optimization_barrier((kv, qb, packet))

    half = [pltpu.VMEM((PIECES, PIECE, PIECE), BF16)]
    accum, stats = call(
        forward_kernel,
        (shape(QUERY_BLOCKS, HEAD_SIZE, QUERY_BLOCK, dtype=F32), shape(QUERY_BLOCKS, 8, QUERY_BLOCK, dtype=F32)),
        half * 2 + [
            pltpu.VMEM((QUERY_BLOCKS, PIECE, QUERY_BLOCK), BF16),
            pltpu.VMEM((2, STEP * PIECE, QUERY_BLOCK), F32),
        ],
        2,
    )(placed, steps, *kv, onehot, kvc, *qb, query_ids)
    all_stats = swap([stats] * 4, KEY_TILES)
    packets = swap([packet] * 4, "head")
    all_stats, packets = lax.optimization_barrier((all_stats, packets))
    weights, stats = lax.optimization_barrier((weights, stats))
    columns = swap(weights, "head")
    parts = call(
        backward_kernel,
        (shape(4, PIECE, PIECE),) * 4 + (shape(4 * PIECE + 64, PIECE),) * 4,
        half * 3 + [pltpu.VMEM((PIECES, PIECE, PIECE), F32), pltpu.VMEM((64, PIECE), F32)],
        2, 10 * 2048 * 2112 * 64, 2**22, 2048 * 2112,
    )(placed, steps, *kv, onehot, kvc, *qb, query_ids, accum, *all_stats)

    parts, columns = lax.optimization_barrier((parts, columns))
    dkv = swap(parts[4:], QUERY_TILES)
    od = swap(parts[:4], KEY_TILES)
    mixed_coarse, dq_coarse, dk_coarse, dv_coarse = call(
        coarse_kernel,
        (shape(480, 256), shape(256, 256), shape(256, 256, dtype=F32), shape(256, 256, dtype=F32)),
        flops=2**29, moved=2**22, exps=2**19,
    )(query_coarse, key_coarse, value_coarse, bias, *packets, *weights, *columns)
    dkv, dk_coarse = lax.optimization_barrier((dkv, dk_coarse))
    sums = call(
        sums_kernel, (shape(2 * PIECE + 64, PIECE),) * 4, [pltpu.VMEM((4, 2 * PIECE, PIECE), BF16)], 1, moved=2**21
    )(placed, *od, *dkv)
    att_fine, dq_fine, dk_fine, dv_fine, coarse_part = call(
        heads_kernel,
        (shape(256, PIECE),) + (shape(PIECE, 256),) * 3 + (shape(4, 64, PIECE),),
        [pltpu.VMEM((256, PIECE), F32), pltpu.VMEM((4, PIECE, PIECE), BF16)], 1, moved=2**20,
    )(placed, *swap(sums, HEADS))
    coarse_parts = swap([coarse_part] * 4, KEY_TILES)
    attended = swap([att_fine] * 4, "head")
    mixed_fine, dk_coarse, dv_coarse = call(
        last_kernel, (shape(480, PIECE), shape(256, 256), shape(256, 256)), (), 1, flops=2**27, moved=2**20
    )(placed, *attended, *columns, *coarse_parts, dk_coarse, dv_coarse)
    return (
        mixed_fine.T, mixed_coarse.T, dq_fine, dk_fine, dv_fine, dq_coarse, dk_coarse, dv_coarse,
    )


def solution(mesh):
    fine_mesh = Mesh(mesh.devices.reshape(2, 2, 2, 2, 2, 2, 4), SEQ + ("head",))
    in_specs = (
        P(SEQ, "head"), P(SEQ, "head"), P(SEQ, "head"),
        P(None, "head"), P(None, "head"), P(None, "head"),
        P("head", None), P(SEQ, "head"), P(None, "head"), P(), P(),
    )
    out_specs = (
        P(SEQ, "head"), P(None, "head"),
        P(SEQ, "head"), P(SEQ, "head"), P(SEQ, "head"),
        P(None, "head"), P(None, "head"), P(None, "head"),
    )
    return jax.shard_map(
        on_device, mesh=fine_mesh, in_specs=in_specs, out_specs=out_specs, check_vma=False
    )
```

```python
import jax
import jax.numpy as jnp
from jax import lax
from jax.experimental import pallas as pl
from jax.experimental.pallas import tpu as pltpu
from jax.sharding import Mesh
from jax.sharding import PartitionSpec as P

HEAD_SIZE = 64
SCALE = HEAD_SIZE ** (-0.5)
FSCALES = 3
HIDE = -30000.0
PIECE = 128
PIECES = 16
QUERY_BLOCKS = 4
QUERY_BLOCK = 512
STEP = 2
F32 = jnp.float32
BF16 = jnp.bfloat16

SEQ = ("xh", "yh", "yl", "zc", "zb", "za")
HEADS = ("xh", "yh")
QUERY_TILES = ("zc", "zb")
KEY_TILES = ("yl", "za")


def product(left, right):
    return jnp.dot(left, right, preferred_element_type=F32)


def product_nt(left, right):
    return lax.dot_general(left, right, (((1,), (1,)), ((), ())), preferred_element_type=F32)


def product_tn(left, right):
    return lax.dot_general(left, right, (((0,), (0,)), ((), ())), preferred_element_type=F32)


def call(kernel, outs, scratch=(), smem=0, flops=0, moved=0, exps=0):
    def run(*operands):
        return pl.pallas_call(
            kernel,
            out_shape=outs,
            in_specs=[pl.BlockSpec(memory_space=pltpu.SMEM)] * smem
            + [pl.BlockSpec(memory_space=pltpu.VMEM)] * (len(operands) - smem),
            out_specs=jax.tree.map(lambda _: pl.BlockSpec(memory_space=pltpu.VMEM), outs),
            scratch_shapes=list(scratch),
            compiler_params=pltpu.CompilerParams(vmem_limit_bytes=48 * 2**20),
            cost_estimate=pl.CostEstimate(
                flops=flops, bytes_accessed=moved, transcendentals=exps
            ),
        )(*operands)

    return run


def shape(*dims, dtype=BF16):
    return jax.ShapeDtypeStruct(dims, dtype)


def weight_blocks_kernel(place_ref, weight_ref, *refs):
    outs, held = refs[:4], refs[4]
    for part in range(4):
        held[part] = weight_ref[:, part * 480:(part + 1) * 480]
    for partner in range(4):
        outs[partner][...] = held[place_ref[2] ^ partner]


def pack_keys_kernel(place_ref, key_ref, value_ref, *refs):
    outs, held = refs[:4], refs[4]
    for head in range(4):
        both = [head_columns(key_ref, head), head_columns(value_ref, head)]
        held[head] = jnp.concatenate(both, axis=1)
    for partner in range(4):
        outs[partner][...] = held[place_ref[0] ^ partner]


def pack_queries_kernel(place_ref, query_ref, *refs):
    grads, weights, outs, held = refs[:4], refs[4:8], refs[8:12], refs[12]
    back = sum(product(weight[...], grad[...]) for weight, grad in zip(weights, grads)).astype(BF16)
    query = (query_ref[...].astype(F32) * SCALE).T.astype(BF16)
    for head in range(4):
        part = slice(head * HEAD_SIZE, (head + 1) * HEAD_SIZE)
        held[head, :HEAD_SIZE] = query[part]
        held[head, HEAD_SIZE:] = back[part]
    for partner in range(4):
        outs[partner][...] = held[place_ref[0] ^ partner]


def own_head_kernel(place_ref, *refs):
    for partner in range(4):
        refs[4][place_ref[0] ^ partner] = refs[partner][...]


def prepare_keys(place_ref, kv_refs, onehot_ref, masked_keys, plain, turned):
    lane = lax.broadcasted_iota(jnp.int32, (PIECE, PIECE), 1)
    for partner, ref in enumerate(kv_refs):
        for source in range(4):
            piece = 4 * source + (place_ref[3] ^ partner)
            both = ref[source]
            masked_keys[piece] = jnp.where(lane < HEAD_SIZE, both, onehot_ref[piece])
            turned[piece] = both.astype(F32).T.astype(BF16)
            if plain is not None:
                plain[piece] = both


def query_side(place_ref, qb_refs, ids_ref, block):
    both = jnp.concatenate([ref[block] for ref in qb_refs], axis=1)
    ids = jnp.concatenate([ids_ref[4 * block + (place_ref[1] ^ part)] for part in range(4)], axis=1)
    row = lax.broadcasted_iota(jnp.int32, (HEAD_SIZE, QUERY_BLOCK), 0)
    hidden = (row > ids) & (row < FSCALES)
    penalty = jnp.where(hidden, HIDE, 0.0).astype(BF16)
    return both, jnp.concatenate([both[:HEAD_SIZE], penalty], axis=0)


def rows_of(ref, step):
    return ref[pl.ds(STEP * step, STEP)].reshape(STEP * PIECE, PIECE)


def turned_of(ref, step, first):
    return jnp.concatenate(
        [ref[STEP * step + part, first:first + HEAD_SIZE, :] for part in range(STEP)], axis=1
    )


def coarse_side(kvc_ref):
    both = kvc_ref[...]
    lane = lax.broadcasted_iota(jnp.int32, both.shape, 1)
    only_keys = jnp.where(lane < HEAD_SIZE, both, jnp.zeros_like(both))
    return both, only_keys, both.astype(F32).T.astype(BF16)


def forward_kernel(
    place_ref, steps_ref, kv0, kv1, kv2, kv3, onehot_ref, kvc_ref, qb0, qb1, qb2, qb3, ids_ref,
    out_ref, stats_ref, masked_keys, turned, queries_held, scores_held,
):
    prepare_keys(place_ref, (kv0, kv1, kv2, kv3), onehot_ref, masked_keys, None, turned)
    _, coarse_keys, coarse_turned = coarse_side(kvc_ref)
    for block in range(QUERY_BLOCKS):
        _, queries = query_side(place_ref, (qb0, qb1, qb2, qb3), ids_ref, block)
        queries_held[block] = queries
        scores = product(coarse_keys, queries)
        top = jnp.max(scores, axis=0, keepdims=True)
        probs = jnp.exp(scores - top)
        total = jnp.sum(probs, axis=0, keepdims=True)
        out_ref[block] = product(coarse_turned[HEAD_SIZE:], probs.astype(BF16))
        stats_ref[block] = jnp.concatenate([top, total, jnp.zeros((6, QUERY_BLOCK), F32)], axis=0)

    def one_block(block, _):
        queries = queries_held[block]
        last = steps_ref[block] - 1
        scores_held[0] = product(rows_of(masked_keys, 0), queries)

        def one_step(step, carried):
            top, total, accum = carried
            slot = step & 1
            scores = scores_held[slot]
            scores_held[1 - slot] = product(rows_of(masked_keys, jnp.minimum(step + 1, last)), queries)
            new_top = jnp.maximum(top, jnp.max(scores, axis=0, keepdims=True))
            fade = jnp.exp(top - new_top)
            probs = jnp.exp(scores - new_top)
            total = total * fade + jnp.sum(probs, axis=0, keepdims=True)
            accum = accum * fade + product(turned_of(turned, step, HEAD_SIZE), probs.astype(BF16))
            return new_top, total, accum

        start = stats_ref[block]
        top, total, accum = lax.fori_loop(
            0, steps_ref[block], one_step, (start[0:1], start[1:2], out_ref[block])
        )
        back = jnp.concatenate([ref[block, HEAD_SIZE:, :] for ref in (qb0, qb1, qb2, qb3)], axis=1)
        offset = jnp.sum(back.astype(F32) * accum, axis=0, keepdims=True)
        out_ref[block] = accum
        stats_ref[block] = jnp.concatenate(
            [top, total, offset, jnp.zeros((5, QUERY_BLOCK), F32)], axis=0
        )
        return 0

    lax.fori_loop(0, QUERY_BLOCKS, one_block, 0)


def backward_kernel(
    place_ref, steps_ref, kv0, kv1, kv2, kv3, onehot_ref, kvc_ref, qb0, qb1, qb2, qb3, ids_ref, accum_ref, own_ref,
    stats1, stats2, stats3, od0, od1, od2, od3, dkv0, dkv1, dkv2, dkv3,
    masked_keys, plain, turned, key_sums, coarse_sums,
):
    prepare_keys(place_ref, (kv0, kv1, kv2, kv3), onehot_ref, masked_keys, plain, turned)
    coarse_both, coarse_keys, coarse_turned = coarse_side(kvc_ref)
    key_sums[...] = jnp.zeros_like(key_sums)
    coarse_sums[...] = jnp.zeros_like(coarse_sums)

    def one_block(block, _):
        both, queries = query_side(place_ref, (qb0, qb1, qb2, qb3), ids_ref, block)
        stats = [own_ref[block]]
        for partner, ref in enumerate((stats1, stats2, stats3), 1):
            theirs = ref[block]
            parts = [theirs[:, (part ^ partner) * PIECE:((part ^ partner) + 1) * PIECE] for part in range(4)]
            stats.append(jnp.concatenate(parts, axis=1))
        top = stats[0][0:1]
        for other in stats[1:]:
            top = jnp.maximum(top, other[0:1])
        total = jnp.zeros_like(top)
        offset = jnp.zeros_like(top)
        for other in stats:
            fade = jnp.exp(other[0:1] - top)
            total = total + fade * other[1:2]
            offset = offset + fade * other[2:3]
        offset = offset / total
        log_total = top + jnp.log(total)
        attended = accum_ref[block] * (jnp.exp(own_ref[block][0:1] - top) / total)
        back = jnp.concatenate(
            [jnp.zeros((HEAD_SIZE, QUERY_BLOCK), BF16), both[HEAD_SIZE:]], axis=0
        )
        token_rows = both.astype(F32).T
        lane = lax.broadcasted_iota(jnp.int32, token_rows.shape, 1)
        query_rows = jnp.where(lane < HEAD_SIZE, token_rows, 0.0).astype(BF16)
        back_rows = jnp.where(lane < HEAD_SIZE, 0.0, token_rows).astype(BF16)

        def terms(only_keys, key_value, key_turned):
            probs = jnp.exp(product(only_keys, queries) - log_total)
            grad_probs = product(key_value, back)
            grad_scores = (probs * (grad_probs - offset)).astype(BF16)
            key_side = product(grad_scores, query_rows) + product(probs.astype(BF16), back_rows)
            return product(key_turned, grad_scores), key_side

        query_grad, coarse_term = terms(coarse_keys, coarse_both, coarse_turned[:HEAD_SIZE])
        coarse_sums[...] += coarse_term

        def one_step(step, query_grad):
            query_term, key_side = terms(
                rows_of(masked_keys, step), rows_of(plain, step), turned_of(turned, step, 0)
            )
            key_sums[pl.ds(STEP * step, STEP)] += key_side.reshape(STEP, PIECE, PIECE)
            return query_grad + query_term

        query_grad = lax.fori_loop(0, steps_ref[block], one_step, query_grad)
        both_out = jnp.concatenate([attended, query_grad * SCALE], axis=0).astype(BF16)
        for part, ref in enumerate((od0, od1, od2, od3)):
            ref[block] = both_out[:, part * PIECE:(part + 1) * PIECE]
        return 0

    lax.fori_loop(0, QUERY_BLOCKS, one_block, 0)
    coarse = coarse_sums[...].astype(BF16)
    for partner, ref in enumerate((dkv0, dkv1, dkv2, dkv3)):
        for source in range(4):
            piece = key_sums[4 * source + (place_ref[3] ^ partner)]
            ref[source * PIECE:(source + 1) * PIECE, :] = piece.astype(BF16)
        ref[4 * PIECE:, :] = coarse


def coarse_probs(query, key, bias):
    scores = product_nt(key, query) + bias
    top = jnp.max(scores, axis=0, keepdims=True)
    total = jnp.sum(jnp.exp(scores - top), axis=0, keepdims=True)
    return jnp.exp(scores - (top + jnp.log(total)))


def head_columns(ref, head):
    return ref[:, head * HEAD_SIZE:(head + 1) * HEAD_SIZE]


def coarse_packet_kernel(query_ref, key_ref, value_ref, bias_ref, grad_ref, out_ref):
    out_ref[:480, :] = grad_ref[...]
    for head in range(4):
        query = (head_columns(query_ref, head).astype(F32) * SCALE).astype(BF16)
        probs = coarse_probs(query, head_columns(key_ref, head), bias_ref[...])
        attended = product_tn(head_columns(value_ref, head), probs.astype(BF16))
        out_ref[480 + head * HEAD_SIZE:480 + (head + 1) * HEAD_SIZE, :] = attended.astype(BF16)


def coarse_kernel(query_ref, key_ref, value_ref, bias_ref, *refs):
    packets, weights, columns, (mixed_ref, dq_ref, dk_ref, dv_ref) = refs[:4], refs[4:8], refs[8:12], refs[12:]
    back_all = sum(
        product(weight[...], packet[:480, :]) for weight, packet in zip(weights, packets)
    ).astype(BF16)
    mixed_ref[...] = sum(
        product_tn(column[...], packet[480:, :]) for column, packet in zip(columns, packets)
    ).astype(BF16)
    query_grads, key_grads, value_grads = [], [], []
    for head in range(4):
        part = slice(head * HEAD_SIZE, (head + 1) * HEAD_SIZE)
        query = (query_ref[:, part].astype(F32) * SCALE).astype(BF16)
        key, value, back = key_ref[:, part], value_ref[:, part], back_all[part]
        probs = coarse_probs(query, key, bias_ref[...])
        rounded = probs.astype(BF16)
        attended = packets[0][480 + part.start:480 + part.stop, :]
        offset = jnp.sum(back.astype(F32) * attended.astype(F32), axis=0, keepdims=True)
        grad_scores = (probs * (product(value, back) - offset)).astype(BF16)
        query_grads.append(product_tn(key, grad_scores) * SCALE)
        key_grads.append(product(grad_scores, query))
        value_grads.append(product_nt(rounded, back))
    dq_ref[...] = jnp.concatenate(query_grads, axis=0).T.astype(BF16)
    dk_ref[...] = jnp.concatenate(key_grads, axis=1)
    dv_ref[...] = jnp.concatenate(value_grads, axis=1)


def sums_kernel(place_ref, *refs):
    od, dkv, outs, held = refs[:4], refs[4:8], refs[8:12], refs[12]
    for source in range(4):
        rows = slice(source * PIECE, (source + 1) * PIECE)
        held[source, :PIECE] = sum(part[source].astype(F32) for part in od).astype(BF16)
        held[source, PIECE:] = sum(part[rows, :].astype(F32) for part in dkv).astype(BF16)
    coarse = sum(part[4 * PIECE:, :].astype(F32) for part in dkv).astype(BF16)
    for partner in range(4):
        outs[partner][:2 * PIECE, :] = held[place_ref[0] ^ partner]
        outs[partner][2 * PIECE:, :] = coarse


def heads_kernel(place_ref, *refs):
    parts, (att_ref, dq_ref, dk_ref, dv_ref, coarse_ref, query_held, key_held) = refs[:4], refs[4:]
    for partner, part in enumerate(parts):
        head = place_ref[0] ^ partner
        rows = pl.ds(pl.multiple_of(head * HEAD_SIZE, HEAD_SIZE), HEAD_SIZE)
        att_ref[rows, :] = part[:HEAD_SIZE, :]
        query_held[rows, :] = part[HEAD_SIZE:PIECE, :].astype(F32)
        key_held[head] = part[PIECE:2 * PIECE, :]
        coarse_ref[head] = part[2 * PIECE:, :]
    dq_ref[...] = query_held[...].T.astype(BF16)
    dk_ref[...] = jnp.concatenate([key_held[head, :, :HEAD_SIZE] for head in range(4)], axis=1)
    dv_ref[...] = jnp.concatenate([key_held[head, :, HEAD_SIZE:] for head in range(4)], axis=1)


def last_kernel(place_ref, *refs):
    attended, columns, received = refs[:4], refs[4:8], refs[8:12]
    dk_ref, dv_ref, mixed_ref, dk_out, dv_out = refs[12:]
    mixed_ref[...] = sum(
        product_tn(column[...], att[...]) for column, att in zip(columns, attended)
    ).astype(BF16)
    for partner, ref in enumerate(received):
        rows = pl.ds(pl.multiple_of((place_ref[1] ^ partner) * 64, 64), 64)
        parts = [ref[head].astype(F32) for head in range(4)]
        keys = jnp.concatenate([part[:, :HEAD_SIZE] for part in parts], axis=1)
        values = jnp.concatenate([part[:, HEAD_SIZE:] for part in parts], axis=1)
        dk_out[rows, :] = (dk_ref[rows, :] + keys).astype(BF16)
        dv_out[rows, :] = (dv_ref[rows, :] + values).astype(BF16)


def swap(arrays, axes):
    out = [arrays[0]]
    for partner in (1, 2, 3):
        out.append(lax.ppermute(arrays[partner], axes, [(i, i ^ partner) for i in range(4)]))
    return out


def on_device(
    query_fine, key_fine, value_fine, query_coarse, key_coarse, value_coarse,
    out_weight, grad_fine, grad_coarse, fine_scale, coarse_scale,
):
    place = {name: lax.axis_index(name) for name in SEQ}
    head_of = place["xh"] * 2 + place["yh"]
    tile_of = place["yl"] * 2 + place["za"]
    placed = jnp.stack(
        [head_of, tile_of, lax.axis_index("head"), place["zc"] * 2 + place["zb"]]
    ).astype(jnp.int32)

    grads = swap([grad_fine.T] * 4, "head")
    swapped = (shape(PIECE, PIECE),) * 4
    packing = [pltpu.VMEM((4, PIECE, PIECE), BF16)]

    def own_head(pieces):
        return call(own_head_kernel, shape(4, PIECE, PIECE), (), 1, moved=2**18)(placed, *swap(pieces, HEADS))

    own_kv = own_head(
        call(pack_keys_kernel, swapped, packing, 1, moved=2**18)(placed, key_fine, value_fine)
    )
    kv = swap([own_kv] * 4, QUERY_TILES)
    weights = call(
        weight_blocks_kernel, (shape(256, 480),) * 4, [pltpu.VMEM((4, 256, 480), BF16)], 1, moved=2**21
    )(placed, out_weight)
    own_qb = own_head(
        call(pack_queries_kernel, swapped, packing, 1, flops=2 * 128 * 256 * 1920, moved=2**21)(
            placed, query_fine, *grads, *weights
        )
    )
    qb = swap([own_qb] * 4, KEY_TILES)

    ids = fine_scale.reshape(2, 2, 2, 2, 2, 2, PIECE)
    query_ids = lax.dynamic_index_in_dim(ids, place["zc"], 3, keepdims=False)
    query_ids = lax.dynamic_index_in_dim(query_ids, place["zb"], 3, keepdims=False)
    query_ids = query_ids.reshape(PIECES, 1, PIECE)
    key_ids = lax.dynamic_index_in_dim(ids, place["yl"], 2, keepdims=False)
    key_ids = lax.dynamic_index_in_dim(key_ids, place["za"], 4, keepdims=False)
    key_ids = key_ids.reshape(PIECES, PIECE)
    lane = lax.broadcasted_iota(jnp.int32, (PIECES, PIECE, PIECE), 2)
    onehot = (lane - HEAD_SIZE == key_ids[:, :, None]).astype(BF16)
    seen = jnp.sum(key_ids[None, :, 0] <= query_ids[3::4, 0, -1:], axis=1)
    steps = ((seen + STEP - 1) // STEP).astype(jnp.int32)

    coarse_rows = [
        lax.dynamic_slice(array, (tile_of * 64, 0), (64, 256)).reshape(64, 4, HEAD_SIZE)
        for array in (key_coarse, value_coarse)
    ]
    kvc = jnp.concatenate(
        [lax.dynamic_index_in_dim(rows, head_of, 1, keepdims=False) for rows in coarse_rows], axis=1
    )

    bias = jnp.where(coarse_scale[:, None] <= coarse_scale[None, :], 0.0, -1e9).astype(F32)
    packet = call(coarse_packet_kernel, shape(736, 256), flops=2**28, moved=2**22, exps=2**18)(
        query_coarse, key_coarse, value_coarse, bias, grad_coarse.T
    )
    kv, qb, packet = lax.optimization_barrier((kv, qb, packet))

    half = [pltpu.VMEM((PIECES, PIECE, PIECE), BF16)]
    accum, stats = call(
        forward_kernel,
        (shape(QUERY_BLOCKS, HEAD_SIZE, QUERY_BLOCK, dtype=F32), shape(QUERY_BLOCKS, 8, QUERY_BLOCK, dtype=F32)),
        half * 2 + [
            pltpu.VMEM((QUERY_BLOCKS, PIECE, QUERY_BLOCK), BF16),
            pltpu.VMEM((2, STEP * PIECE, QUERY_BLOCK), F32),
        ],
        2,
    )(placed, steps, *kv, onehot, kvc, *qb, query_ids)
    all_stats = swap([stats] * 4, KEY_TILES)
    packets = swap([packet] * 4, "head")
    all_stats, packets = lax.optimization_barrier((all_stats, packets))
    weights, stats = lax.optimization_barrier((weights, stats))
    columns = swap(weights, "head")
    parts = call(
        backward_kernel,
        (shape(4, PIECE, PIECE),) * 4 + (shape(4 * PIECE + 64, PIECE),) * 4,
        half * 3 + [pltpu.VMEM((PIECES, PIECE, PIECE), F32), pltpu.VMEM((64, PIECE), F32)],
        2, 10 * 2048 * 2112 * 64, 2**22, 2048 * 2112,
    )(placed, steps, *kv, onehot, kvc, *qb, query_ids, accum, *all_stats)

    parts, columns = lax.optimization_barrier((parts, columns))
    dkv = swap(parts[4:], QUERY_TILES)
    od = swap(parts[:4], KEY_TILES)
    mixed_coarse, dq_coarse, dk_coarse, dv_coarse = call(
        coarse_kernel,
        (shape(480, 256), shape(256, 256), shape(256, 256, dtype=F32), shape(256, 256, dtype=F32)),
        flops=2**29, moved=2**22, exps=2**19,
    )(query_coarse, key_coarse, value_coarse, bias, *packets, *weights, *columns)
    dkv, dk_coarse = lax.optimization_barrier((dkv, dk_coarse))
    sums = call(
        sums_kernel, (shape(2 * PIECE + 64, PIECE),) * 4, [pltpu.VMEM((4, 2 * PIECE, PIECE), BF16)], 1, moved=2**21
    )(placed, *od, *dkv)
    att_fine, dq_fine, dk_fine, dv_fine, coarse_part = call(
        heads_kernel,
        (shape(256, PIECE),) + (shape(PIECE, 256),) * 3 + (shape(4, 64, PIECE),),
        [pltpu.VMEM((256, PIECE), F32), pltpu.VMEM((4, PIECE, PIECE), BF16)], 1, moved=2**20,
    )(placed, *swap(sums, HEADS))
    coarse_parts = swap([coarse_part] * 4, KEY_TILES)
    attended = swap([att_fine] * 4, "head")
    mixed_fine, dk_coarse, dv_coarse = call(
        last_kernel, (shape(480, PIECE), shape(256, 256), shape(256, 256)), (), 1, flops=2**27, moved=2**20
    )(placed, *attended, *columns, *coarse_parts, dk_coarse, dv_coarse)
    return (
        mixed_fine.T, mixed_coarse.T, dq_fine, dk_fine, dv_fine, dq_coarse, dk_coarse, dv_coarse,
    )


def solution(mesh):
    fine_mesh = Mesh(mesh.devices.reshape(2, 2, 2, 2, 2, 2, 4), SEQ + ("head",))
    in_specs = (
        P(SEQ, "head"), P(SEQ, "head"), P(SEQ, "head"),
        P(None, "head"), P(None, "head"), P(None, "head"),
        P("head", None), P(SEQ, "head"), P(None, "head"), P(), P(),
    )
    out_specs = (
        P(SEQ, "head"), P(None, "head"),
        P(SEQ, "head"), P(SEQ, "head"), P(SEQ, "head"),
        P(None, "head"), P(None, "head"), P(None, "head"),
    )
    return jax.shard_map(
        on_device, mesh=fine_mesh, in_specs=in_specs, out_specs=out_specs, check_vma=False
    )
```

```python
import jax
import jax.numpy as jnp
from jax import lax
from jax.experimental import pallas as pl
from jax.experimental.pallas import tpu as pltpu
from jax.sharding import Mesh
from jax.sharding import PartitionSpec as P

HEAD_SIZE = 64
SCALE = HEAD_SIZE ** (-0.5)
FSCALES = 3
HIDE = -30000.0
PIECE = 128
PIECES = 16
QUERY_BLOCKS = 4
QUERY_BLOCK = 512
STEP = 2
F32 = jnp.float32
BF16 = jnp.bfloat16

SEQ = ("xh", "yh", "yl", "zc", "zb", "za")
HEADS = ("xh", "yh")
QUERY_TILES = ("zc", "zb")
KEY_TILES = ("yl", "za")


def product(left, right):
    return jnp.dot(left, right, preferred_element_type=F32)


def product_nt(left, right):
    return lax.dot_general(left, right, (((1,), (1,)), ((), ())), preferred_element_type=F32)


def product_tn(left, right):
    return lax.dot_general(left, right, (((0,), (0,)), ((), ())), preferred_element_type=F32)


def call(kernel, outs, scratch=(), smem=0, flops=0, moved=0, exps=0):
    def run(*operands):
        return pl.pallas_call(
            kernel,
            out_shape=outs,
            in_specs=[pl.BlockSpec(memory_space=pltpu.SMEM)] * smem
            + [pl.BlockSpec(memory_space=pltpu.VMEM)] * (len(operands) - smem),
            out_specs=jax.tree.map(lambda _: pl.BlockSpec(memory_space=pltpu.VMEM), outs),
            scratch_shapes=list(scratch),
            compiler_params=pltpu.CompilerParams(vmem_limit_bytes=48 * 2**20),
            cost_estimate=pl.CostEstimate(
                flops=flops, bytes_accessed=moved, transcendentals=exps
            ),
        )(*operands)

    return run


def shape(*dims, dtype=BF16):
    return jax.ShapeDtypeStruct(dims, dtype)


def weight_blocks_kernel(place_ref, weight_ref, *refs):
    outs, held = refs[:4], refs[4]
    for part in range(4):
        held[part] = weight_ref[:, part * 480:(part + 1) * 480]
    for partner in range(4):
        outs[partner][...] = held[place_ref[2] ^ partner]


def pack_keys_kernel(place_ref, key_ref, value_ref, *refs):
    outs, held = refs[:4], refs[4]
    for head in range(4):
        both = [head_columns(key_ref, head), head_columns(value_ref, head)]
        held[head] = jnp.concatenate(both, axis=1)
    for partner in range(4):
        outs[partner][...] = held[place_ref[0] ^ partner]


def pack_queries_kernel(query_ref, *refs):
    grads, weights, out_ref = refs[:4], refs[4:8], refs[8]
    back = sum(product(weight[...], grad[...]) for weight, grad in zip(weights, grads)).astype(BF16)
    query = (query_ref[...].astype(F32) * SCALE).T.astype(BF16)
    for head in range(4):
        part = slice(head * HEAD_SIZE, (head + 1) * HEAD_SIZE)
        both = jnp.concatenate([query[part], back[part]], axis=0)
        for other in range(4):
            out_ref[4 * head + other] = both


def own_head_kernel(place_ref, *refs):
    for partner in range(4):
        refs[4][place_ref[0] ^ partner] = refs[partner][...]


def prepare_keys(place_ref, kv_refs, onehot_ref, masked_keys, plain, turned):
    lane = lax.broadcasted_iota(jnp.int32, (PIECE, PIECE), 1)
    for partner, ref in enumerate(kv_refs):
        for source in range(4):
            piece = 4 * source + (place_ref[3] ^ partner)
            both = ref[source]
            masked_keys[piece] = jnp.where(lane < HEAD_SIZE, both, onehot_ref[piece])
            turned[piece] = both.astype(F32).T.astype(BF16)
            if plain is not None:
                plain[piece] = both


def query_pieces(place_ref, qb_ref, block):
    return jnp.concatenate([qb_ref[4 * block + (place_ref[1] ^ part)] for part in range(4)], axis=1)


def query_side(place_ref, qb_ref, ids_ref, block):
    both = query_pieces(place_ref, qb_ref, block)
    ids = jnp.concatenate([ids_ref[4 * block + (place_ref[1] ^ part)] for part in range(4)], axis=1)
    row = lax.broadcasted_iota(jnp.int32, (HEAD_SIZE, QUERY_BLOCK), 0)
    hidden = (row > ids) & (row < FSCALES)
    penalty = jnp.where(hidden, HIDE, 0.0).astype(BF16)
    return both, jnp.concatenate([both[:HEAD_SIZE], penalty], axis=0)


def rows_of(ref, step):
    return ref[pl.ds(STEP * step, STEP)].reshape(STEP * PIECE, PIECE)


def turned_of(ref, step, first):
    return jnp.concatenate(
        [ref[STEP * step + part, first:first + HEAD_SIZE, :] for part in range(STEP)], axis=1
    )


def coarse_side(kvc_ref):
    both = kvc_ref[...]
    lane = lax.broadcasted_iota(jnp.int32, both.shape, 1)
    only_keys = jnp.where(lane < HEAD_SIZE, both, jnp.zeros_like(both))
    return both, only_keys, both.astype(F32).T.astype(BF16)


def forward_kernel(
    place_ref, steps_ref, kv0, kv1, kv2, kv3, onehot_ref, kvc_ref, qb_ref, ids_ref,
    out_ref, stats_ref, masked_keys, turned, queries_held, scores_held,
):
    prepare_keys(place_ref, (kv0, kv1, kv2, kv3), onehot_ref, masked_keys, None, turned)
    _, coarse_keys, coarse_turned = coarse_side(kvc_ref)
    for block in range(QUERY_BLOCKS):
        _, queries = query_side(place_ref, qb_ref, ids_ref, block)
        queries_held[block] = queries
        scores = product(coarse_keys, queries)
        top = jnp.max(scores, axis=0, keepdims=True)
        probs = jnp.exp(scores - top)
        total = jnp.sum(probs, axis=0, keepdims=True)
        out_ref[block] = product(coarse_turned[HEAD_SIZE:], probs.astype(BF16))
        stats_ref[block] = jnp.concatenate([top, total, jnp.zeros((6, QUERY_BLOCK), F32)], axis=0)

    def one_block(block, _):
        queries = queries_held[block]
        last = steps_ref[block] - 1
        scores_held[0] = product(rows_of(masked_keys, 0), queries)

        def one_step(step, carried):
            top, total, accum = carried
            slot = step & 1
            scores = scores_held[slot]
            scores_held[1 - slot] = product(rows_of(masked_keys, jnp.minimum(step + 1, last)), queries)
            new_top = jnp.maximum(top, jnp.max(scores, axis=0, keepdims=True))
            fade = jnp.exp(top - new_top)
            probs = jnp.exp(scores - new_top)
            total = total * fade + jnp.sum(probs, axis=0, keepdims=True)
            accum = accum * fade + product(turned_of(turned, step, HEAD_SIZE), probs.astype(BF16))
            return new_top, total, accum

        start = stats_ref[block]
        top, total, accum = lax.fori_loop(
            0, steps_ref[block], one_step, (start[0:1], start[1:2], out_ref[block])
        )
        back = query_pieces(place_ref, qb_ref, block)[HEAD_SIZE:]
        offset = jnp.sum(back.astype(F32) * accum, axis=0, keepdims=True)
        out_ref[block] = accum
        stats_ref[block] = jnp.concatenate(
            [top, total, offset, jnp.zeros((5, QUERY_BLOCK), F32)], axis=0
        )
        return 0

    lax.fori_loop(0, QUERY_BLOCKS, one_block, 0)


def backward_kernel(
    place_ref, steps_ref, kv0, kv1, kv2, kv3, onehot_ref, kvc_ref, qb_ref, ids_ref, accum_ref, own_ref,
    stats1, stats2, stats3, od0, od1, od2, od3, dkv0, dkv1, dkv2, dkv3,
    masked_keys, plain, turned, key_sums, coarse_sums,
):
    prepare_keys(place_ref, (kv0, kv1, kv2, kv3), onehot_ref, masked_keys, plain, turned)
    coarse_both, coarse_keys, coarse_turned = coarse_side(kvc_ref)
    key_sums[...] = jnp.zeros_like(key_sums)
    coarse_sums[...] = jnp.zeros_like(coarse_sums)

    def one_block(block, _):
        both, queries = query_side(place_ref, qb_ref, ids_ref, block)
        stats = [own_ref[block]]
        for partner, ref in enumerate((stats1, stats2, stats3), 1):
            theirs = ref[block]
            parts = [theirs[:, (part ^ partner) * PIECE:((part ^ partner) + 1) * PIECE] for part in range(4)]
            stats.append(jnp.concatenate(parts, axis=1))
        top = stats[0][0:1]
        for other in stats[1:]:
            top = jnp.maximum(top, other[0:1])
        total = jnp.zeros_like(top)
        offset = jnp.zeros_like(top)
        for other in stats:
            fade = jnp.exp(other[0:1] - top)
            total = total + fade * other[1:2]
            offset = offset + fade * other[2:3]
        offset = offset / total
        log_total = top + jnp.log(total)
        attended = accum_ref[block] * (jnp.exp(own_ref[block][0:1] - top) / total)
        back = jnp.concatenate(
            [jnp.zeros((HEAD_SIZE, QUERY_BLOCK), BF16), both[HEAD_SIZE:]], axis=0
        )
        token_rows = both.astype(F32).T
        lane = lax.broadcasted_iota(jnp.int32, token_rows.shape, 1)
        query_rows = jnp.where(lane < HEAD_SIZE, token_rows, 0.0).astype(BF16)
        back_rows = jnp.where(lane < HEAD_SIZE, 0.0, token_rows).astype(BF16)

        def terms(only_keys, key_value, key_turned):
            probs = jnp.exp(product(only_keys, queries) - log_total)
            grad_probs = product(key_value, back)
            grad_scores = (probs * (grad_probs - offset)).astype(BF16)
            key_side = product(grad_scores, query_rows) + product(probs.astype(BF16), back_rows)
            return product(key_turned, grad_scores), key_side

        query_grad, coarse_term = terms(coarse_keys, coarse_both, coarse_turned[:HEAD_SIZE])
        coarse_sums[...] += coarse_term

        def one_step(step, query_grad):
            query_term, key_side = terms(
                rows_of(masked_keys, step), rows_of(plain, step), turned_of(turned, step, 0)
            )
            key_sums[pl.ds(STEP * step, STEP)] += key_side.reshape(STEP, PIECE, PIECE)
            return query_grad + query_term

        query_grad = lax.fori_loop(0, steps_ref[block], one_step, query_grad)
        both_out = jnp.concatenate([attended, query_grad * SCALE], axis=0).astype(BF16)
        for part, ref in enumerate((od0, od1, od2, od3)):
            ref[block] = both_out[:, part * PIECE:(part + 1) * PIECE]
        return 0

    lax.fori_loop(0, QUERY_BLOCKS, one_block, 0)
    coarse = coarse_sums[...].astype(BF16)
    for partner, ref in enumerate((dkv0, dkv1, dkv2, dkv3)):
        for source in range(4):
            piece = key_sums[4 * source + (place_ref[3] ^ partner)]
            ref[source * PIECE:(source + 1) * PIECE, :] = piece.astype(BF16)
        ref[4 * PIECE:, :] = coarse


def coarse_probs(query, key, bias):
    scores = product_nt(key, query) + bias
    top = jnp.max(scores, axis=0, keepdims=True)
    total = jnp.sum(jnp.exp(scores - top), axis=0, keepdims=True)
    return jnp.exp(scores - (top + jnp.log(total)))


def head_columns(ref, head):
    return ref[:, head * HEAD_SIZE:(head + 1) * HEAD_SIZE]


def coarse_packet_kernel(query_ref, key_ref, value_ref, bias_ref, *refs):
    weights, outs = refs[:4], refs[4:]
    attended = []
    for head in range(4):
        query = (head_columns(query_ref, head).astype(F32) * SCALE).astype(BF16)
        probs = coarse_probs(query, head_columns(key_ref, head), bias_ref[...])
        attended.append(product_tn(head_columns(value_ref, head), probs.astype(BF16)).astype(BF16))
    attended = jnp.concatenate(attended, axis=0)
    for weight, out in zip(weights, outs):
        out[:, :256] = attended
        out[:, 256:] = weight[...]


def coarse_kernel(query_ref, key_ref, value_ref, bias_ref, *refs):
    grads, weights, columns, (mixed_ref, dq_ref, dk_ref, dv_ref) = refs[:4], refs[4:8], refs[8:12], refs[12:]
    back_all = sum(product(weight[...], grad[...]) for weight, grad in zip(weights, grads)).astype(BF16)
    mixed_ref[...] = sum(product_tn(column[:, 256:], column[:, :256]) for column in columns).astype(BF16)
    query_grads, key_grads, value_grads = [], [], []
    for head in range(4):
        part = slice(head * HEAD_SIZE, (head + 1) * HEAD_SIZE)
        query = (query_ref[:, part].astype(F32) * SCALE).astype(BF16)
        key, value, back = key_ref[:, part], value_ref[:, part], back_all[part]
        probs = coarse_probs(query, key, bias_ref[...])
        rounded = probs.astype(BF16)
        attended = columns[0][part, :256]
        offset = jnp.sum(back.astype(F32) * attended.astype(F32), axis=0, keepdims=True)
        grad_scores = (probs * (product(value, back) - offset)).astype(BF16)
        query_grads.append(product_tn(key, grad_scores) * SCALE)
        key_grads.append(product(grad_scores, query))
        value_grads.append(product_nt(rounded, back))
    dq_ref[...] = jnp.concatenate(query_grads, axis=0).T.astype(BF16)
    dk_ref[...] = jnp.concatenate(key_grads, axis=1)
    dv_ref[...] = jnp.concatenate(value_grads, axis=1)


def sums_kernel(place_ref, *refs):
    od, dkv, outs, held = refs[:4], refs[4:8], refs[8:12], refs[12]
    for source in range(4):
        rows = slice(source * PIECE, (source + 1) * PIECE)
        held[source, :PIECE] = sum(part[source].astype(F32) for part in od).astype(BF16)
        held[source, PIECE:] = sum(part[rows, :].astype(F32) for part in dkv).astype(BF16)
    coarse = sum(part[4 * PIECE:, :].astype(F32) for part in dkv).astype(BF16)
    for partner in range(4):
        outs[partner][:2 * PIECE, :] = held[place_ref[0] ^ partner]
        outs[partner][2 * PIECE:, :] = coarse


def heads_kernel(place_ref, *refs):
    parts, (att_ref, dq_ref, dk_ref, dv_ref, coarse_ref, query_held, key_held) = refs[:4], refs[4:]
    for partner, part in enumerate(parts):
        head = place_ref[0] ^ partner
        rows = pl.ds(pl.multiple_of(head * HEAD_SIZE, HEAD_SIZE), HEAD_SIZE)
        att_ref[rows, :] = part[:HEAD_SIZE, :]
        query_held[rows, :] = part[HEAD_SIZE:PIECE, :].astype(F32)
        key_held[head] = part[PIECE:2 * PIECE, :]
        coarse_ref[head] = part[2 * PIECE:, :]
    dq_ref[...] = query_held[...].T.astype(BF16)
    dk_ref[...] = jnp.concatenate([key_held[head, :, :HEAD_SIZE] for head in range(4)], axis=1)
    dv_ref[...] = jnp.concatenate([key_held[head, :, HEAD_SIZE:] for head in range(4)], axis=1)


def last_kernel(place_ref, *refs):
    attended, columns, received = refs[:4], refs[4:8], refs[8:12]
    dk_ref, dv_ref, mixed_ref, dk_out, dv_out = refs[12:]
    mixed_ref[...] = sum(
        product_tn(column[:, 256:], att[...]) for column, att in zip(columns, attended)
    ).astype(BF16)
    for partner, ref in enumerate(received):
        rows = pl.ds(pl.multiple_of((place_ref[1] ^ partner) * 64, 64), 64)
        parts = [ref[head].astype(F32) for head in range(4)]
        keys = jnp.concatenate([part[:, :HEAD_SIZE] for part in parts], axis=1)
        values = jnp.concatenate([part[:, HEAD_SIZE:] for part in parts], axis=1)
        dk_out[rows, :] = (dk_ref[rows, :] + keys).astype(BF16)
        dv_out[rows, :] = (dv_ref[rows, :] + values).astype(BF16)


def swap(arrays, axes):
    out = [arrays[0]]
    for partner in (1, 2, 3):
        out.append(lax.ppermute(arrays[partner], axes, [(i, i ^ partner) for i in range(4)]))
    return out


def on_device(
    query_fine, key_fine, value_fine, query_coarse, key_coarse, value_coarse,
    out_weight, grad_fine, grad_coarse, fine_scale, coarse_scale,
):
    place = {name: lax.axis_index(name) for name in SEQ}
    head_of = place["xh"] * 2 + place["yh"]
    tile_of = place["yl"] * 2 + place["za"]
    placed = jnp.stack(
        [head_of, tile_of, lax.axis_index("head"), place["zc"] * 2 + place["zb"]]
    ).astype(jnp.int32)

    grads = swap([grad_fine.T] * 4, "head")
    swapped = (shape(PIECE, PIECE),) * 4
    packing = [pltpu.VMEM((4, PIECE, PIECE), BF16)]

    def own_head(pieces):
        return call(own_head_kernel, shape(4, PIECE, PIECE), (), 1, moved=2**18)(placed, *swap(pieces, HEADS))

    own_kv = own_head(
        call(pack_keys_kernel, swapped, packing, 1, moved=2**18)(placed, key_fine, value_fine)
    )
    kv = swap([own_kv] * 4, QUERY_TILES)
    weights = call(
        weight_blocks_kernel, (shape(256, 480),) * 4, [pltpu.VMEM((4, 256, 480), BF16)], 1, moved=2**21
    )(placed, out_weight)
    packed_q = call(pack_queries_kernel, shape(PIECES, PIECE, PIECE), flops=2 * 128 * 256 * 1920, moved=2**21)(
        query_fine, *grads, *weights
    )

    ids = fine_scale.reshape(2, 2, 2, 2, 2, 2, PIECE)
    query_ids = lax.dynamic_index_in_dim(ids, place["zc"], 3, keepdims=False)
    query_ids = lax.dynamic_index_in_dim(query_ids, place["zb"], 3, keepdims=False)
    query_ids = query_ids.reshape(PIECES, 1, PIECE)
    key_ids = lax.dynamic_index_in_dim(ids, place["yl"], 2, keepdims=False)
    key_ids = lax.dynamic_index_in_dim(key_ids, place["za"], 4, keepdims=False)
    key_ids = key_ids.reshape(PIECES, PIECE)
    lane = lax.broadcasted_iota(jnp.int32, (PIECES, PIECE, PIECE), 2)
    onehot = (lane - HEAD_SIZE == key_ids[:, :, None]).astype(BF16)
    seen = jnp.sum(key_ids[None, :, 0] <= query_ids[3::4, 0, -1:], axis=1)
    steps = ((seen + STEP - 1) // STEP).astype(jnp.int32)

    coarse_rows = [
        lax.dynamic_slice(array, (tile_of * 64, 0), (64, 256)).reshape(64, 4, HEAD_SIZE)
        for array in (key_coarse, value_coarse)
    ]
    kvc = jnp.concatenate(
        [lax.dynamic_index_in_dim(rows, head_of, 1, keepdims=False) for rows in coarse_rows], axis=1
    )

    bias = jnp.where(coarse_scale[:, None] <= coarse_scale[None, :], 0.0, -1e9).astype(F32)
    columns = call(coarse_packet_kernel, (shape(256, 736),) * 4, flops=2**28, moved=2**22, exps=2**18)(
        query_coarse, key_coarse, value_coarse, bias, *weights
    )
    packed_q, columns, onehot, kvc, steps, query_ids = lax.optimization_barrier(
        (packed_q, columns, onehot, kvc, steps, query_ids)
    )
    qb = lax.all_to_all(packed_q, HEADS + KEY_TILES, 0, 0, tiled=True)
    kv, qb, coarse_grad = lax.optimization_barrier((kv, qb, grad_coarse.T))

    half = [pltpu.VMEM((PIECES, PIECE, PIECE), BF16)]
    accum, stats = call(
        forward_kernel,
        (shape(QUERY_BLOCKS, HEAD_SIZE, QUERY_BLOCK, dtype=F32), shape(QUERY_BLOCKS, 8, QUERY_BLOCK, dtype=F32)),
        half * 2 + [
            pltpu.VMEM((QUERY_BLOCKS, PIECE, QUERY_BLOCK), BF16),
            pltpu.VMEM((2, STEP * PIECE, QUERY_BLOCK), F32),
        ],
        2,
    )(placed, steps, *kv, onehot, kvc, qb, query_ids)
    coarse_grads = swap([coarse_grad] * 4, "head")
    stats, coarse_grads, columns = lax.optimization_barrier((stats, coarse_grads, columns))
    all_stats = swap([stats] * 4, KEY_TILES)
    all_stats, columns = lax.optimization_barrier((all_stats, columns))
    columns = swap(columns, "head")
    parts = call(
        backward_kernel,
        (shape(4, PIECE, PIECE),) * 4 + (shape(4 * PIECE + 64, PIECE),) * 4,
        half * 3 + [pltpu.VMEM((PIECES, PIECE, PIECE), F32), pltpu.VMEM((64, PIECE), F32)],
        2, 10 * 2048 * 2112 * 64, 2**22, 2048 * 2112,
    )(placed, steps, *kv, onehot, kvc, qb, query_ids, accum, *all_stats)

    parts, columns = lax.optimization_barrier((parts, columns))
    dkv = swap(parts[4:], QUERY_TILES)
    od = swap(parts[:4], KEY_TILES)
    mixed_coarse, dq_coarse, dk_coarse, dv_coarse = call(
        coarse_kernel,
        (shape(480, 256), shape(256, 256), shape(256, 256, dtype=F32), shape(256, 256, dtype=F32)),
        flops=2**29, moved=2**22, exps=2**19,
    )(query_coarse, key_coarse, value_coarse, bias, *coarse_grads, *weights, *columns)
    dkv, dk_coarse = lax.optimization_barrier((dkv, dk_coarse))
    sums = call(
        sums_kernel, (shape(2 * PIECE + 64, PIECE),) * 4, [pltpu.VMEM((4, 2 * PIECE, PIECE), BF16)], 1, moved=2**21
    )(placed, *od, *dkv)
    att_fine, dq_fine, dk_fine, dv_fine, coarse_part = call(
        heads_kernel,
        (shape(256, PIECE),) + (shape(PIECE, 256),) * 3 + (shape(4, 64, PIECE),),
        [pltpu.VMEM((256, PIECE), F32), pltpu.VMEM((4, PIECE, PIECE), BF16)], 1, moved=2**20,
    )(placed, *swap(sums, HEADS))
    coarse_parts = swap([coarse_part] * 4, KEY_TILES)
    attended = swap([att_fine] * 4, "head")
    mixed_fine, dk_coarse, dv_coarse = call(
        last_kernel, (shape(480, PIECE), shape(256, 256), shape(256, 256)), (), 1, flops=2**27, moved=2**20
    )(placed, *attended, *columns, *coarse_parts, dk_coarse, dv_coarse)
    return (
        mixed_fine.T, mixed_coarse.T, dq_fine, dk_fine, dv_fine, dq_coarse, dk_coarse, dv_coarse,
    )


def solution(mesh):
    fine_mesh = Mesh(mesh.devices.reshape(2, 2, 2, 2, 2, 2, 4), SEQ + ("head",))
    in_specs = (
        P(SEQ, "head"), P(SEQ, "head"), P(SEQ, "head"),
        P(None, "head"), P(None, "head"), P(None, "head"),
        P("head", None), P(SEQ, "head"), P(None, "head"), P(), P(),
    )
    out_specs = (
        P(SEQ, "head"), P(None, "head"),
        P(SEQ, "head"), P(SEQ, "head"), P(SEQ, "head"),
        P(None, "head"), P(None, "head"), P(None, "head"),
    )
    return jax.shard_map(
        on_device, mesh=fine_mesh, in_specs=in_specs, out_specs=out_specs, check_vma=False
    )
```

```python
import jax
import jax.numpy as jnp
from jax import lax
from jax.experimental import pallas as pl
from jax.experimental.pallas import tpu as pltpu
from jax.sharding import Mesh
from jax.sharding import PartitionSpec as P

HEAD_SIZE = 64
SCALE = HEAD_SIZE ** (-0.5)
FSCALES = 3
HIDE = -30000.0
PIECE = 128
PIECES = 16
QUERY_BLOCKS = 4
QUERY_BLOCK = 512
STEP = 2
F32 = jnp.float32
BF16 = jnp.bfloat16

SEQ = ("xh", "yh", "yl", "zc", "zb", "za")
HEADS = ("xh", "za")
QUERY_TILES = ("zc", "zb")
KEY_TILES = ("yh", "yl")


def product(left, right):
    return jnp.dot(left, right, preferred_element_type=F32)


def product_nt(left, right):
    return lax.dot_general(left, right, (((1,), (1,)), ((), ())), preferred_element_type=F32)


def product_tn(left, right):
    return lax.dot_general(left, right, (((0,), (0,)), ((), ())), preferred_element_type=F32)


def call(kernel, outs, scratch=(), smem=0, flops=0, moved=0, exps=0):
    def run(*operands):
        return pl.pallas_call(
            kernel,
            out_shape=outs,
            in_specs=[pl.BlockSpec(memory_space=pltpu.SMEM)] * smem
            + [pl.BlockSpec(memory_space=pltpu.VMEM)] * (len(operands) - smem),
            out_specs=jax.tree.map(lambda _: pl.BlockSpec(memory_space=pltpu.VMEM), outs),
            scratch_shapes=list(scratch),
            compiler_params=pltpu.CompilerParams(vmem_limit_bytes=48 * 2**20),
            cost_estimate=pl.CostEstimate(
                flops=flops, bytes_accessed=moved, transcendentals=exps
            ),
        )(*operands)

    return run


def shape(*dims, dtype=BF16):
    return jax.ShapeDtypeStruct(dims, dtype)


def weight_blocks_kernel(place_ref, weight_ref, *refs):
    outs, held = refs[:4], refs[4]
    for part in range(4):
        held[part] = weight_ref[:, part * 480:(part + 1) * 480]
    for partner in range(4):
        outs[partner][...] = held[place_ref[2] ^ partner]


def pack_kernel(place_ref, query_ref, key_ref, value_ref, *refs):
    grads, weights, outs, held = refs[:4], refs[4:8], refs[8:12], refs[12]
    back = sum(product(weight[...], grad[...]) for weight, grad in zip(weights, grads)).astype(BF16)
    query = (query_ref[...].astype(F32) * SCALE).T.astype(BF16)
    for head in range(4):
        part = slice(head * HEAD_SIZE, (head + 1) * HEAD_SIZE)
        held[head, :HEAD_SIZE] = query[part]
        held[head, HEAD_SIZE:PIECE] = back[part]
        held[head, PIECE:] = jnp.concatenate([key_ref[:, part], value_ref[:, part]], axis=1)
    for partner in range(4):
        outs[partner][...] = held[place_ref[0] ^ partner]


def own_head_kernel(place_ref, *refs):
    parts, (qb_ref, kv_ref) = refs[:4], refs[4:]
    for partner, part in enumerate(parts):
        source = place_ref[0] ^ partner
        qb_ref[source] = part[:PIECE, :]
        kv_ref[source] = part[PIECE:, :]


def key_piece(place_ref, source, partner):
    return 8 * (source // 2) + 2 * (place_ref[3] ^ partner) + source % 2


def prepare_queries(qb_refs, held):
    for part, ref in enumerate(qb_refs):
        for source in range(4):
            held[8 * (source // 2) + 2 * part + source % 2] = ref[source]


def prepare_keys(place_ref, kv_refs, onehot_ref, masked_keys, plain, turned):
    lane = lax.broadcasted_iota(jnp.int32, (PIECE, PIECE), 1)
    for partner, ref in enumerate(kv_refs):
        for source in range(4):
            piece = key_piece(place_ref, source, partner)
            both = ref[source]
            masked_keys[piece] = jnp.where(lane < HEAD_SIZE, both, onehot_ref[piece])
            turned[piece] = both.astype(F32).T.astype(BF16)
            if plain is not None:
                plain[piece] = both


def query_pieces(held, block):
    return jnp.concatenate([held[4 * block + part] for part in range(4)], axis=1)


def query_side(place_ref, held, ids_ref, block):
    both = query_pieces(held, block)
    own = 8 * (block // 2) if isinstance(block, int) else 8 * (block >> 1)
    first = own + 4 * ((place_ref[1] >> 1) ^ (block & 1))
    ids = jnp.concatenate(
        [ids_ref[first + 2 * ((place_ref[1] & 1) ^ (part // 2)) + part % 2] for part in range(4)], axis=1
    )
    row = lax.broadcasted_iota(jnp.int32, (HEAD_SIZE, QUERY_BLOCK), 0)
    hidden = (row > ids) & (row < FSCALES)
    penalty = jnp.where(hidden, HIDE, 0.0).astype(BF16)
    return both, jnp.concatenate([both[:HEAD_SIZE], penalty], axis=0)


def rows_of(ref, step):
    return ref[pl.ds(STEP * step, STEP)].reshape(STEP * PIECE, PIECE)


def turned_of(ref, step, first):
    return jnp.concatenate(
        [ref[STEP * step + part, first:first + HEAD_SIZE, :] for part in range(STEP)], axis=1
    )


def coarse_side(kvc_ref):
    both = kvc_ref[...]
    lane = lax.broadcasted_iota(jnp.int32, both.shape, 1)
    only_keys = jnp.where(lane < HEAD_SIZE, both, jnp.zeros_like(both))
    return both, only_keys, both.astype(F32).T.astype(BF16)


def forward_kernel(
    place_ref, steps_ref, kv0, kv1, kv2, kv3, onehot_ref, kvc_ref, qb0, qb1, qb2, qb3, ids_ref,
    out_ref, stats_ref, masked_keys, turned, query_held, queries_held, scores_held,
):
    prepare_keys(place_ref, (kv0, kv1, kv2, kv3), onehot_ref, masked_keys, None, turned)
    prepare_queries((qb0, qb1, qb2, qb3), query_held)
    _, coarse_keys, coarse_turned = coarse_side(kvc_ref)
    for block in range(QUERY_BLOCKS):
        _, queries = query_side(place_ref, query_held, ids_ref, block)
        queries_held[block] = queries
        scores = product(coarse_keys, queries)
        top = jnp.max(scores, axis=0, keepdims=True)
        probs = jnp.exp(scores - top)
        total = jnp.sum(probs, axis=0, keepdims=True)
        out_ref[block] = product(coarse_turned[HEAD_SIZE:], probs.astype(BF16))
        stats_ref[block] = jnp.concatenate([top, total, jnp.zeros((6, QUERY_BLOCK), F32)], axis=0)

    def one_block(block, _):
        queries = queries_held[block]
        last = steps_ref[block] - 1
        scores_held[0] = product(rows_of(masked_keys, 0), queries)

        def one_step(step, carried):
            top, total, accum = carried
            slot = step & 1
            scores = scores_held[slot]
            scores_held[1 - slot] = product(rows_of(masked_keys, jnp.minimum(step + 1, last)), queries)
            new_top = jnp.maximum(top, jnp.max(scores, axis=0, keepdims=True))
            fade = jnp.exp(top - new_top)
            probs = jnp.exp(scores - new_top)
            total = total * fade + jnp.sum(probs, axis=0, keepdims=True)
            accum = accum * fade + product(turned_of(turned, step, HEAD_SIZE), probs.astype(BF16))
            return new_top, total, accum

        start = stats_ref[block]
        top, total, accum = lax.fori_loop(
            0, steps_ref[block], one_step, (start[0:1], start[1:2], out_ref[block])
        )
        back = query_pieces(query_held, block)[HEAD_SIZE:]
        offset = jnp.sum(back.astype(F32) * accum, axis=0, keepdims=True)
        out_ref[block] = accum
        stats_ref[block] = jnp.concatenate(
            [top, total, offset, jnp.zeros((5, QUERY_BLOCK), F32)], axis=0
        )
        return 0

    lax.fori_loop(0, QUERY_BLOCKS, one_block, 0)


def backward_kernel(
    place_ref, steps_ref, kv0, kv1, kv2, kv3, onehot_ref, kvc_ref, qb0, qb1, qb2, qb3, ids_ref, accum_ref, own_ref,
    stats1, stats2, stats3, od0, od1, od2, od3, dkv0, dkv1, dkv2, dkv3,
    masked_keys, plain, turned, query_held, out_held, key_sums, coarse_sums,
):
    prepare_keys(place_ref, (kv0, kv1, kv2, kv3), onehot_ref, masked_keys, plain, turned)
    prepare_queries((qb0, qb1, qb2, qb3), query_held)
    coarse_both, coarse_keys, coarse_turned = coarse_side(kvc_ref)
    key_sums[...] = jnp.zeros_like(key_sums)
    coarse_sums[...] = jnp.zeros_like(coarse_sums)

    def one_block(block, _):
        both, queries = query_side(place_ref, query_held, ids_ref, block)
        stats = [own_ref[block]]
        for partner, ref in enumerate((stats1, stats2, stats3), 1):
            theirs = ref[block ^ (partner // 2)]
            flip = 2 * (partner % 2)
            parts = [theirs[:, (part ^ flip) * PIECE:((part ^ flip) + 1) * PIECE] for part in range(4)]
            stats.append(jnp.concatenate(parts, axis=1))
        top = stats[0][0:1]
        for other in stats[1:]:
            top = jnp.maximum(top, other[0:1])
        total = jnp.zeros_like(top)
        offset = jnp.zeros_like(top)
        for other in stats:
            fade = jnp.exp(other[0:1] - top)
            total = total + fade * other[1:2]
            offset = offset + fade * other[2:3]
        offset = offset / total
        log_total = top + jnp.log(total)
        attended = accum_ref[block] * (jnp.exp(own_ref[block][0:1] - top) / total)
        back = jnp.concatenate(
            [jnp.zeros((HEAD_SIZE, QUERY_BLOCK), BF16), both[HEAD_SIZE:]], axis=0
        )
        token_rows = both.astype(F32).T
        lane = lax.broadcasted_iota(jnp.int32, token_rows.shape, 1)
        query_rows = jnp.where(lane < HEAD_SIZE, token_rows, 0.0).astype(BF16)
        back_rows = jnp.where(lane < HEAD_SIZE, 0.0, token_rows).astype(BF16)

        def terms(only_keys, key_value, key_turned):
            probs = jnp.exp(product(only_keys, queries) - log_total)
            grad_probs = product(key_value, back)
            grad_scores = (probs * (grad_probs - offset)).astype(BF16)
            key_side = product(grad_scores, query_rows) + product(probs.astype(BF16), back_rows)
            return product(key_turned, grad_scores), key_side

        query_grad, coarse_term = terms(coarse_keys, coarse_both, coarse_turned[:HEAD_SIZE])
        coarse_sums[...] += coarse_term

        def one_step(step, query_grad):
            query_term, key_side = terms(
                rows_of(masked_keys, step), rows_of(plain, step), turned_of(turned, step, 0)
            )
            key_sums[pl.ds(STEP * step, STEP)] += key_side.reshape(STEP, PIECE, PIECE)
            return query_grad + query_term

        query_grad = lax.fori_loop(0, steps_ref[block], one_step, query_grad)
        both_out = jnp.concatenate([attended, query_grad * SCALE], axis=0).astype(BF16)
        for part in range(4):
            out_held[4 * block + part] = both_out[:, part * PIECE:(part + 1) * PIECE]
        return 0

    lax.fori_loop(0, QUERY_BLOCKS, one_block, 0)
    for part, ref in enumerate((od0, od1, od2, od3)):
        for source in range(4):
            ref[source] = out_held[8 * (source // 2) + 2 * part + source % 2]
    coarse = coarse_sums[...].astype(BF16)
    for partner, ref in enumerate((dkv0, dkv1, dkv2, dkv3)):
        for source in range(4):
            piece = key_sums[key_piece(place_ref, source, partner)]
            ref[source * PIECE:(source + 1) * PIECE, :] = piece.astype(BF16)
        ref[4 * PIECE:, :] = coarse


def coarse_probs(query, key, bias):
    scores = product_nt(key, query) + bias
    top = jnp.max(scores, axis=0, keepdims=True)
    total = jnp.sum(jnp.exp(scores - top), axis=0, keepdims=True)
    return jnp.exp(scores - (top + jnp.log(total)))


def head_columns(ref, head):
    return ref[:, head * HEAD_SIZE:(head + 1) * HEAD_SIZE]


def coarse_packet_kernel(query_ref, key_ref, value_ref, bias_ref, grad_ref, out_ref):
    out_ref[:480, :] = grad_ref[...]
    for head in range(4):
        query = (head_columns(query_ref, head).astype(F32) * SCALE).astype(BF16)
        probs = coarse_probs(query, head_columns(key_ref, head), bias_ref[...])
        attended = product_tn(head_columns(value_ref, head), probs.astype(BF16))
        out_ref[480 + head * HEAD_SIZE:480 + (head + 1) * HEAD_SIZE, :] = attended.astype(BF16)


def coarse_kernel(query_ref, key_ref, value_ref, bias_ref, *refs):
    packets, weights, columns, (mixed_ref, dq_ref, dk_ref, dv_ref) = refs[:4], refs[4:8], refs[8:12], refs[12:]
    back_all = sum(
        product(weight[...], packet[:480, :]) for weight, packet in zip(weights, packets)
    ).astype(BF16)
    mixed_ref[...] = sum(
        product_tn(column[...], packet[480:, :]) for column, packet in zip(columns, packets)
    ).astype(BF16)
    query_grads, key_grads, value_grads = [], [], []
    for head in range(4):
        part = slice(head * HEAD_SIZE, (head + 1) * HEAD_SIZE)
        query = (query_ref[:, part].astype(F32) * SCALE).astype(BF16)
        key, value, back = key_ref[:, part], value_ref[:, part], back_all[part]
        probs = coarse_probs(query, key, bias_ref[...])
        rounded = probs.astype(BF16)
        attended = packets[0][480 + part.start:480 + part.stop, :]
        offset = jnp.sum(back.astype(F32) * attended.astype(F32), axis=0, keepdims=True)
        grad_scores = (probs * (product(value, back) - offset)).astype(BF16)
        query_grads.append(product_tn(key, grad_scores) * SCALE)
        key_grads.append(product(grad_scores, query))
        value_grads.append(product_nt(rounded, back))
    dq_ref[...] = jnp.concatenate(query_grads, axis=0).T.astype(BF16)
    dk_ref[...] = jnp.concatenate(key_grads, axis=1)
    dv_ref[...] = jnp.concatenate(value_grads, axis=1)


def sums_kernel(place_ref, *refs):
    od, dkv, outs, held = refs[:4], refs[4:8], refs[8:12], refs[12]
    for source in range(4):
        rows = slice(source * PIECE, (source + 1) * PIECE)
        held[source, :PIECE] = sum(part[source].astype(F32) for part in od).astype(BF16)
        held[source, PIECE:] = sum(part[rows, :].astype(F32) for part in dkv).astype(BF16)
    coarse = sum(part[4 * PIECE:, :].astype(F32) for part in dkv).astype(BF16)
    for partner in range(4):
        outs[partner][:2 * PIECE, :] = held[place_ref[0] ^ partner]
        outs[partner][2 * PIECE:, :] = coarse


def heads_kernel(place_ref, *refs):
    parts, (att_ref, dq_ref, dk_ref, dv_ref, coarse_ref, query_held, key_held) = refs[:4], refs[4:]
    for partner, part in enumerate(parts):
        head = place_ref[0] ^ partner
        rows = pl.ds(pl.multiple_of(head * HEAD_SIZE, HEAD_SIZE), HEAD_SIZE)
        att_ref[rows, :] = part[:HEAD_SIZE, :]
        query_held[rows, :] = part[HEAD_SIZE:PIECE, :].astype(F32)
        key_held[head] = part[PIECE:2 * PIECE, :]
        coarse_ref[head] = part[2 * PIECE:, :]
    dq_ref[...] = query_held[...].T.astype(BF16)
    dk_ref[...] = jnp.concatenate([key_held[head, :, :HEAD_SIZE] for head in range(4)], axis=1)
    dv_ref[...] = jnp.concatenate([key_held[head, :, HEAD_SIZE:] for head in range(4)], axis=1)


def last_kernel(place_ref, *refs):
    attended, columns, received = refs[:4], refs[4:8], refs[8:12]
    dk_ref, dv_ref, mixed_ref, dk_out, dv_out = refs[12:]
    mixed_ref[...] = sum(
        product_tn(column[...], att[...]) for column, att in zip(columns, attended)
    ).astype(BF16)
    for partner, ref in enumerate(received):
        rows = pl.ds(pl.multiple_of((place_ref[1] ^ partner) * 64, 64), 64)
        parts = [ref[head].astype(F32) for head in range(4)]
        keys = jnp.concatenate([part[:, :HEAD_SIZE] for part in parts], axis=1)
        values = jnp.concatenate([part[:, HEAD_SIZE:] for part in parts], axis=1)
        dk_out[rows, :] = (dk_ref[rows, :] + keys).astype(BF16)
        dv_out[rows, :] = (dv_ref[rows, :] + values).astype(BF16)


def swap(arrays, axes):
    out = [arrays[0]]
    for partner in (1, 2, 3):
        out.append(lax.ppermute(arrays[partner], axes, [(i, i ^ partner) for i in range(4)]))
    return out


def on_device(
    query_fine, key_fine, value_fine, query_coarse, key_coarse, value_coarse,
    out_weight, grad_fine, grad_coarse, fine_scale, coarse_scale,
):
    place = {name: lax.axis_index(name) for name in SEQ}
    head_of = place["xh"] * 2 + place["za"]
    tile_of = place["yh"] * 2 + place["yl"]
    placed = jnp.stack(
        [head_of, tile_of, lax.axis_index("head"), place["zc"] * 2 + place["zb"]]
    ).astype(jnp.int32)

    grads = swap([grad_fine.T] * 4, "head")
    weights = call(
        weight_blocks_kernel, (shape(256, 480),) * 4, [pltpu.VMEM((4, 256, 480), BF16)], 1, moved=2**21
    )(placed, out_weight)
    packed = call(
        pack_kernel, (shape(2 * PIECE, PIECE),) * 4, [pltpu.VMEM((4, 2 * PIECE, PIECE), BF16)], 1,
        flops=2 * 128 * 256 * 1920, moved=2**21,
    )(placed, query_fine, key_fine, value_fine, *grads, *weights)
    own_qb, own_kv = call(own_head_kernel, (shape(4, PIECE, PIECE),) * 2, (), 1, moved=2**19)(
        placed, *swap(packed, HEADS)
    )
    kv = swap([own_kv] * 4, QUERY_TILES)
    qb = swap([own_qb] * 4, KEY_TILES)

    ids = fine_scale.reshape(2, 2, 2, 2, 2, 2, PIECE)
    query_ids = lax.dynamic_index_in_dim(ids, place["zc"], 3, keepdims=False)
    query_ids = lax.dynamic_index_in_dim(query_ids, place["zb"], 3, keepdims=False)
    query_ids = query_ids.reshape(PIECES, 1, PIECE)
    key_ids = lax.dynamic_index_in_dim(ids, place["yh"], 1, keepdims=False)
    key_ids = lax.dynamic_index_in_dim(key_ids, place["yl"], 1, keepdims=False)
    key_ids = key_ids.reshape(PIECES, PIECE)
    lane = lax.broadcasted_iota(jnp.int32, (PIECES, PIECE, PIECE), 2)
    onehot = (lane - HEAD_SIZE == key_ids[:, :, None]).astype(BF16)
    seen = jnp.sum(key_ids[None, :, 0] <= query_ids[3::4, 0, -1:], axis=1)
    steps = ((seen + STEP - 1) // STEP).astype(jnp.int32).reshape(2, 2)
    steps = jnp.where(place["yh"] == 0, steps, steps[:, ::-1]).reshape(4)

    coarse_rows = [
        lax.dynamic_slice(array, (tile_of * 64, 0), (64, 256)).reshape(64, 4, HEAD_SIZE)
        for array in (key_coarse, value_coarse)
    ]
    kvc = jnp.concatenate(
        [lax.dynamic_index_in_dim(rows, head_of, 1, keepdims=False) for rows in coarse_rows], axis=1
    )

    bias = jnp.where(coarse_scale[:, None] <= coarse_scale[None, :], 0.0, -1e9).astype(F32)
    packet = call(coarse_packet_kernel, shape(736, 256), flops=2**28, moved=2**22, exps=2**18)(
        query_coarse, key_coarse, value_coarse, bias, grad_coarse.T
    )
    kv, qb, packet = lax.optimization_barrier((kv, qb, packet))

    half = [pltpu.VMEM((PIECES, PIECE, PIECE), BF16)]
    accum, stats = call(
        forward_kernel,
        (shape(QUERY_BLOCKS, HEAD_SIZE, QUERY_BLOCK, dtype=F32), shape(QUERY_BLOCKS, 8, QUERY_BLOCK, dtype=F32)),
        half * 3 + [
            pltpu.VMEM((QUERY_BLOCKS, PIECE, QUERY_BLOCK), BF16),
            pltpu.VMEM((2, STEP * PIECE, QUERY_BLOCK), F32),
        ],
        2,
    )(placed, steps, *kv, onehot, kvc, *qb, query_ids)
    packets = swap([packet] * 4, "head")
    stats, packets[1] = lax.optimization_barrier((stats, packets[1]))
    all_stats = swap([stats] * 4, KEY_TILES)
    all_stats, weights = lax.optimization_barrier((all_stats, weights))
    all_stats, packets = lax.optimization_barrier((all_stats, packets))
    columns = swap(weights, "head")
    parts = call(
        backward_kernel,
        (shape(4, PIECE, PIECE),) * 4 + (shape(4 * PIECE + 64, PIECE),) * 4,
        half * 5 + [pltpu.VMEM((PIECES, PIECE, PIECE), F32), pltpu.VMEM((64, PIECE), F32)],
        2, 10 * 2048 * 2112 * 64, 2**22, 2048 * 2112,
    )(placed, steps, *kv, onehot, kvc, *qb, query_ids, accum, *all_stats)

    parts, columns = lax.optimization_barrier((parts, columns))
    dkv = swap(parts[4:], QUERY_TILES)
    od = swap(parts[:4], KEY_TILES)
    mixed_coarse, dq_coarse, dk_coarse, dv_coarse = call(
        coarse_kernel,
        (shape(480, 256), shape(256, 256), shape(256, 256, dtype=F32), shape(256, 256, dtype=F32)),
        flops=2**29, moved=2**22, exps=2**19,
    )(query_coarse, key_coarse, value_coarse, bias, *packets, *weights, *columns)
    dkv, dk_coarse = lax.optimization_barrier((dkv, dk_coarse))
    sums = call(
        sums_kernel, (shape(2 * PIECE + 64, PIECE),) * 4, [pltpu.VMEM((4, 2 * PIECE, PIECE), BF16)], 1, moved=2**21
    )(placed, *od, *dkv)
    att_fine, dq_fine, dk_fine, dv_fine, coarse_part = call(
        heads_kernel,
        (shape(256, PIECE),) + (shape(PIECE, 256),) * 3 + (shape(4, 64, PIECE),),
        [pltpu.VMEM((256, PIECE), F32), pltpu.VMEM((4, PIECE, PIECE), BF16)], 1, moved=2**20,
    )(placed, *swap(sums, HEADS))
    coarse_parts = swap([coarse_part] * 4, KEY_TILES)
    attended = swap([att_fine] * 4, "head")
    mixed_fine, dk_coarse, dv_coarse = call(
        last_kernel, (shape(480, PIECE), shape(256, 256), shape(256, 256)), (), 1, flops=2**27, moved=2**20
    )(placed, *attended, *columns, *coarse_parts, dk_coarse, dv_coarse)
    return (
        mixed_fine.T, mixed_coarse.T, dq_fine, dk_fine, dv_fine, dq_coarse, dk_coarse, dv_coarse,
    )


def solution(mesh):
    fine_mesh = Mesh(mesh.devices.reshape(2, 2, 2, 2, 2, 2, 4), SEQ + ("head",))
    in_specs = (
        P(SEQ, "head"), P(SEQ, "head"), P(SEQ, "head"),
        P(None, "head"), P(None, "head"), P(None, "head"),
        P("head", None), P(SEQ, "head"), P(None, "head"), P(), P(),
    )
    out_specs = (
        P(SEQ, "head"), P(None, "head"),
        P(SEQ, "head"), P(SEQ, "head"), P(SEQ, "head"),
        P(None, "head"), P(None, "head"), P(None, "head"),
    )
    return jax.shard_map(
        on_device, mesh=fine_mesh, in_specs=in_specs, out_specs=out_specs, check_vma=False
    )
```

```python
import jax
import jax.numpy as jnp
from jax import lax
from jax.experimental import pallas as pl
from jax.experimental.pallas import tpu as pltpu
from jax.sharding import Mesh
from jax.sharding import PartitionSpec as P

HEAD_SIZE = 64
SCALE = HEAD_SIZE ** (-0.5)
FSCALES = 3
HIDE = -30000.0
PIECE = 128
PIECES = 16
QUERY_BLOCKS = 4
QUERY_BLOCK = 512
STEP = 2
F32 = jnp.float32
BF16 = jnp.bfloat16

SEQ = ("xh", "yh", "yl", "zc", "zb", "za")
HEADS = ("xh", "za")
QUERY_TILES = ("zc", "zb")
KEY_TILES = ("yh", "yl")


def product(left, right):
    return jnp.dot(left, right, preferred_element_type=F32)


def product_nt(left, right):
    return lax.dot_general(left, right, (((1,), (1,)), ((), ())), preferred_element_type=F32)


def product_tn(left, right):
    return lax.dot_general(left, right, (((0,), (0,)), ((), ())), preferred_element_type=F32)


def call(kernel, outs, scratch=(), smem=0, flops=0, moved=0, exps=0):
    def run(*operands):
        return pl.pallas_call(
            kernel,
            out_shape=outs,
            in_specs=[pl.BlockSpec(memory_space=pltpu.SMEM)] * smem
            + [pl.BlockSpec(memory_space=pltpu.VMEM)] * (len(operands) - smem),
            out_specs=jax.tree.map(lambda _: pl.BlockSpec(memory_space=pltpu.VMEM), outs),
            scratch_shapes=list(scratch),
            compiler_params=pltpu.CompilerParams(vmem_limit_bytes=48 * 2**20),
            cost_estimate=pl.CostEstimate(
                flops=flops, bytes_accessed=moved, transcendentals=exps
            ),
        )(*operands)

    return run


def shape(*dims, dtype=BF16):
    return jax.ShapeDtypeStruct(dims, dtype)


def weight_blocks_kernel(place_ref, weight_ref, *refs):
    outs, held = refs[:4], refs[4]
    for part in range(4):
        held[part] = weight_ref[:, part * 480:(part + 1) * 480]
    for partner in range(4):
        outs[partner][...] = held[place_ref[2] ^ partner]


def pack_kernel(place_ref, query_ref, key_ref, value_ref, *refs):
    grads, weights, outs, held = refs[:4], refs[4:8], refs[8:12], refs[12]
    back = sum(product(weight[...], grad[...]) for weight, grad in zip(weights, grads)).astype(BF16)
    query = (query_ref[...].astype(F32) * SCALE).T.astype(BF16)
    for head in range(4):
        part = slice(head * HEAD_SIZE, (head + 1) * HEAD_SIZE)
        held[head, :HEAD_SIZE] = query[part]
        held[head, HEAD_SIZE:PIECE] = back[part]
        held[head, PIECE:] = jnp.concatenate([key_ref[:, part], value_ref[:, part]], axis=1)
    for partner in range(4):
        outs[partner][...] = held[place_ref[0] ^ partner]


def own_head_kernel(place_ref, *refs):
    parts, (qb_ref, kv_ref) = refs[:4], refs[4:]
    for partner, part in enumerate(parts):
        source = place_ref[0] ^ partner
        qb_ref[source] = part[:PIECE, :]
        kv_ref[source] = part[PIECE:, :]


def key_piece(place_ref, source, partner):
    return 8 * (source // 2) + 2 * (place_ref[3] ^ partner) + source % 2


def prepare_queries(qb_refs, held):
    for part, ref in enumerate(qb_refs):
        for source in range(4):
            held[8 * (source // 2) + 2 * part + source % 2] = ref[source]


def prepare_keys(place_ref, kv_refs, onehot_ref, masked_keys, plain, turned):
    lane = lax.broadcasted_iota(jnp.int32, (PIECE, PIECE), 1)
    for partner, ref in enumerate(kv_refs):
        for source in range(4):
            piece = key_piece(place_ref, source, partner)
            both = ref[source]
            masked_keys[piece] = jnp.where(lane < HEAD_SIZE, both, onehot_ref[piece])
            turned[piece] = both.astype(F32).T.astype(BF16)
            if plain is not None:
                plain[piece] = both


def query_pieces(held, block):
    return jnp.concatenate([held[4 * block + part] for part in range(4)], axis=1)


def query_side(place_ref, held, ids_ref, block):
    both = query_pieces(held, block)
    own = 8 * (block // 2) if isinstance(block, int) else 8 * (block >> 1)
    first = own + 4 * ((place_ref[1] >> 1) ^ (block & 1))
    ids = jnp.concatenate(
        [ids_ref[first + 2 * ((place_ref[1] & 1) ^ (part // 2)) + part % 2] for part in range(4)], axis=1
    )
    row = lax.broadcasted_iota(jnp.int32, (HEAD_SIZE, QUERY_BLOCK), 0)
    hidden = (row > ids) & (row < FSCALES)
    penalty = jnp.where(hidden, HIDE, 0.0).astype(BF16)
    return both, jnp.concatenate([both[:HEAD_SIZE], penalty], axis=0)


def rows_of(ref, step, size=STEP):
    return ref[pl.ds(size * step, size)].reshape(size * PIECE, PIECE)


def turned_of(ref, step, first, size=STEP):
    return jnp.concatenate(
        [ref[size * step + part, first:first + HEAD_SIZE, :] for part in range(size)], axis=1
    )


def coarse_side(kvc_ref):
    both = kvc_ref[...]
    lane = lax.broadcasted_iota(jnp.int32, both.shape, 1)
    only_keys = jnp.where(lane < HEAD_SIZE, both, jnp.zeros_like(both))
    return both, only_keys, both.astype(F32).T.astype(BF16)


def forward_kernel(
    place_ref, steps_ref, kv0, kv1, kv2, kv3, onehot_ref, kvc_ref, qb0, qb1, qb2, qb3, ids_ref,
    out_ref, stats_ref, masked_keys, turned, query_held, queries_held, scores_held,
):
    prepare_keys(place_ref, (kv0, kv1, kv2, kv3), onehot_ref, masked_keys, None, turned)
    prepare_queries((qb0, qb1, qb2, qb3), query_held)
    _, coarse_keys, coarse_turned = coarse_side(kvc_ref)
    for block in range(QUERY_BLOCKS):
        _, queries = query_side(place_ref, query_held, ids_ref, block)
        queries_held[block] = queries
        scores = product(coarse_keys, queries)
        top = jnp.max(scores, axis=0, keepdims=True)
        probs = jnp.exp(scores - top)
        total = jnp.sum(probs, axis=0, keepdims=True)
        out_ref[block] = product(coarse_turned[HEAD_SIZE:], probs.astype(BF16))
        stats_ref[block] = jnp.concatenate([top, total, jnp.zeros((6, QUERY_BLOCK), F32)], axis=0)

    def one_block(block, _):
        queries = queries_held[block]
        steps = steps_ref[block ^ (place_ref[1] >> 1)]
        last = steps - 1
        scores_held[0] = product(rows_of(masked_keys, 0), queries)

        def one_step(step, carried):
            top, total, accum = carried
            slot = step & 1
            scores = scores_held[slot]
            scores_held[1 - slot] = product(rows_of(masked_keys, jnp.minimum(step + 1, last)), queries)
            new_top = jnp.maximum(top, jnp.max(scores, axis=0, keepdims=True))
            fade = jnp.exp(top - new_top)
            probs = jnp.exp(scores - new_top)
            total = total * fade + jnp.sum(probs, axis=0, keepdims=True)
            accum = accum * fade + product(turned_of(turned, step, HEAD_SIZE), probs.astype(BF16))
            return new_top, total, accum

        start = stats_ref[block]
        top, total, accum = lax.fori_loop(
            0, steps, one_step, (start[0:1], start[1:2], out_ref[block])
        )
        back = query_pieces(query_held, block)[HEAD_SIZE:]
        offset = jnp.sum(back.astype(F32) * accum, axis=0, keepdims=True)
        out_ref[block] = accum
        stats_ref[block] = jnp.concatenate(
            [top, total, offset, jnp.zeros((5, QUERY_BLOCK), F32)], axis=0
        )
        return 0

    lax.fori_loop(0, QUERY_BLOCKS, one_block, 0)


def backward_kernel(
    place_ref, steps_ref, kv0, kv1, kv2, kv3, onehot_ref, kvc_ref, qb0, qb1, qb2, qb3, ids_ref, accum_ref, own_ref,
    stats1, stats2, stats3, od0, od1, od2, od3, dkv0, dkv1, dkv2, dkv3,
    masked_keys, plain, turned, query_held, out_held, key_sums, coarse_sums,
):
    prepare_keys(place_ref, (kv0, kv1, kv2, kv3), onehot_ref, masked_keys, plain, turned)
    prepare_queries((qb0, qb1, qb2, qb3), query_held)
    coarse_both, coarse_keys, coarse_turned = coarse_side(kvc_ref)
    key_sums[...] = jnp.zeros_like(key_sums)
    coarse_sums[...] = jnp.zeros_like(coarse_sums)

    def one_block(block, _):
        both, queries = query_side(place_ref, query_held, ids_ref, block)
        stats = [own_ref[block]]
        for partner, ref in enumerate((stats1, stats2, stats3), 1):
            theirs = ref[block ^ (partner // 2)]
            flip = 2 * (partner % 2)
            parts = [theirs[:, (part ^ flip) * PIECE:((part ^ flip) + 1) * PIECE] for part in range(4)]
            stats.append(jnp.concatenate(parts, axis=1))
        top = stats[0][0:1]
        for other in stats[1:]:
            top = jnp.maximum(top, other[0:1])
        total = jnp.zeros_like(top)
        offset = jnp.zeros_like(top)
        for other in stats:
            fade = jnp.exp(other[0:1] - top)
            total = total + fade * other[1:2]
            offset = offset + fade * other[2:3]
        offset = offset / total
        log_total = top + jnp.log(total)
        attended = accum_ref[block] * (jnp.exp(own_ref[block][0:1] - top) / total)
        back = jnp.concatenate(
            [jnp.zeros((HEAD_SIZE, QUERY_BLOCK), BF16), both[HEAD_SIZE:]], axis=0
        )
        token_rows = both.astype(F32).T
        lane = lax.broadcasted_iota(jnp.int32, token_rows.shape, 1)
        query_rows = jnp.where(lane < HEAD_SIZE, token_rows, 0.0).astype(BF16)
        back_rows = jnp.where(lane < HEAD_SIZE, 0.0, token_rows).astype(BF16)

        def terms(only_keys, key_value, key_turned):
            probs = jnp.exp(product(only_keys, queries) - log_total)
            grad_probs = product(key_value, back)
            grad_scores = (probs * (grad_probs - offset)).astype(BF16)
            key_side = product(grad_scores, query_rows) + product(probs.astype(BF16), back_rows)
            return product(key_turned, grad_scores), key_side

        query_grad, coarse_term = terms(coarse_keys, coarse_both, coarse_turned[:HEAD_SIZE])
        coarse_sums[...] += coarse_term

        def one_step(step, query_grad):
            query_term, key_side = terms(
                rows_of(masked_keys, step, 4), rows_of(plain, step, 4), turned_of(turned, step, 0, 4)
            )
            key_sums[pl.ds(4 * step, 4)] += key_side.reshape(4, PIECE, PIECE)
            return query_grad + query_term

        steps = lax.div(steps_ref[block ^ (place_ref[1] >> 1)] + 1, 2)
        query_grad = lax.fori_loop(0, steps, one_step, query_grad)
        both_out = jnp.concatenate([attended, query_grad * SCALE], axis=0).astype(BF16)
        for part in range(4):
            out_held[4 * block + part] = both_out[:, part * PIECE:(part + 1) * PIECE]
        return 0

    lax.fori_loop(0, QUERY_BLOCKS, one_block, 0)
    for part, ref in enumerate((od0, od1, od2, od3)):
        for source in range(4):
            ref[source] = out_held[8 * (source // 2) + 2 * part + source % 2]
    coarse = coarse_sums[...].astype(BF16)
    for partner, ref in enumerate((dkv0, dkv1, dkv2, dkv3)):
        for source in range(4):
            piece = key_sums[key_piece(place_ref, source, partner)]
            ref[source * PIECE:(source + 1) * PIECE, :] = piece.astype(BF16)
        ref[4 * PIECE:, :] = coarse


def coarse_probs(query, key, bias):
    scores = product_nt(key, query) + bias
    top = jnp.max(scores, axis=0, keepdims=True)
    total = jnp.sum(jnp.exp(scores - top), axis=0, keepdims=True)
    return jnp.exp(scores - (top + jnp.log(total)))


def head_columns(ref, head):
    return ref[:, head * HEAD_SIZE:(head + 1) * HEAD_SIZE]


def packet_kernel(place_ref, query_ref, key_ref, value_ref, bias_ref, weight_ref, grad_ref, *refs):
    outs, held = refs[:4], refs[4]
    for part in range(4):
        held[part] = weight_ref[:, part * 480:(part + 1) * 480].astype(F32).T.astype(BF16)
    attended = []
    for head in range(4):
        query = (head_columns(query_ref, head).astype(F32) * SCALE).astype(BF16)
        probs = coarse_probs(query, head_columns(key_ref, head), bias_ref[...])
        attended.append(product_tn(head_columns(value_ref, head), probs.astype(BF16)).astype(BF16))
    attended = jnp.concatenate(attended, axis=0)
    for partner in range(4):
        outs[partner][:480, :] = held[place_ref[2] ^ partner]
        outs[partner][480:960, :] = grad_ref[...]
        outs[partner][960:, :] = attended


def coarse_kernel(query_ref, key_ref, value_ref, bias_ref, *refs):
    packets, weights, (mixed_ref, dq_ref, dk_ref, dv_ref) = refs[:4], refs[4:8], refs[8:]
    back_all = sum(
        product(weight[...], packet[480:960, :]) for weight, packet in zip(weights, packets)
    ).astype(BF16)
    mixed_ref[...] = sum(product(packet[:480, :], packet[960:, :]) for packet in packets).astype(BF16)
    query_grads, key_grads, value_grads = [], [], []
    for head in range(4):
        part = slice(head * HEAD_SIZE, (head + 1) * HEAD_SIZE)
        query = (query_ref[:, part].astype(F32) * SCALE).astype(BF16)
        key, value, back = key_ref[:, part], value_ref[:, part], back_all[part]
        probs = coarse_probs(query, key, bias_ref[...])
        rounded = probs.astype(BF16)
        attended = packets[0][960 + part.start:960 + part.stop, :]
        offset = jnp.sum(back.astype(F32) * attended.astype(F32), axis=0, keepdims=True)
        grad_scores = (probs * (product(value, back) - offset)).astype(BF16)
        query_grads.append(product_tn(key, grad_scores) * SCALE)
        key_grads.append(product(grad_scores, query))
        value_grads.append(product_nt(rounded, back))
    dq_ref[...] = jnp.concatenate(query_grads, axis=0).T.astype(BF16)
    dk_ref[...] = jnp.concatenate(key_grads, axis=1)
    dv_ref[...] = jnp.concatenate(value_grads, axis=1)


def sums_kernel(place_ref, *refs):
    od, dkv, outs, held = refs[:4], refs[4:8], refs[8:12], refs[12]
    for source in range(4):
        rows = slice(source * PIECE, (source + 1) * PIECE)
        held[source, :PIECE] = sum(part[source].astype(F32) for part in od).astype(BF16)
        held[source, PIECE:] = sum(part[rows, :].astype(F32) for part in dkv).astype(BF16)
    coarse = sum(part[4 * PIECE:, :].astype(F32) for part in dkv).astype(BF16)
    for partner in range(4):
        outs[partner][:2 * PIECE, :] = held[place_ref[0] ^ partner]
        outs[partner][2 * PIECE:, :] = coarse


def heads_kernel(place_ref, *refs):
    parts, (att_ref, dq_ref, dk_ref, dv_ref, coarse_ref, query_held, key_held) = refs[:4], refs[4:]
    for partner, part in enumerate(parts):
        head = place_ref[0] ^ partner
        rows = pl.ds(pl.multiple_of(head * HEAD_SIZE, HEAD_SIZE), HEAD_SIZE)
        att_ref[rows, :] = part[:HEAD_SIZE, :]
        query_held[rows, :] = part[HEAD_SIZE:PIECE, :].astype(F32)
        key_held[head] = part[PIECE:2 * PIECE, :]
        coarse_ref[head] = part[2 * PIECE:, :]
    dq_ref[...] = query_held[...].T.astype(BF16)
    dk_ref[...] = jnp.concatenate([key_held[head, :, :HEAD_SIZE] for head in range(4)], axis=1)
    dv_ref[...] = jnp.concatenate([key_held[head, :, HEAD_SIZE:] for head in range(4)], axis=1)


def last_kernel(place_ref, *refs):
    attended, packets, received = refs[:4], refs[4:8], refs[8:12]
    dk_ref, dv_ref, mixed_ref, dk_out, dv_out = refs[12:]
    mixed_ref[...] = sum(
        product(packet[:480, :], att[...]) for packet, att in zip(packets, attended)
    ).astype(BF16)
    for partner, ref in enumerate(received):
        rows = pl.ds(pl.multiple_of((place_ref[1] ^ partner) * 64, 64), 64)
        parts = [ref[head].astype(F32) for head in range(4)]
        keys = jnp.concatenate([part[:, :HEAD_SIZE] for part in parts], axis=1)
        values = jnp.concatenate([part[:, HEAD_SIZE:] for part in parts], axis=1)
        dk_out[rows, :] = (dk_ref[rows, :] + keys).astype(BF16)
        dv_out[rows, :] = (dv_ref[rows, :] + values).astype(BF16)


def swap(arrays, axes):
    out = [arrays[0]]
    sent = {
        partner: lax.ppermute(arrays[partner], axes, [(i, i ^ partner) for i in range(4)])
        for partner in (1, 3, 2)
    }
    return out + [sent[1], sent[2], sent[3]]


def on_device(
    query_fine, key_fine, value_fine, query_coarse, key_coarse, value_coarse,
    out_weight, grad_fine, grad_coarse, fine_scale, coarse_scale,
):
    place = {name: lax.axis_index(name) for name in SEQ}
    head_of = place["xh"] * 2 + place["za"]
    tile_of = place["yh"] * 2 + place["yl"]
    placed = jnp.stack(
        [head_of, tile_of, lax.axis_index("head"), place["zc"] * 2 + place["zb"]]
    ).astype(jnp.int32)

    grads = swap([grad_fine.T] * 4, "head")
    weights = call(
        weight_blocks_kernel, (shape(256, 480),) * 4, [pltpu.VMEM((4, 256, 480), BF16)], 1, moved=2**21
    )(placed, out_weight)
    packed = call(
        pack_kernel, (shape(2 * PIECE, PIECE),) * 4, [pltpu.VMEM((4, 2 * PIECE, PIECE), BF16)], 1,
        flops=2 * 128 * 256 * 1920, moved=2**21,
    )(placed, query_fine, key_fine, value_fine, *grads, *weights)
    own_qb, own_kv = call(own_head_kernel, (shape(4, PIECE, PIECE),) * 2, (), 1, moved=2**19)(
        placed, *swap(packed, HEADS)
    )
    kv = swap([own_kv] * 4, QUERY_TILES)
    qb = swap([own_qb] * 4, KEY_TILES)

    ids = fine_scale.reshape(2, 2, 2, 2, 2, 2, PIECE)
    query_ids = lax.dynamic_index_in_dim(ids, place["zc"], 3, keepdims=False)
    query_ids = lax.dynamic_index_in_dim(query_ids, place["zb"], 3, keepdims=False)
    query_ids = query_ids.reshape(PIECES, 1, PIECE)
    key_ids = lax.dynamic_index_in_dim(ids, place["yh"], 1, keepdims=False)
    key_ids = lax.dynamic_index_in_dim(key_ids, place["yl"], 1, keepdims=False)
    key_ids = key_ids.reshape(PIECES, PIECE)
    lane = lax.broadcasted_iota(jnp.int32, (PIECES, PIECE, PIECE), 2)
    onehot = (lane - HEAD_SIZE == key_ids[:, :, None]).astype(BF16)
    seen = jnp.sum(key_ids[None, :, 0] <= query_ids[3::4, 0, -1:], axis=1)
    steps = ((seen + STEP - 1) // STEP).astype(jnp.int32)

    coarse_rows = [
        lax.dynamic_slice(array, (tile_of * 64, 0), (64, 256)).reshape(64, 4, HEAD_SIZE)
        for array in (key_coarse, value_coarse)
    ]
    kvc = jnp.concatenate(
        [lax.dynamic_index_in_dim(rows, head_of, 1, keepdims=False) for rows in coarse_rows], axis=1
    )

    bias = jnp.where(coarse_scale[:, None] <= coarse_scale[None, :], 0.0, -1e9).astype(F32)
    packed = call(
        packet_kernel, (shape(1216, 256),) * 4, [pltpu.VMEM((4, 480, 256), BF16)], 1,
        flops=2**28, moved=2**22, exps=2**18,
    )(placed, query_coarse, key_coarse, value_coarse, bias, out_weight, grad_coarse.T)
    kv, qb, packed, onehot, kvc, steps, query_ids = lax.optimization_barrier(
        (kv, qb, packed, onehot, kvc, steps, query_ids)
    )

    half = [pltpu.VMEM((PIECES, PIECE, PIECE), BF16)]
    accum, stats = call(
        forward_kernel,
        (shape(QUERY_BLOCKS, HEAD_SIZE, QUERY_BLOCK, dtype=F32), shape(QUERY_BLOCKS, 8, QUERY_BLOCK, dtype=F32)),
        half * 3 + [
            pltpu.VMEM((QUERY_BLOCKS, PIECE, QUERY_BLOCK), BF16),
            pltpu.VMEM((2, STEP * PIECE, QUERY_BLOCK), F32),
        ],
        2,
    )(placed, steps, *kv, onehot, kvc, *qb, query_ids)
    packets = swap(packed, "head")
    stats, packets[1] = lax.optimization_barrier((stats, packets[1]))
    all_stats = swap([stats] * 4, KEY_TILES)
    parts = call(
        backward_kernel,
        (shape(4, PIECE, PIECE),) * 4 + (shape(4 * PIECE + 64, PIECE),) * 4,
        half * 5 + [pltpu.VMEM((PIECES, PIECE, PIECE), F32), pltpu.VMEM((64, PIECE), F32)],
        2, 10 * 2048 * 2112 * 64, 2**22, 2048 * 2112,
    )(placed, steps, *kv, onehot, kvc, *qb, query_ids, accum, *all_stats)

    parts, packets = lax.optimization_barrier((parts, packets))
    dkv = swap(parts[4:], QUERY_TILES)
    od = swap(parts[:4], KEY_TILES)
    mixed_coarse, dq_coarse, dk_coarse, dv_coarse = call(
        coarse_kernel,
        (shape(480, 256), shape(256, 256), shape(256, 256, dtype=F32), shape(256, 256, dtype=F32)),
        flops=2**29, moved=2**22, exps=2**19,
    )(query_coarse, key_coarse, value_coarse, bias, *packets, *weights)
    dkv, dk_coarse = lax.optimization_barrier((dkv, dk_coarse))
    sums = call(
        sums_kernel, (shape(2 * PIECE + 64, PIECE),) * 4, [pltpu.VMEM((4, 2 * PIECE, PIECE), BF16)], 1, moved=2**21
    )(placed, *od, *dkv)
    att_fine, dq_fine, dk_fine, dv_fine, coarse_part = call(
        heads_kernel,
        (shape(256, PIECE),) + (shape(PIECE, 256),) * 3 + (shape(4, 64, PIECE),),
        [pltpu.VMEM((256, PIECE), F32), pltpu.VMEM((4, PIECE, PIECE), BF16)], 1, moved=2**20,
    )(placed, *swap(sums, HEADS))
    coarse_parts = swap([coarse_part] * 4, KEY_TILES)
    attended = swap([att_fine] * 4, "head")
    mixed_fine, dk_coarse, dv_coarse = call(
        last_kernel, (shape(480, PIECE), shape(256, 256), shape(256, 256)), (), 1, flops=2**27, moved=2**20
    )(placed, *attended, *packets, *coarse_parts, dk_coarse, dv_coarse)
    return (
        mixed_fine.T, mixed_coarse.T, dq_fine, dk_fine, dv_fine, dq_coarse, dk_coarse, dv_coarse,
    )


def solution(mesh):
    fine_mesh = Mesh(mesh.devices.reshape(2, 2, 2, 2, 2, 2, 4), SEQ + ("head",))
    in_specs = (
        P(SEQ, "head"), P(SEQ, "head"), P(SEQ, "head"),
        P(None, "head"), P(None, "head"), P(None, "head"),
        P("head", None), P(SEQ, "head"), P(None, "head"), P(), P(),
    )
    out_specs = (
        P(SEQ, "head"), P(None, "head"),
        P(SEQ, "head"), P(SEQ, "head"), P(SEQ, "head"),
        P(None, "head"), P(None, "head"), P(None, "head"),
    )
    return jax.shard_map(
        on_device, mesh=fine_mesh, in_specs=in_specs, out_specs=out_specs, check_vma=False
    )
```

```python
import jax
import jax.numpy as jnp
from jax import lax
from jax.experimental import pallas as pl
from jax.experimental.pallas import tpu as pltpu
from jax.sharding import Mesh
from jax.sharding import PartitionSpec as P

HEAD_SIZE = 64
SCALE = HEAD_SIZE ** (-0.5)
FSCALES = 3
HIDE = -30000.0
PIECE = 128
PIECES = 16
QUERY_BLOCKS = 4
QUERY_BLOCK = 512
STEP = 2
F32 = jnp.float32
BF16 = jnp.bfloat16

SEQ = ("xh", "yh", "yl", "zc", "zb", "za")
HEADS = ("xh", "za")
QUERY_TILES = ("zc", "zb")
KEY_TILES = ("yh", "yl")


def product(left, right):
    return jnp.dot(left, right, preferred_element_type=F32)


def product_nt(left, right):
    return lax.dot_general(left, right, (((1,), (1,)), ((), ())), preferred_element_type=F32)


def product_tn(left, right):
    return lax.dot_general(left, right, (((0,), (0,)), ((), ())), preferred_element_type=F32)


def call(kernel, outs, scratch=(), smem=0, flops=0, moved=0, exps=0):
    def run(*operands):
        return pl.pallas_call(
            kernel,
            out_shape=outs,
            in_specs=[pl.BlockSpec(memory_space=pltpu.SMEM)] * smem
            + [pl.BlockSpec(memory_space=pltpu.VMEM)] * (len(operands) - smem),
            out_specs=jax.tree.map(lambda _: pl.BlockSpec(memory_space=pltpu.VMEM), outs),
            scratch_shapes=list(scratch),
            compiler_params=pltpu.CompilerParams(vmem_limit_bytes=48 * 2**20),
            cost_estimate=pl.CostEstimate(
                flops=flops, bytes_accessed=moved, transcendentals=exps
            ),
        )(*operands)

    return run


def shape(*dims, dtype=BF16):
    return jax.ShapeDtypeStruct(dims, dtype)


def weight_blocks_kernel(place_ref, weight_ref, *refs):
    outs, held = refs[:4], refs[4]
    for part in range(4):
        held[part] = weight_ref[:, part * 480:(part + 1) * 480]
    for partner in range(4):
        outs[partner][...] = held[place_ref[2] ^ partner]


def pack_kernel(place_ref, query_ref, key_ref, value_ref, *refs):
    grads, weights, outs, held = refs[:4], refs[4:8], refs[8:12], refs[12]
    back = sum(product(weight[...], grad[...]) for weight, grad in zip(weights, grads)).astype(BF16)
    query = (query_ref[...].astype(F32) * SCALE).T.astype(BF16)
    for head in range(4):
        part = slice(head * HEAD_SIZE, (head + 1) * HEAD_SIZE)
        held[head, :HEAD_SIZE] = query[part]
        held[head, HEAD_SIZE:PIECE] = back[part]
        held[head, PIECE:] = jnp.concatenate([key_ref[:, part], value_ref[:, part]], axis=1)
    for partner in range(4):
        outs[partner][...] = held[place_ref[0] ^ partner]


def own_head_kernel(place_ref, *refs):
    parts, (qb_ref, kv_ref) = refs[:4], refs[4:]
    for partner, part in enumerate(parts):
        source = place_ref[0] ^ partner
        qb_ref[source] = part[:PIECE, :]
        kv_ref[source] = part[PIECE:, :]


def key_piece(place_ref, source, partner):
    return 8 * (source // 2) + 2 * (place_ref[3] ^ partner) + source % 2


def prepare_queries(qb_refs, held):
    for part, ref in enumerate(qb_refs):
        for source in range(4):
            held[8 * (source // 2) + 2 * part + source % 2] = ref[source]


def prepare_keys(place_ref, kv_refs, onehot_ref, masked_keys, plain, turned):
    lane = lax.broadcasted_iota(jnp.int32, (PIECE, PIECE), 1)
    for partner, ref in enumerate(kv_refs):
        for source in range(4):
            piece = key_piece(place_ref, source, partner)
            both = ref[source]
            masked_keys[piece] = jnp.where(lane < HEAD_SIZE, both, onehot_ref[piece])
            turned[piece] = both.astype(F32).T.astype(BF16)
            plain[piece] = both


def query_pieces(held, block):
    return jnp.concatenate([held[4 * block + part] for part in range(4)], axis=1)


def query_side(place_ref, held, ids_ref, block):
    both = query_pieces(held, block)
    own = 8 * (block // 2) if isinstance(block, int) else 8 * (block >> 1)
    first = own + 4 * ((place_ref[1] >> 1) ^ (block & 1))
    ids = jnp.concatenate(
        [ids_ref[first + 2 * ((place_ref[1] & 1) ^ (part // 2)) + part % 2] for part in range(4)], axis=1
    )
    row = lax.broadcasted_iota(jnp.int32, (HEAD_SIZE, QUERY_BLOCK), 0)
    hidden = (row > ids) & (row < FSCALES)
    penalty = jnp.where(hidden, HIDE, 0.0).astype(BF16)
    return both, jnp.concatenate([both[:HEAD_SIZE], penalty], axis=0)


def rows_of(ref, step, size=STEP):
    return ref[pl.ds(size * step, size)].reshape(size * PIECE, PIECE)


def turned_of(ref, step, first, size=STEP):
    return jnp.concatenate(
        [ref[size * step + part, first:first + HEAD_SIZE, :] for part in range(size)], axis=1
    )


def coarse_side(kvc_ref):
    both = kvc_ref[...]
    lane = lax.broadcasted_iota(jnp.int32, both.shape, 1)
    only_keys = jnp.where(lane < HEAD_SIZE, both, jnp.zeros_like(both))
    return both, only_keys, both.astype(F32).T.astype(BF16)


def forward_kernel(
    place_ref, steps_ref, kv0, kv1, kv2, kv3, onehot_ref, kvc_ref, qb0, qb1, qb2, qb3, ids_ref,
    out_ref, packed_ref, masked_keys, plain, turned, query_held, queries_held, scores_held, stats_ref,
):
    prepare_keys(place_ref, (kv0, kv1, kv2, kv3), onehot_ref, masked_keys, plain, turned)
    prepare_queries((qb0, qb1, qb2, qb3), query_held)
    _, coarse_keys, coarse_turned = coarse_side(kvc_ref)
    for block in range(QUERY_BLOCKS):
        _, queries = query_side(place_ref, query_held, ids_ref, block)
        queries_held[block] = queries
        scores = product(coarse_keys, queries)
        top = jnp.max(scores, axis=0, keepdims=True)
        probs = jnp.exp(scores - top)
        total = jnp.sum(probs, axis=0, keepdims=True)
        out_ref[block] = product(coarse_turned[HEAD_SIZE:], probs.astype(BF16))
        stats_ref[block] = jnp.concatenate([top, total, jnp.zeros((6, QUERY_BLOCK), F32)], axis=0)

    def one_block(block, _):
        queries = queries_held[block]
        steps = steps_ref[block ^ (place_ref[1] >> 1)]
        last = steps - 1
        scores_held[0] = product(rows_of(masked_keys, 0), queries)

        def one_step(step, carried):
            top, total, accum = carried
            slot = step & 1
            scores = scores_held[slot]
            scores_held[1 - slot] = product(rows_of(masked_keys, jnp.minimum(step + 1, last)), queries)
            new_top = jnp.maximum(top, jnp.max(scores, axis=0, keepdims=True))
            fade = jnp.exp(top - new_top)
            probs = jnp.exp(scores - new_top)
            total = total * fade + jnp.sum(probs, axis=0, keepdims=True)
            accum = accum * fade + product(turned_of(turned, step, HEAD_SIZE), probs.astype(BF16))
            return new_top, total, accum

        start = stats_ref[block]
        top, total, accum = lax.fori_loop(
            0, steps, one_step, (start[0:1], start[1:2], out_ref[block])
        )
        back = query_pieces(query_held, block)[HEAD_SIZE:]
        offset = jnp.sum(back.astype(F32) * accum, axis=0, keepdims=True)
        out_ref[block] = accum
        stats_ref[block] = jnp.concatenate(
            [top, total, offset, jnp.zeros((5, QUERY_BLOCK), F32)], axis=0
        )
        return 0

    lax.fori_loop(0, QUERY_BLOCKS, one_block, 0)
    for pair in range(2):
        packed_ref[pair] = jnp.concatenate([stats_ref[2 * pair, :4, :], stats_ref[2 * pair + 1, :4, :]], axis=0)


def backward_kernel(
    place_ref, steps_ref, masked_keys, plain, turned, query_held, kvc_ref, ids_ref, accum_ref,
    stats0, stats1, stats2, stats3, od0, od1, od2, od3, dkv0, dkv1, dkv2, dkv3,
    out_held, key_sums, coarse_sums, stats_held,
):
    for partner, ref in enumerate((stats0, stats1, stats2, stats3)):
        for block in range(QUERY_BLOCKS):
            rows = slice(4 * (block % 2), 4 * (block % 2) + 4)
            stats_held[4 * partner + block, :4, :] = ref[block // 2, rows, :]
    coarse_both, coarse_keys, coarse_turned = coarse_side(kvc_ref)
    key_sums[...] = jnp.zeros_like(key_sums)
    coarse_sums[...] = jnp.zeros_like(coarse_sums)

    def one_block(block, _):
        both, queries = query_side(place_ref, query_held, ids_ref, block)
        own = stats_held[block]
        stats = [own]
        for partner in (1, 2, 3):
            theirs = stats_held[4 * partner + (block ^ (partner // 2))]
            flip = 2 * (partner % 2)
            parts = [theirs[:, (part ^ flip) * PIECE:((part ^ flip) + 1) * PIECE] for part in range(4)]
            stats.append(jnp.concatenate(parts, axis=1))
        top = stats[0][0:1]
        for other in stats[1:]:
            top = jnp.maximum(top, other[0:1])
        total = jnp.zeros_like(top)
        offset = jnp.zeros_like(top)
        for other in stats:
            fade = jnp.exp(other[0:1] - top)
            total = total + fade * other[1:2]
            offset = offset + fade * other[2:3]
        offset = offset / total
        log_total = top + jnp.log(total)
        attended = accum_ref[block] * (jnp.exp(own[0:1] - top) / total)
        back = jnp.concatenate(
            [jnp.zeros((HEAD_SIZE, QUERY_BLOCK), BF16), both[HEAD_SIZE:]], axis=0
        )
        token_rows = both.astype(F32).T
        lane = lax.broadcasted_iota(jnp.int32, token_rows.shape, 1)
        query_rows = jnp.where(lane < HEAD_SIZE, token_rows, 0.0).astype(BF16)
        back_rows = jnp.where(lane < HEAD_SIZE, 0.0, token_rows).astype(BF16)

        def terms(only_keys, key_value, key_turned):
            probs = jnp.exp(product(only_keys, queries) - log_total)
            grad_probs = product(key_value, back)
            grad_scores = (probs * (grad_probs - offset)).astype(BF16)
            key_side = product(grad_scores, query_rows) + product(probs.astype(BF16), back_rows)
            return product(key_turned, grad_scores), key_side

        query_grad, coarse_term = terms(coarse_keys, coarse_both, coarse_turned[:HEAD_SIZE])
        coarse_sums[...] += coarse_term

        def one_step(step, query_grad):
            query_term, key_side = terms(
                rows_of(masked_keys, step, 4), rows_of(plain, step, 4), turned_of(turned, step, 0, 4)
            )
            key_sums[pl.ds(4 * step, 4)] += key_side.reshape(4, PIECE, PIECE)
            return query_grad + query_term

        steps = lax.div(steps_ref[block ^ (place_ref[1] >> 1)] + 1, 2)
        query_grad = lax.fori_loop(0, steps, one_step, query_grad)
        both_out = jnp.concatenate([attended, query_grad * SCALE], axis=0).astype(BF16)
        for part in range(4):
            out_held[4 * block + part] = both_out[:, part * PIECE:(part + 1) * PIECE]
        return 0

    lax.fori_loop(0, QUERY_BLOCKS, one_block, 0)
    for part, ref in enumerate((od0, od1, od2, od3)):
        for source in range(4):
            ref[source] = out_held[8 * (source // 2) + 2 * part + source % 2]
    coarse = coarse_sums[...].astype(BF16)
    for partner, ref in enumerate((dkv0, dkv1, dkv2, dkv3)):
        for source in range(4):
            piece = key_sums[key_piece(place_ref, source, partner)]
            ref[source * PIECE:(source + 1) * PIECE, :] = piece.astype(BF16)
        ref[4 * PIECE:, :] = coarse


def coarse_probs(query, key, bias):
    scores = product_nt(key, query) + bias
    top = jnp.max(scores, axis=0, keepdims=True)
    total = jnp.sum(jnp.exp(scores - top), axis=0, keepdims=True)
    return jnp.exp(scores - (top + jnp.log(total)))


def head_columns(ref, head):
    return ref[:, head * HEAD_SIZE:(head + 1) * HEAD_SIZE]


def packet_kernel(place_ref, query_ref, key_ref, value_ref, bias_ref, weight_ref, grad_ref, *refs):
    outs, held = refs[:4], refs[4]
    for part in range(4):
        held[part] = weight_ref[:, part * 480:(part + 1) * 480].astype(F32).T.astype(BF16)
    attended = []
    for head in range(4):
        query = (head_columns(query_ref, head).astype(F32) * SCALE).astype(BF16)
        probs = coarse_probs(query, head_columns(key_ref, head), bias_ref[...])
        attended.append(product_tn(head_columns(value_ref, head), probs.astype(BF16)).astype(BF16))
    attended = jnp.concatenate(attended, axis=0)
    for partner in range(4):
        outs[partner][:480, :] = held[place_ref[2] ^ partner]
        outs[partner][480:960, :] = grad_ref[...]
        outs[partner][960:, :] = attended


def coarse_kernel(query_ref, key_ref, value_ref, bias_ref, *refs):
    packets, weights, (mixed_ref, dq_ref, dk_ref, dv_ref) = refs[:4], refs[4:8], refs[8:]
    back_all = sum(
        product(weight[...], packet[480:960, :]) for weight, packet in zip(weights, packets)
    ).astype(BF16)
    mixed_ref[...] = sum(product(packet[:480, :], packet[960:, :]) for packet in packets).astype(BF16)
    query_grads, key_grads, value_grads = [], [], []
    for head in range(4):
        part = slice(head * HEAD_SIZE, (head + 1) * HEAD_SIZE)
        query = (query_ref[:, part].astype(F32) * SCALE).astype(BF16)
        key, value, back = key_ref[:, part], value_ref[:, part], back_all[part]
        probs = coarse_probs(query, key, bias_ref[...])
        rounded = probs.astype(BF16)
        attended = packets[0][960 + part.start:960 + part.stop, :]
        offset = jnp.sum(back.astype(F32) * attended.astype(F32), axis=0, keepdims=True)
        grad_scores = (probs * (product(value, back) - offset)).astype(BF16)
        query_grads.append(product_tn(key, grad_scores) * SCALE)
        key_grads.append(product(grad_scores, query))
        value_grads.append(product_nt(rounded, back))
    dq_ref[...] = jnp.concatenate(query_grads, axis=0).T.astype(BF16)
    dk_ref[...] = jnp.concatenate(key_grads, axis=1)
    dv_ref[...] = jnp.concatenate(value_grads, axis=1)


def sums_kernel(place_ref, *refs):
    od, dkv, outs, held = refs[:4], refs[4:8], refs[8:12], refs[12]
    for source in range(4):
        rows = slice(source * PIECE, (source + 1) * PIECE)
        held[source, :PIECE] = sum(part[source].astype(F32) for part in od).astype(BF16)
        held[source, PIECE:] = sum(part[rows, :].astype(F32) for part in dkv).astype(BF16)
    coarse = sum(part[4 * PIECE:, :].astype(F32) for part in dkv).astype(BF16)
    for partner in range(4):
        outs[partner][:2 * PIECE, :] = held[place_ref[0] ^ partner]
        outs[partner][2 * PIECE:, :] = coarse


def heads_kernel(place_ref, *refs):
    parts, (att_ref, dq_ref, dk_ref, dv_ref, coarse_ref, query_held, key_held) = refs[:4], refs[4:]
    for partner, part in enumerate(parts):
        head = place_ref[0] ^ partner
        rows = pl.ds(pl.multiple_of(head * HEAD_SIZE, HEAD_SIZE), HEAD_SIZE)
        att_ref[rows, :] = part[:HEAD_SIZE, :]
        query_held[rows, :] = part[HEAD_SIZE:PIECE, :].astype(F32)
        key_held[head] = part[PIECE:2 * PIECE, :]
        coarse_ref[head] = part[2 * PIECE:, :]
    dq_ref[...] = query_held[...].T.astype(BF16)
    dk_ref[...] = jnp.concatenate([key_held[head, :, :HEAD_SIZE] for head in range(4)], axis=1)
    dv_ref[...] = jnp.concatenate([key_held[head, :, HEAD_SIZE:] for head in range(4)], axis=1)


def last_kernel(place_ref, *refs):
    attended, packets, received = refs[:4], refs[4:8], refs[8:12]
    dk_ref, dv_ref, mixed_ref, dk_out, dv_out = refs[12:]
    mixed_ref[...] = sum(
        product(packet[:480, :], att[...]) for packet, att in zip(packets, attended)
    ).astype(BF16)
    for partner, ref in enumerate(received):
        rows = pl.ds(pl.multiple_of((place_ref[1] ^ partner) * 64, 64), 64)
        parts = [ref[head].astype(F32) for head in range(4)]
        keys = jnp.concatenate([part[:, :HEAD_SIZE] for part in parts], axis=1)
        values = jnp.concatenate([part[:, HEAD_SIZE:] for part in parts], axis=1)
        dk_out[rows, :] = (dk_ref[rows, :] + keys).astype(BF16)
        dv_out[rows, :] = (dv_ref[rows, :] + values).astype(BF16)


def swap(arrays, axes):
    out = [arrays[0]]
    sent = {
        partner: lax.ppermute(arrays[partner], axes, [(i, i ^ partner) for i in range(4)])
        for partner in (1, 3, 2)
    }
    return out + [sent[1], sent[2], sent[3]]


def on_device(
    query_fine, key_fine, value_fine, query_coarse, key_coarse, value_coarse,
    out_weight, grad_fine, grad_coarse, fine_scale, coarse_scale,
):
    place = {name: lax.axis_index(name) for name in SEQ}
    head_of = place["xh"] * 2 + place["za"]
    tile_of = place["yh"] * 2 + place["yl"]
    placed = jnp.stack(
        [head_of, tile_of, lax.axis_index("head"), place["zc"] * 2 + place["zb"]]
    ).astype(jnp.int32)

    grads = swap([grad_fine.T] * 4, "head")
    weights = call(
        weight_blocks_kernel, (shape(256, 480),) * 4, [pltpu.VMEM((4, 256, 480), BF16)], 1, moved=2**21
    )(placed, out_weight)
    packed = call(
        pack_kernel, (shape(2 * PIECE, PIECE),) * 4, [pltpu.VMEM((4, 2 * PIECE, PIECE), BF16)], 1,
        flops=2 * 128 * 256 * 1920, moved=2**21,
    )(placed, query_fine, key_fine, value_fine, *grads, *weights)
    own_qb, own_kv = call(own_head_kernel, (shape(4, PIECE, PIECE),) * 2, (), 1, moved=2**19)(
        placed, *swap(packed, HEADS)
    )
    kv = swap([own_kv] * 4, QUERY_TILES)
    qb = swap([own_qb] * 4, KEY_TILES)

    ids = fine_scale.reshape(2, 2, 2, 2, 2, 2, PIECE)
    query_ids = lax.dynamic_index_in_dim(ids, place["zc"], 3, keepdims=False)
    query_ids = lax.dynamic_index_in_dim(query_ids, place["zb"], 3, keepdims=False)
    query_ids = query_ids.reshape(PIECES, 1, PIECE)
    key_ids = lax.dynamic_index_in_dim(ids, place["yh"], 1, keepdims=False)
    key_ids = lax.dynamic_index_in_dim(key_ids, place["yl"], 1, keepdims=False)
    key_ids = key_ids.reshape(PIECES, PIECE)
    lane = lax.broadcasted_iota(jnp.int32, (PIECES, PIECE, PIECE), 2)
    onehot = (lane - HEAD_SIZE == key_ids[:, :, None]).astype(BF16)
    seen = jnp.sum(key_ids[None, :, 0] <= query_ids[3::4, 0, -1:], axis=1)
    steps = ((seen + STEP - 1) // STEP).astype(jnp.int32)

    coarse_rows = [
        lax.dynamic_slice(array, (tile_of * 64, 0), (64, 256)).reshape(64, 4, HEAD_SIZE)
        for array in (key_coarse, value_coarse)
    ]
    kvc = jnp.concatenate(
        [lax.dynamic_index_in_dim(rows, head_of, 1, keepdims=False) for rows in coarse_rows], axis=1
    )

    bias = jnp.where(coarse_scale[:, None] <= coarse_scale[None, :], 0.0, -1e9).astype(F32)
    packed = call(
        packet_kernel, (shape(1216, 256),) * 4, [pltpu.VMEM((4, 480, 256), BF16)], 1,
        flops=2**28, moved=2**22, exps=2**18,
    )(placed, query_coarse, key_coarse, value_coarse, bias, out_weight, grad_coarse.T)
    kv, qb, packed, onehot, kvc, steps, query_ids = lax.optimization_barrier(
        (kv, qb, packed, onehot, kvc, steps, query_ids)
    )

    half = [pltpu.VMEM((PIECES, PIECE, PIECE), BF16)]
    accum, stats, *prepared = call(
        forward_kernel,
        (shape(QUERY_BLOCKS, HEAD_SIZE, QUERY_BLOCK, dtype=F32), shape(2, 8, QUERY_BLOCK, dtype=F32))
        + (shape(PIECES, PIECE, PIECE),) * 4,
        [
            pltpu.VMEM((QUERY_BLOCKS, PIECE, QUERY_BLOCK), BF16),
            pltpu.VMEM((2, STEP * PIECE, QUERY_BLOCK), F32),
            pltpu.VMEM((QUERY_BLOCKS, 8, QUERY_BLOCK), F32),
        ],
        2,
    )(placed, steps, *kv, onehot, kvc, *qb, query_ids)
    packets = swap(packed, "head")
    stats, packets[1] = lax.optimization_barrier((stats, packets[1]))
    all_stats = swap([stats] * 4, KEY_TILES)
    parts = call(
        backward_kernel,
        (shape(4, PIECE, PIECE),) * 4 + (shape(4 * PIECE + 64, PIECE),) * 4,
        half
        + [
            pltpu.VMEM((PIECES, PIECE, PIECE), F32),
            pltpu.VMEM((64, PIECE), F32),
            pltpu.VMEM((4 * QUERY_BLOCKS, 8, QUERY_BLOCK), F32),
        ],
        2, 10 * 2048 * 2112 * 64, 2**22, 2048 * 2112,
    )(placed, steps, *prepared, kvc, query_ids, accum, *all_stats)

    parts, packets = lax.optimization_barrier((parts, packets))
    dkv = swap(parts[4:], QUERY_TILES)
    od = swap(parts[:4], KEY_TILES)
    mixed_coarse, dq_coarse, dk_coarse, dv_coarse = call(
        coarse_kernel,
        (shape(480, 256), shape(256, 256), shape(256, 256, dtype=F32), shape(256, 256, dtype=F32)),
        flops=2**29, moved=2**22, exps=2**19,
    )(query_coarse, key_coarse, value_coarse, bias, *packets, *weights)
    dkv, dk_coarse = lax.optimization_barrier((dkv, dk_coarse))
    sums = call(
        sums_kernel, (shape(2 * PIECE + 64, PIECE),) * 4, [pltpu.VMEM((4, 2 * PIECE, PIECE), BF16)], 1, moved=2**21
    )(placed, *od, *dkv)
    att_fine, dq_fine, dk_fine, dv_fine, coarse_part = call(
        heads_kernel,
        (shape(256, PIECE),) + (shape(PIECE, 256),) * 3 + (shape(4, 64, PIECE),),
        [pltpu.VMEM((256, PIECE), F32), pltpu.VMEM((4, PIECE, PIECE), BF16)], 1, moved=2**20,
    )(placed, *swap(sums, HEADS))
    coarse_parts = swap([coarse_part] * 4, KEY_TILES)
    attended = swap([att_fine] * 4, "head")
    mixed_fine, dk_coarse, dv_coarse = call(
        last_kernel, (shape(480, PIECE), shape(256, 256), shape(256, 256)), (), 1, flops=2**27, moved=2**20
    )(placed, *attended, *packets, *coarse_parts, dk_coarse, dv_coarse)
    return (
        mixed_fine.T, mixed_coarse.T, dq_fine, dk_fine, dv_fine, dq_coarse, dk_coarse, dv_coarse,
    )


def solution(mesh):
    fine_mesh = Mesh(mesh.devices.reshape(2, 2, 2, 2, 2, 2, 4), SEQ + ("head",))
    in_specs = (
        P(SEQ, "head"), P(SEQ, "head"), P(SEQ, "head"),
        P(None, "head"), P(None, "head"), P(None, "head"),
        P("head", None), P(SEQ, "head"), P(None, "head"), P(), P(),
    )
    out_specs = (
        P(SEQ, "head"), P(None, "head"),
        P(SEQ, "head"), P(SEQ, "head"), P(SEQ, "head"),
        P(None, "head"), P(None, "head"), P(None, "head"),
    )
    return jax.shard_map(
        on_device, mesh=fine_mesh, in_specs=in_specs, out_specs=out_specs, check_vma=False
    )
```

```python
import jax
import jax.numpy as jnp
from jax import lax
from jax.experimental import pallas as pl
from jax.experimental.pallas import tpu as pltpu
from jax.sharding import Mesh
from jax.sharding import PartitionSpec as P

HEAD_SIZE = 64
SCALE = HEAD_SIZE ** (-0.5)
FSCALES = 3
HIDE = -30000.0
PIECE = 128
PIECES = 16
QUERY_BLOCKS = 4
QUERY_BLOCK = 512
STEP = 2
F32 = jnp.float32
BF16 = jnp.bfloat16

SEQ = ("xh", "yh", "yl", "zc", "zb", "za")
HEADS = ("xh", "za")
QUERY_TILES = ("zc", "zb")
KEY_TILES = ("yh", "yl")


def product(left, right):
    return jnp.dot(left, right, preferred_element_type=F32)


def product_nt(left, right):
    return lax.dot_general(left, right, (((1,), (1,)), ((), ())), preferred_element_type=F32)


def product_tn(left, right):
    return lax.dot_general(left, right, (((0,), (0,)), ((), ())), preferred_element_type=F32)


def call(kernel, outs, scratch=(), smem=0, flops=0, moved=0, exps=0):
    def run(*operands):
        return pl.pallas_call(
            kernel,
            out_shape=outs,
            in_specs=[pl.BlockSpec(memory_space=pltpu.SMEM)] * smem
            + [pl.BlockSpec(memory_space=pltpu.VMEM)] * (len(operands) - smem),
            out_specs=jax.tree.map(lambda _: pl.BlockSpec(memory_space=pltpu.VMEM), outs),
            scratch_shapes=list(scratch),
            compiler_params=pltpu.CompilerParams(vmem_limit_bytes=48 * 2**20),
            cost_estimate=pl.CostEstimate(
                flops=flops, bytes_accessed=moved, transcendentals=exps
            ),
        )(*operands)

    return run


def shape(*dims, dtype=BF16):
    return jax.ShapeDtypeStruct(dims, dtype)


def weight_blocks_kernel(place_ref, weight_ref, *refs):
    outs, held = refs[:4], refs[4]
    for part in range(4):
        held[part] = weight_ref[:, part * 480:(part + 1) * 480]
    for partner in range(4):
        outs[partner][...] = held[place_ref[2] ^ partner]


def pack_kernel(place_ref, query_ref, key_ref, value_ref, *refs):
    grads, weights, outs, held = refs[:4], refs[4:8], refs[8:12], refs[12]
    back = sum(product(weight[...], grad[...]) for weight, grad in zip(weights, grads)).astype(BF16)
    query = (query_ref[...].astype(F32) * SCALE).T.astype(BF16)
    for head in range(4):
        part = slice(head * HEAD_SIZE, (head + 1) * HEAD_SIZE)
        held[head, :HEAD_SIZE] = query[part]
        held[head, HEAD_SIZE:PIECE] = back[part]
        held[head, PIECE:] = jnp.concatenate([key_ref[:, part], value_ref[:, part]], axis=1)
    for partner in range(4):
        outs[partner][...] = held[place_ref[0] ^ partner]


def own_head_kernel(place_ref, *refs):
    parts, (qb_ref, kv_ref) = refs[:4], refs[4:]
    for partner, part in enumerate(parts):
        source = place_ref[0] ^ partner
        qb_ref[source] = part[:PIECE, :]
        kv_ref[source] = part[PIECE:, :]


def key_piece(place_ref, source, partner):
    return 8 * (source // 2) + 2 * (place_ref[3] ^ partner) + source % 2


def prepare_queries(qb_refs, held):
    for part, ref in enumerate(qb_refs):
        for source in range(4):
            held[8 * (source // 2) + 2 * part + source % 2] = ref[source]


def prepare_keys(place_ref, kv_refs, onehot_ref, masked_keys, plain, turned):
    lane = lax.broadcasted_iota(jnp.int32, (PIECE, PIECE), 1)
    for partner, ref in enumerate(kv_refs):
        for source in range(4):
            piece = key_piece(place_ref, source, partner)
            both = ref[source]
            masked_keys[piece] = jnp.where(lane < HEAD_SIZE, both, onehot_ref[piece])
            turned[piece] = both.astype(F32).T.astype(BF16)
            plain[piece] = both


def query_pieces(held, block):
    return jnp.concatenate([held[4 * block + part] for part in range(4)], axis=1)


def query_side(place_ref, held, ids_ref, block):
    both = query_pieces(held, block)
    own = 8 * (block // 2) if isinstance(block, int) else 8 * (block >> 1)
    first = own + 4 * ((place_ref[1] >> 1) ^ (block & 1))
    ids = jnp.concatenate(
        [ids_ref[first + 2 * ((place_ref[1] & 1) ^ (part // 2)) + part % 2] for part in range(4)], axis=1
    )
    row = lax.broadcasted_iota(jnp.int32, (HEAD_SIZE, QUERY_BLOCK), 0)
    hidden = (row > ids) & (row < FSCALES)
    penalty = jnp.where(hidden, HIDE, 0.0).astype(BF16)
    return both, jnp.concatenate([both[:HEAD_SIZE], penalty], axis=0)


def rows_of(ref, step, size=STEP):
    return ref[pl.ds(size * step, size)].reshape(size * PIECE, PIECE)


def turned_of(ref, step, first, size=STEP):
    return jnp.concatenate(
        [ref[size * step + part, first:first + HEAD_SIZE, :] for part in range(size)], axis=1
    )


def coarse_side(kvc_ref):
    both = kvc_ref[...]
    lane = lax.broadcasted_iota(jnp.int32, both.shape, 1)
    only_keys = jnp.where(lane < HEAD_SIZE, both, jnp.zeros_like(both))
    return both, only_keys, both.astype(F32).T.astype(BF16)


def forward_kernel(
    place_ref, steps_ref, kv0, kv1, kv2, kv3, onehot_ref, kvc_ref, qb0, qb1, qb2, qb3, ids_ref,
    out_ref, packed_ref, masked_keys, plain, turned, query_held, queries_held, scores_held, stats_ref,
):
    prepare_keys(place_ref, (kv0, kv1, kv2, kv3), onehot_ref, masked_keys, plain, turned)
    prepare_queries((qb0, qb1, qb2, qb3), query_held)
    _, coarse_keys, coarse_turned = coarse_side(kvc_ref)
    for block in range(QUERY_BLOCKS):
        _, queries = query_side(place_ref, query_held, ids_ref, block)
        queries_held[block] = queries
        scores = product(coarse_keys, queries)
        top = jnp.max(scores, axis=0, keepdims=True)
        probs = jnp.exp(scores - top)
        total = jnp.sum(probs, axis=0, keepdims=True)
        out_ref[block] = product(coarse_turned[HEAD_SIZE:], probs.astype(BF16))
        stats_ref[block] = jnp.concatenate([top, total, jnp.zeros((6, QUERY_BLOCK), F32)], axis=0)

    def one_block(block, _):
        queries = queries_held[block]
        steps = steps_ref[block ^ (place_ref[1] >> 1)]
        last = steps - 1
        scores_held[0] = product(rows_of(masked_keys, 0), queries)

        def one_step(step, carried):
            top, total, accum = carried
            slot = step & 1
            scores = scores_held[slot]
            scores_held[1 - slot] = product(rows_of(masked_keys, jnp.minimum(step + 1, last)), queries)
            new_top = jnp.maximum(top, jnp.max(scores, axis=0, keepdims=True))
            fade = jnp.exp(top - new_top)
            probs = jnp.exp(scores - new_top)
            total = total * fade + jnp.sum(probs, axis=0, keepdims=True)
            accum = accum * fade + product(turned_of(turned, step, HEAD_SIZE), probs.astype(BF16))
            return new_top, total, accum

        start = stats_ref[block]
        top, total, accum = lax.fori_loop(
            0, steps, one_step, (start[0:1], start[1:2], out_ref[block])
        )
        back = query_pieces(query_held, block)[HEAD_SIZE:]
        offset = jnp.sum(back.astype(F32) * accum, axis=0, keepdims=True)
        out_ref[block] = accum
        stats_ref[block] = jnp.concatenate(
            [top, total, offset, jnp.zeros((5, QUERY_BLOCK), F32)], axis=0
        )
        return 0

    lax.fori_loop(0, QUERY_BLOCKS, one_block, 0)
    for pair in range(2):
        packed_ref[pair] = jnp.concatenate([stats_ref[2 * pair, :4, :], stats_ref[2 * pair + 1, :4, :]], axis=0)


def backward_kernel(
    place_ref, steps_ref, masked_keys, plain, turned, query_held, kvc_ref, ids_ref, accum_ref,
    stats0, stats1, stats2, stats3, od0, od1, od2, od3, dkv0, dkv1, dkv2, dkv3,
    out_held, key_sums, coarse_sums, stats_held,
):
    for partner, ref in enumerate((stats0, stats1, stats2, stats3)):
        for block in range(QUERY_BLOCKS):
            rows = slice(4 * (block % 2), 4 * (block % 2) + 4)
            stats_held[4 * partner + block, :4, :] = ref[block // 2, rows, :]
    coarse_both, coarse_keys, coarse_turned = coarse_side(kvc_ref)
    key_sums[...] = jnp.zeros_like(key_sums)
    coarse_sums[...] = jnp.zeros_like(coarse_sums)

    def one_block(block, _):
        both, queries = query_side(place_ref, query_held, ids_ref, block)
        own = stats_held[block]
        stats = [own]
        for partner in (1, 2, 3):
            theirs = stats_held[4 * partner + (block ^ (partner // 2))]
            flip = 2 * (partner % 2)
            parts = [theirs[:, (part ^ flip) * PIECE:((part ^ flip) + 1) * PIECE] for part in range(4)]
            stats.append(jnp.concatenate(parts, axis=1))
        top = stats[0][0:1]
        for other in stats[1:]:
            top = jnp.maximum(top, other[0:1])
        total = jnp.zeros_like(top)
        offset = jnp.zeros_like(top)
        for other in stats:
            fade = jnp.exp(other[0:1] - top)
            total = total + fade * other[1:2]
            offset = offset + fade * other[2:3]
        offset = offset / total
        log_total = top + jnp.log(total)
        attended = accum_ref[block] * (jnp.exp(own[0:1] - top) / total)
        back = jnp.concatenate(
            [jnp.zeros((HEAD_SIZE, QUERY_BLOCK), BF16), both[HEAD_SIZE:]], axis=0
        )
        token_rows = both.astype(F32).T
        lane = lax.broadcasted_iota(jnp.int32, token_rows.shape, 1)
        query_rows = jnp.where(lane < HEAD_SIZE, token_rows, 0.0).astype(BF16)
        back_rows = jnp.where(lane < HEAD_SIZE, 0.0, token_rows).astype(BF16)

        def terms(only_keys, key_value, key_turned):
            probs = jnp.exp(product(only_keys, queries) - log_total)
            grad_probs = product(key_value, back)
            grad_scores = (probs * (grad_probs - offset)).astype(BF16)
            key_side = product(grad_scores, query_rows) + product(probs.astype(BF16), back_rows)
            return product(key_turned, grad_scores), key_side

        query_grad, coarse_term = terms(coarse_keys, coarse_both, coarse_turned[:HEAD_SIZE])
        coarse_sums[...] += coarse_term

        def one_step(step, query_grad):
            query_term, key_side = terms(
                rows_of(masked_keys, step, 4), rows_of(plain, step, 4), turned_of(turned, step, 0, 4)
            )
            key_sums[pl.ds(4 * step, 4)] += key_side.reshape(4, PIECE, PIECE)
            return query_grad + query_term

        steps = lax.div(steps_ref[block ^ (place_ref[1] >> 1)] + 1, 2)
        query_grad = lax.fori_loop(0, steps, one_step, query_grad)
        both_out = jnp.concatenate([attended, query_grad * SCALE], axis=0).astype(BF16)
        for part in range(4):
            out_held[4 * block + part] = both_out[:, part * PIECE:(part + 1) * PIECE]
        return 0

    lax.fori_loop(0, QUERY_BLOCKS, one_block, 0)
    for part, ref in enumerate((od0, od1, od2, od3)):
        for source in range(4):
            ref[source] = out_held[8 * (source // 2) + 2 * part + source % 2]
    coarse = coarse_sums[...].astype(BF16)
    for partner, ref in enumerate((dkv0, dkv1, dkv2, dkv3)):
        for source in range(4):
            piece = key_sums[key_piece(place_ref, source, partner)]
            ref[source * PIECE:(source + 1) * PIECE, :] = piece.astype(BF16)
        ref[4 * PIECE:, :] = coarse


def coarse_probs(query, key, bias):
    scores = product_nt(key, query) + bias
    top = jnp.max(scores, axis=0, keepdims=True)
    total = jnp.sum(jnp.exp(scores - top), axis=0, keepdims=True)
    return jnp.exp(scores - (top + jnp.log(total)))


def head_columns(ref, head):
    return ref[:, head * HEAD_SIZE:(head + 1) * HEAD_SIZE]


def packet_kernel(place_ref, query_ref, key_ref, value_ref, bias_ref, weight_ref, grad_ref, *refs):
    outs, held = refs[:4], refs[4]
    for part in range(4):
        held[part] = weight_ref[:, part * 480:(part + 1) * 480].astype(F32).T.astype(BF16)
    attended = []
    for head in range(4):
        query = (head_columns(query_ref, head).astype(F32) * SCALE).astype(BF16)
        probs = coarse_probs(query, head_columns(key_ref, head), bias_ref[...])
        attended.append(product_tn(head_columns(value_ref, head), probs.astype(BF16)).astype(BF16))
    attended = jnp.concatenate(attended, axis=0)
    for partner in range(4):
        outs[partner][:480, :] = held[place_ref[2] ^ partner]
        outs[partner][480:960, :] = grad_ref[...]
        outs[partner][960:, :] = attended


def coarse_kernel(query_ref, key_ref, value_ref, bias_ref, *refs):
    packets, weights, (mixed_ref, dq_ref, dk_ref, dv_ref) = refs[:4], refs[4:8], refs[8:]
    back_all = sum(
        product(weight[...], packet[480:960, :]) for weight, packet in zip(weights, packets)
    ).astype(BF16)
    mixed_ref[...] = sum(product(packet[:480, :], packet[960:, :]) for packet in packets).astype(BF16)
    query_grads, key_grads, value_grads = [], [], []
    for head in range(4):
        part = slice(head * HEAD_SIZE, (head + 1) * HEAD_SIZE)
        query = (query_ref[:, part].astype(F32) * SCALE).astype(BF16)
        key, value, back = key_ref[:, part], value_ref[:, part], back_all[part]
        probs = coarse_probs(query, key, bias_ref[...])
        rounded = probs.astype(BF16)
        attended = packets[0][960 + part.start:960 + part.stop, :]
        offset = jnp.sum(back.astype(F32) * attended.astype(F32), axis=0, keepdims=True)
        grad_scores = (probs * (product(value, back) - offset)).astype(BF16)
        query_grads.append(product_tn(key, grad_scores) * SCALE)
        key_grads.append(product(grad_scores, query))
        value_grads.append(product_nt(rounded, back))
    dq_ref[...] = jnp.concatenate(query_grads, axis=0).T.astype(BF16)
    dk_ref[...] = jnp.concatenate(key_grads, axis=1)
    dv_ref[...] = jnp.concatenate(value_grads, axis=1)


def attended_kernel(*refs):
    parts, out_ref = refs[:4], refs[4]
    for source in range(4):
        total = sum(part[source, :HEAD_SIZE, :].astype(F32) for part in parts)
        out_ref[source] = total.astype(BF16)


def sums_kernel(place_ref, *refs):
    attended, od, dkv, outs, held = refs[:4], refs[4:8], refs[8:12], refs[12:16], refs[16]
    for source in range(4):
        rows = slice(source * PIECE, (source + 1) * PIECE)
        for part in range(4):
            held[source, part * HEAD_SIZE:(part + 1) * HEAD_SIZE] = attended[part][source]
        held[source, 256:320] = sum(part[source, HEAD_SIZE:, :].astype(F32) for part in od).astype(BF16)
        held[source, 320:] = sum(part[rows, :].astype(F32) for part in dkv).astype(BF16)
    coarse = sum(part[4 * PIECE:, :].astype(F32) for part in dkv).astype(BF16)
    for partner in range(4):
        outs[partner][:448, :] = held[place_ref[0] ^ partner]
        outs[partner][448:, :] = coarse


def heads_kernel(place_ref, *refs):
    parts, (att_ref, dq_ref, dk_ref, dv_ref, coarse_ref, query_held, key_held) = refs[:4], refs[4:]
    for partner, part in enumerate(parts):
        head = place_ref[0] ^ partner
        rows = pl.ds(pl.multiple_of(head * HEAD_SIZE, HEAD_SIZE), HEAD_SIZE)
        for group in range(4):
            att_ref[group, rows, :] = part[group * HEAD_SIZE:(group + 1) * HEAD_SIZE, :]
        query_held[rows, :] = part[256:320, :].astype(F32)
        key_held[head] = part[320:448, :]
        coarse_ref[head] = part[448:, :]
    dq_ref[...] = query_held[...].T.astype(BF16)
    dk_ref[...] = jnp.concatenate([key_held[head, :, :HEAD_SIZE] for head in range(4)], axis=1)
    dv_ref[...] = jnp.concatenate([key_held[head, :, HEAD_SIZE:] for head in range(4)], axis=1)


def mix_kernel(att_ref, *refs):
    packets, mixed_ref = refs[:4], refs[4]
    mixed_ref[...] = sum(
        product(packet[:480, :], att_ref[group]) for group, packet in enumerate(packets)
    ).astype(BF16)


def last_kernel(place_ref, *refs):
    received, (dk_ref, dv_ref, dk_out, dv_out) = refs[:4], refs[4:]
    for partner, ref in enumerate(received):
        rows = pl.ds(pl.multiple_of((place_ref[1] ^ partner) * 64, 64), 64)
        parts = [ref[head].astype(F32) for head in range(4)]
        keys = jnp.concatenate([part[:, :HEAD_SIZE] for part in parts], axis=1)
        values = jnp.concatenate([part[:, HEAD_SIZE:] for part in parts], axis=1)
        dk_out[rows, :] = (dk_ref[rows, :] + keys).astype(BF16)
        dv_out[rows, :] = (dv_ref[rows, :] + values).astype(BF16)


def swap(arrays, axes):
    out = [arrays[0]]
    sent = {
        partner: lax.ppermute(arrays[partner], axes, [(i, i ^ partner) for i in range(4)])
        for partner in (1, 3, 2)
    }
    return out + [sent[1], sent[2], sent[3]]


def on_device(
    query_fine, key_fine, value_fine, query_coarse, key_coarse, value_coarse,
    out_weight, grad_fine, grad_coarse, fine_scale, coarse_scale,
):
    place = {name: lax.axis_index(name) for name in SEQ}
    head_of = place["xh"] * 2 + place["za"]
    tile_of = place["yh"] * 2 + place["yl"]
    placed = jnp.stack(
        [head_of, tile_of, lax.axis_index("head"), place["zc"] * 2 + place["zb"]]
    ).astype(jnp.int32)

    grads = swap([grad_fine.T] * 4, "head")
    weights = call(
        weight_blocks_kernel, (shape(256, 480),) * 4, [pltpu.VMEM((4, 256, 480), BF16)], 1, moved=2**21
    )(placed, out_weight)
    packed = call(
        pack_kernel, (shape(2 * PIECE, PIECE),) * 4, [pltpu.VMEM((4, 2 * PIECE, PIECE), BF16)], 1,
        flops=2 * 128 * 256 * 1920, moved=2**21,
    )(placed, query_fine, key_fine, value_fine, *grads, *weights)
    own_qb, own_kv = call(own_head_kernel, (shape(4, PIECE, PIECE),) * 2, (), 1, moved=2**19)(
        placed, *swap(packed, HEADS)
    )
    kv = swap([own_kv] * 4, QUERY_TILES)
    qb = swap([own_qb] * 4, KEY_TILES)

    ids = fine_scale.reshape(2, 2, 2, 2, 2, 2, PIECE)
    query_ids = lax.dynamic_index_in_dim(ids, place["zc"], 3, keepdims=False)
    query_ids = lax.dynamic_index_in_dim(query_ids, place["zb"], 3, keepdims=False)
    query_ids = query_ids.reshape(PIECES, 1, PIECE)
    key_ids = lax.dynamic_index_in_dim(ids, place["yh"], 1, keepdims=False)
    key_ids = lax.dynamic_index_in_dim(key_ids, place["yl"], 1, keepdims=False)
    key_ids = key_ids.reshape(PIECES, PIECE)
    lane = lax.broadcasted_iota(jnp.int32, (PIECES, PIECE, PIECE), 2)
    onehot = (lane - HEAD_SIZE == key_ids[:, :, None]).astype(BF16)
    seen = jnp.sum(key_ids[None, :, 0] <= query_ids[3::4, 0, -1:], axis=1)
    steps = ((seen + STEP - 1) // STEP).astype(jnp.int32)

    coarse_rows = [
        lax.dynamic_slice(array, (tile_of * 64, 0), (64, 256)).reshape(64, 4, HEAD_SIZE)
        for array in (key_coarse, value_coarse)
    ]
    kvc = jnp.concatenate(
        [lax.dynamic_index_in_dim(rows, head_of, 1, keepdims=False) for rows in coarse_rows], axis=1
    )

    bias = jnp.where(coarse_scale[:, None] <= coarse_scale[None, :], 0.0, -1e9).astype(F32)
    packed = call(
        packet_kernel, (shape(1216, 256),) * 4, [pltpu.VMEM((4, 480, 256), BF16)], 1,
        flops=2**28, moved=2**22, exps=2**18,
    )(placed, query_coarse, key_coarse, value_coarse, bias, out_weight, grad_coarse.T)
    kv, qb, packed, onehot, kvc, steps, query_ids = lax.optimization_barrier(
        (kv, qb, packed, onehot, kvc, steps, query_ids)
    )

    half = [pltpu.VMEM((PIECES, PIECE, PIECE), BF16)]
    accum, stats, *prepared = call(
        forward_kernel,
        (shape(QUERY_BLOCKS, HEAD_SIZE, QUERY_BLOCK, dtype=F32), shape(2, 8, QUERY_BLOCK, dtype=F32))
        + (shape(PIECES, PIECE, PIECE),) * 4,
        [
            pltpu.VMEM((QUERY_BLOCKS, PIECE, QUERY_BLOCK), BF16),
            pltpu.VMEM((2, STEP * PIECE, QUERY_BLOCK), F32),
            pltpu.VMEM((QUERY_BLOCKS, 8, QUERY_BLOCK), F32),
        ],
        2,
    )(placed, steps, *kv, onehot, kvc, *qb, query_ids)
    packets = swap(packed, "head")
    stats, packets[1] = lax.optimization_barrier((stats, packets[1]))
    all_stats = swap([stats] * 4, KEY_TILES)
    parts = call(
        backward_kernel,
        (shape(4, PIECE, PIECE),) * 4 + (shape(4 * PIECE + 64, PIECE),) * 4,
        half
        + [
            pltpu.VMEM((PIECES, PIECE, PIECE), F32),
            pltpu.VMEM((64, PIECE), F32),
            pltpu.VMEM((4 * QUERY_BLOCKS, 8, QUERY_BLOCK), F32),
        ],
        2, 10 * 2048 * 2112 * 64, 2**22, 2048 * 2112,
    )(placed, steps, *prepared, kvc, query_ids, accum, *all_stats)

    parts, packets = lax.optimization_barrier((parts, packets))
    dkv = swap(parts[4:], QUERY_TILES)
    od = swap(parts[:4], KEY_TILES)
    attended = call(attended_kernel, shape(4, HEAD_SIZE, PIECE), moved=2**20)(*od)
    attended = swap([attended] * 4, "head")
    mixed_coarse, dq_coarse, dk_coarse, dv_coarse = call(
        coarse_kernel,
        (shape(480, 256), shape(256, 256), shape(256, 256, dtype=F32), shape(256, 256, dtype=F32)),
        flops=2**29, moved=2**22, exps=2**19,
    )(query_coarse, key_coarse, value_coarse, bias, *packets, *weights)
    dkv, dk_coarse = lax.optimization_barrier((dkv, dk_coarse))
    sums = call(
        sums_kernel, (shape(512, PIECE),) * 4, [pltpu.VMEM((4, 448, PIECE), BF16)], 1, moved=2**21
    )(placed, *attended, *od, *dkv)
    attended, dq_fine, dk_fine, dv_fine, coarse_part = call(
        heads_kernel,
        (shape(4, 256, PIECE),) + (shape(PIECE, 256),) * 3 + (shape(4, 64, PIECE),),
        [pltpu.VMEM((256, PIECE), F32), pltpu.VMEM((4, PIECE, PIECE), BF16)], 1, moved=2**20,
    )(placed, *swap(sums, HEADS))
    coarse_parts = swap([coarse_part] * 4, KEY_TILES)
    mixed_fine = call(mix_kernel, shape(480, PIECE), flops=2**27, moved=2**20)(attended, *packets)
    coarse_parts, mixed_fine = lax.optimization_barrier((coarse_parts, mixed_fine))
    dk_coarse, dv_coarse = call(
        last_kernel, (shape(256, 256), shape(256, 256)), (), 1, moved=2**20
    )(placed, *coarse_parts, dk_coarse, dv_coarse)
    return (
        mixed_fine.T, mixed_coarse.T, dq_fine, dk_fine, dv_fine, dq_coarse, dk_coarse, dv_coarse,
    )


def solution(mesh):
    fine_mesh = Mesh(mesh.devices.reshape(2, 2, 2, 2, 2, 2, 4), SEQ + ("head",))
    in_specs = (
        P(SEQ, "head"), P(SEQ, "head"), P(SEQ, "head"),
        P(None, "head"), P(None, "head"), P(None, "head"),
        P("head", None), P(SEQ, "head"), P(None, "head"), P(), P(),
    )
    out_specs = (
        P(SEQ, "head"), P(None, "head"),
        P(SEQ, "head"), P(SEQ, "head"), P(SEQ, "head"),
        P(None, "head"), P(None, "head"), P(None, "head"),
    )
    return jax.shard_map(
        on_device, mesh=fine_mesh, in_specs=in_specs, out_specs=out_specs, check_vma=False
    )
```

```python
import jax
import jax.numpy as jnp
from jax import lax
from jax.experimental import pallas as pl
from jax.experimental.pallas import tpu as pltpu
from jax.sharding import Mesh
from jax.sharding import PartitionSpec as P

HEAD_SIZE = 64
SCALE = HEAD_SIZE ** (-0.5)
FSCALES = 3
HIDE = -30000.0
PIECE = 128
PIECES = 16
QUERY_BLOCKS = 4
QUERY_BLOCK = 512
STEP = 2
F32 = jnp.float32
BF16 = jnp.bfloat16

SEQ = ("xh", "yh", "yl", "zc", "zb", "za")
HEADS = ("xh", "za")
QUERY_TILES = ("zc", "zb")
KEY_TILES = ("yh", "yl")


def product(left, right):
    return jnp.dot(left, right, preferred_element_type=F32)


def product_nt(left, right):
    return lax.dot_general(left, right, (((1,), (1,)), ((), ())), preferred_element_type=F32)


def product_tn(left, right):
    return lax.dot_general(left, right, (((0,), (0,)), ((), ())), preferred_element_type=F32)


def call(kernel, outs, scratch=(), smem=0, flops=0, moved=0, exps=0):
    def run(*operands):
        return pl.pallas_call(
            kernel,
            out_shape=outs,
            in_specs=[pl.BlockSpec(memory_space=pltpu.SMEM)] * smem
            + [pl.BlockSpec(memory_space=pltpu.VMEM)] * (len(operands) - smem),
            out_specs=jax.tree.map(lambda _: pl.BlockSpec(memory_space=pltpu.VMEM), outs),
            scratch_shapes=list(scratch),
            compiler_params=pltpu.CompilerParams(vmem_limit_bytes=48 * 2**20),
            cost_estimate=pl.CostEstimate(
                flops=flops, bytes_accessed=moved, transcendentals=exps
            ),
        )(*operands)

    return run


def shape(*dims, dtype=BF16):
    return jax.ShapeDtypeStruct(dims, dtype)


def weight_blocks_kernel(place_ref, weight_ref, *refs):
    outs, held = refs[:4], refs[4]
    for part in range(4):
        held[part] = weight_ref[:, part * 480:(part + 1) * 480]
    for partner in range(4):
        outs[partner][...] = held[place_ref[2] ^ partner]


def pack_kernel(place_ref, query_ref, key_ref, value_ref, *refs):
    grads, weights, outs, held = refs[:4], refs[4:8], refs[8:12], refs[12]
    back = sum(product(weight[...], grad[...]) for weight, grad in zip(weights, grads)).astype(BF16)
    query = (query_ref[...].astype(F32) * SCALE).T.astype(BF16)
    for head in range(4):
        part = slice(head * HEAD_SIZE, (head + 1) * HEAD_SIZE)
        held[head, :HEAD_SIZE] = query[part]
        held[head, HEAD_SIZE:PIECE] = back[part]
        held[head, PIECE:] = jnp.concatenate([key_ref[:, part], value_ref[:, part]], axis=1)
    for partner in range(4):
        outs[partner][...] = held[place_ref[0] ^ partner]


def own_head_kernel(place_ref, *refs):
    parts, (qb_ref, kv_ref) = refs[:4], refs[4:]
    for partner, part in enumerate(parts):
        source = place_ref[0] ^ partner
        qb_ref[source] = part[:PIECE, :]
        kv_ref[source] = part[PIECE:, :]


def key_piece(place_ref, source, partner):
    return 8 * (source // 2) + 2 * (place_ref[3] ^ partner) + source % 2


def prepare_queries(qb_refs, held):
    for part, ref in enumerate(qb_refs):
        for source in range(4):
            held[8 * (source // 2) + 2 * part + source % 2] = ref[source]


def prepare_keys(place_ref, kv_refs, onehot_ref, masked_keys, plain, turned):
    lane = lax.broadcasted_iota(jnp.int32, (PIECE, PIECE), 1)
    for partner, ref in enumerate(kv_refs):
        for source in range(4):
            piece = key_piece(place_ref, source, partner)
            both = ref[source]
            masked_keys[piece] = jnp.where(lane < HEAD_SIZE, both, onehot_ref[piece])
            turned[piece] = both.astype(F32).T.astype(BF16)
            plain[piece] = both


def query_pieces(held, block):
    return jnp.concatenate([held[4 * block + part] for part in range(4)], axis=1)


def query_side(place_ref, held, ids_ref, block):
    both = query_pieces(held, block)
    own = 8 * (block // 2) if isinstance(block, int) else 8 * (block >> 1)
    first = own + 4 * ((place_ref[1] >> 1) ^ (block & 1))
    ids = jnp.concatenate(
        [ids_ref[first + 2 * ((place_ref[1] & 1) ^ (part // 2)) + part % 2] for part in range(4)], axis=1
    )
    row = lax.broadcasted_iota(jnp.int32, (HEAD_SIZE, QUERY_BLOCK), 0)
    hidden = (row > ids) & (row < FSCALES)
    penalty = jnp.where(hidden, HIDE, 0.0).astype(BF16)
    return both, jnp.concatenate([both[:HEAD_SIZE], penalty], axis=0)


def rows_of(ref, step, size=STEP):
    return ref[pl.ds(size * step, size)].reshape(size * PIECE, PIECE)


def turned_of(ref, step, first, size=STEP):
    return jnp.concatenate(
        [ref[size * step + part, first:first + HEAD_SIZE, :] for part in range(size)], axis=1
    )


def coarse_side(kvc_ref):
    both = kvc_ref[...]
    lane = lax.broadcasted_iota(jnp.int32, both.shape, 1)
    only_keys = jnp.where(lane < HEAD_SIZE, both, jnp.zeros_like(both))
    return both, only_keys, both.astype(F32).T.astype(BF16)


def forward_kernel(
    place_ref, steps_ref, kv0, kv1, kv2, kv3, onehot_ref, kvc_ref, qb0, qb1, qb2, qb3, ids_ref,
    out_ref, packed_ref, masked_keys, plain, turned, query_held, queries_held, scores_held, stats_ref,
):
    prepare_keys(place_ref, (kv0, kv1, kv2, kv3), onehot_ref, masked_keys, plain, turned)
    prepare_queries((qb0, qb1, qb2, qb3), query_held)
    _, coarse_keys, coarse_turned = coarse_side(kvc_ref)
    for block in range(QUERY_BLOCKS):
        _, queries = query_side(place_ref, query_held, ids_ref, block)
        queries_held[block] = queries
        scores = product(coarse_keys, queries)
        top = jnp.max(scores, axis=0, keepdims=True)
        probs = jnp.exp(scores - top)
        total = jnp.sum(probs, axis=0, keepdims=True)
        out_ref[block] = product(coarse_turned[HEAD_SIZE:], probs.astype(BF16))
        stats_ref[block] = jnp.concatenate([top, total, jnp.zeros((6, QUERY_BLOCK), F32)], axis=0)

    def one_block(block, _):
        queries = queries_held[block]
        steps = steps_ref[block ^ (place_ref[1] >> 1)]
        last = steps - 1
        scores_held[0] = product(rows_of(masked_keys, 0), queries)

        def one_step(step, carried):
            top, total, accum = carried
            slot = step & 1
            scores = scores_held[slot]
            scores_held[1 - slot] = product(rows_of(masked_keys, jnp.minimum(step + 1, last)), queries)
            new_top = jnp.maximum(top, jnp.max(scores, axis=0, keepdims=True))
            fade = jnp.exp(top - new_top)
            probs = jnp.exp(scores - new_top)
            total = total * fade + jnp.sum(probs, axis=0, keepdims=True)
            accum = accum * fade + product(turned_of(turned, step, HEAD_SIZE), probs.astype(BF16))
            return new_top, total, accum

        start = stats_ref[block]
        top, total, accum = lax.fori_loop(
            0, steps, one_step, (start[0:1], start[1:2], out_ref[block])
        )
        back = query_pieces(query_held, block)[HEAD_SIZE:]
        offset = jnp.sum(back.astype(F32) * accum, axis=0, keepdims=True)
        out_ref[block] = accum
        stats_ref[block] = jnp.concatenate(
            [top, total, offset, jnp.zeros((5, QUERY_BLOCK), F32)], axis=0
        )
        return 0

    lax.fori_loop(0, QUERY_BLOCKS, one_block, 0)
    for pair in range(2):
        packed_ref[pair] = jnp.concatenate([stats_ref[2 * pair, :4, :], stats_ref[2 * pair + 1, :4, :]], axis=0)


def backward_kernel(
    place_ref, steps_ref, masked_keys, plain, turned, query_held, kvc_ref, ids_ref, accum_ref,
    stats0, stats1, stats2, stats3, od0, od1, od2, od3, dkv0, dkv1, dkv2, dkv3,
    out_held, key_sums, coarse_sums, stats_held,
):
    for partner, ref in enumerate((stats0, stats1, stats2, stats3)):
        for block in range(QUERY_BLOCKS):
            rows = slice(4 * (block % 2), 4 * (block % 2) + 4)
            stats_held[4 * partner + block, :4, :] = ref[block // 2, rows, :]
    coarse_both, coarse_keys, coarse_turned = coarse_side(kvc_ref)
    key_sums[...] = jnp.zeros_like(key_sums)
    coarse_sums[...] = jnp.zeros_like(coarse_sums)

    def one_block(block, _):
        both, queries = query_side(place_ref, query_held, ids_ref, block)
        own = stats_held[block]
        stats = [own]
        for partner in (1, 2, 3):
            theirs = stats_held[4 * partner + (block ^ (partner // 2))]
            flip = 2 * (partner % 2)
            parts = [theirs[:, (part ^ flip) * PIECE:((part ^ flip) + 1) * PIECE] for part in range(4)]
            stats.append(jnp.concatenate(parts, axis=1))
        top = stats[0][0:1]
        for other in stats[1:]:
            top = jnp.maximum(top, other[0:1])
        total = jnp.zeros_like(top)
        offset = jnp.zeros_like(top)
        for other in stats:
            fade = jnp.exp(other[0:1] - top)
            total = total + fade * other[1:2]
            offset = offset + fade * other[2:3]
        offset = offset / total
        log_total = top + jnp.log(total)
        attended = accum_ref[block] * (jnp.exp(own[0:1] - top) / total)
        back = jnp.concatenate(
            [jnp.zeros((HEAD_SIZE, QUERY_BLOCK), BF16), both[HEAD_SIZE:]], axis=0
        )
        token_rows = both.astype(F32).T
        lane = lax.broadcasted_iota(jnp.int32, token_rows.shape, 1)
        query_rows = jnp.where(lane < HEAD_SIZE, token_rows, 0.0).astype(BF16)
        back_rows = jnp.where(lane < HEAD_SIZE, 0.0, token_rows).astype(BF16)

        def terms(only_keys, key_value, key_turned):
            probs = jnp.exp(product(only_keys, queries) - log_total)
            grad_probs = product(key_value, back)
            grad_scores = (probs * (grad_probs - offset)).astype(BF16)
            key_side = product(grad_scores, query_rows) + product(probs.astype(BF16), back_rows)
            return product(key_turned, grad_scores), key_side

        query_grad, coarse_term = terms(coarse_keys, coarse_both, coarse_turned[:HEAD_SIZE])
        coarse_sums[...] += coarse_term

        def one_step(step, query_grad):
            query_term, key_side = terms(
                rows_of(masked_keys, step, 4), rows_of(plain, step, 4), turned_of(turned, step, 0, 4)
            )
            key_sums[pl.ds(4 * step, 4)] += key_side.reshape(4, PIECE, PIECE)
            return query_grad + query_term

        steps = lax.div(steps_ref[block ^ (place_ref[1] >> 1)] + 1, 2)
        query_grad = lax.fori_loop(0, steps, one_step, query_grad)
        both_out = jnp.concatenate([attended, query_grad * SCALE], axis=0).astype(BF16)
        for part in range(4):
            out_held[4 * block + part] = both_out[:, part * PIECE:(part + 1) * PIECE]
        return 0

    lax.fori_loop(0, QUERY_BLOCKS, one_block, 0)
    for part, ref in enumerate((od0, od1, od2, od3)):
        for source in range(4):
            ref[source] = out_held[8 * (source // 2) + 2 * part + source % 2]
    coarse = coarse_sums[...].astype(BF16)
    for partner, ref in enumerate((dkv0, dkv1, dkv2, dkv3)):
        for source in range(4):
            piece = key_sums[key_piece(place_ref, source, partner)]
            ref[source * PIECE:(source + 1) * PIECE, :] = piece.astype(BF16)
        ref[4 * PIECE:, :] = coarse


def coarse_probs(query, key, bias):
    scores = product_nt(key, query) + bias
    top = jnp.max(scores, axis=0, keepdims=True)
    total = jnp.sum(jnp.exp(scores - top), axis=0, keepdims=True)
    return jnp.exp(scores - (top + jnp.log(total)))


def head_columns(ref, head):
    return ref[:, head * HEAD_SIZE:(head + 1) * HEAD_SIZE]


def packet_kernel(place_ref, query_ref, key_ref, value_ref, bias_ref, weight_ref, grad_ref, *refs):
    outs, held = refs[:4], refs[4]
    for part in range(4):
        held[part] = weight_ref[:, part * 480:(part + 1) * 480].astype(F32).T.astype(BF16)
    attended = []
    for head in range(4):
        query = (head_columns(query_ref, head).astype(F32) * SCALE).astype(BF16)
        probs = coarse_probs(query, head_columns(key_ref, head), bias_ref[...])
        attended.append(product_tn(head_columns(value_ref, head), probs.astype(BF16)).astype(BF16))
    attended = jnp.concatenate(attended, axis=0)
    for partner in range(4):
        outs[partner][:480, :] = held[place_ref[2] ^ partner]
        outs[partner][480:960, :] = grad_ref[...]
        outs[partner][960:, :] = attended


def coarse_kernel(query_ref, key_ref, value_ref, bias_ref, *refs):
    packets, weights, (mixed_ref, dq_ref, dk_ref, dv_ref) = refs[:4], refs[4:8], refs[8:]
    back_all = sum(
        product(weight[...], packet[480:960, :]) for weight, packet in zip(weights, packets)
    ).astype(BF16)
    mixed_ref[...] = sum(product(packet[:480, :], packet[960:, :]) for packet in packets).astype(BF16)
    query_grads, key_grads, value_grads = [], [], []
    for head in range(4):
        part = slice(head * HEAD_SIZE, (head + 1) * HEAD_SIZE)
        query = (query_ref[:, part].astype(F32) * SCALE).astype(BF16)
        key, value, back = key_ref[:, part], value_ref[:, part], back_all[part]
        probs = coarse_probs(query, key, bias_ref[...])
        rounded = probs.astype(BF16)
        attended = packets[0][960 + part.start:960 + part.stop, :]
        offset = jnp.sum(back.astype(F32) * attended.astype(F32), axis=0, keepdims=True)
        grad_scores = (probs * (product(value, back) - offset)).astype(BF16)
        query_grads.append(product_tn(key, grad_scores) * SCALE)
        key_grads.append(product(grad_scores, query))
        value_grads.append(product_nt(rounded, back))
    dq_ref[...] = jnp.concatenate(query_grads, axis=0).T.astype(BF16)
    dk_ref[...] = jnp.concatenate(key_grads, axis=1)
    dv_ref[...] = jnp.concatenate(value_grads, axis=1)


def attended_kernel(*refs):
    parts, out_ref = refs[:4], refs[4]
    for source in range(4):
        total = sum(part[source, :HEAD_SIZE, :].astype(F32) for part in parts)
        out_ref[source] = total.astype(BF16)


def key_sums_kernel(*refs):
    refs[4][...] = sum(part[...].astype(F32) for part in refs[:4]).astype(BF16)


def sums_kernel(place_ref, *refs):
    attended, od, dkv, outs, held = refs[:4], refs[4:8], refs[8], refs[9:13], refs[13]
    for source in range(4):
        rows = slice(source * PIECE, (source + 1) * PIECE)
        for part in range(4):
            held[source, part * HEAD_SIZE:(part + 1) * HEAD_SIZE] = attended[part][source]
        held[source, 256:320] = sum(part[source, HEAD_SIZE:, :].astype(F32) for part in od).astype(BF16)
        held[source, 320:] = dkv[rows, :]
    coarse = dkv[4 * PIECE:, :]
    for partner in range(4):
        outs[partner][:448, :] = held[place_ref[0] ^ partner]
        outs[partner][448:, :] = coarse


def heads_kernel(place_ref, *refs):
    parts, (att_ref, dq_ref, dk_ref, dv_ref, coarse_ref, query_held, key_held) = refs[:4], refs[4:]
    for partner, part in enumerate(parts):
        head = place_ref[0] ^ partner
        rows = pl.ds(pl.multiple_of(head * HEAD_SIZE, HEAD_SIZE), HEAD_SIZE)
        for group in range(4):
            att_ref[group, rows, :] = part[group * HEAD_SIZE:(group + 1) * HEAD_SIZE, :]
        query_held[rows, :] = part[256:320, :].astype(F32)
        key_held[head] = part[320:448, :]
        coarse_ref[head] = part[448:, :]
    dq_ref[...] = query_held[...].T.astype(BF16)
    dk_ref[...] = jnp.concatenate([key_held[head, :, :HEAD_SIZE] for head in range(4)], axis=1)
    dv_ref[...] = jnp.concatenate([key_held[head, :, HEAD_SIZE:] for head in range(4)], axis=1)


def mix_kernel(att_ref, *refs):
    packets, mixed_ref = refs[:4], refs[4]
    mixed_ref[...] = sum(
        product(packet[:480, :], att_ref[group]) for group, packet in enumerate(packets)
    ).astype(BF16)


def last_kernel(place_ref, *refs):
    received, (dk_ref, dv_ref, dk_out, dv_out) = refs[:4], refs[4:]
    for partner, ref in enumerate(received):
        rows = pl.ds(pl.multiple_of((place_ref[1] ^ partner) * 64, 64), 64)
        parts = [ref[head].astype(F32) for head in range(4)]
        keys = jnp.concatenate([part[:, :HEAD_SIZE] for part in parts], axis=1)
        values = jnp.concatenate([part[:, HEAD_SIZE:] for part in parts], axis=1)
        dk_out[rows, :] = (dk_ref[rows, :] + keys).astype(BF16)
        dv_out[rows, :] = (dv_ref[rows, :] + values).astype(BF16)


def swap(arrays, axes):
    out = [arrays[0]]
    sent = {
        partner: lax.ppermute(arrays[partner], axes, [(i, i ^ partner) for i in range(4)])
        for partner in (1, 3, 2)
    }
    return out + [sent[1], sent[2], sent[3]]


def on_device(
    query_fine, key_fine, value_fine, query_coarse, key_coarse, value_coarse,
    out_weight, grad_fine, grad_coarse, fine_scale, coarse_scale,
):
    place = {name: lax.axis_index(name) for name in SEQ}
    head_of = place["xh"] * 2 + place["za"]
    tile_of = place["yh"] * 2 + place["yl"]
    placed = jnp.stack(
        [head_of, tile_of, lax.axis_index("head"), place["zc"] * 2 + place["zb"]]
    ).astype(jnp.int32)

    grads = swap([grad_fine.T] * 4, "head")
    weights = call(
        weight_blocks_kernel, (shape(256, 480),) * 4, [pltpu.VMEM((4, 256, 480), BF16)], 1, moved=2**21
    )(placed, out_weight)
    packed = call(
        pack_kernel, (shape(2 * PIECE, PIECE),) * 4, [pltpu.VMEM((4, 2 * PIECE, PIECE), BF16)], 1,
        flops=2 * 128 * 256 * 1920, moved=2**21,
    )(placed, query_fine, key_fine, value_fine, *grads, *weights)
    own_qb, own_kv = call(own_head_kernel, (shape(4, PIECE, PIECE),) * 2, (), 1, moved=2**19)(
        placed, *swap(packed, HEADS)
    )
    kv = swap([own_kv] * 4, QUERY_TILES)
    qb = swap([own_qb] * 4, KEY_TILES)

    ids = fine_scale.reshape(2, 2, 2, 2, 2, 2, PIECE)
    query_ids = lax.dynamic_index_in_dim(ids, place["zc"], 3, keepdims=False)
    query_ids = lax.dynamic_index_in_dim(query_ids, place["zb"], 3, keepdims=False)
    query_ids = query_ids.reshape(PIECES, 1, PIECE)
    key_ids = lax.dynamic_index_in_dim(ids, place["yh"], 1, keepdims=False)
    key_ids = lax.dynamic_index_in_dim(key_ids, place["yl"], 1, keepdims=False)
    key_ids = key_ids.reshape(PIECES, PIECE)
    lane = lax.broadcasted_iota(jnp.int32, (PIECES, PIECE, PIECE), 2)
    onehot = (lane - HEAD_SIZE == key_ids[:, :, None]).astype(BF16)
    seen = jnp.sum(key_ids[None, :, 0] <= query_ids[3::4, 0, -1:], axis=1)
    steps = ((seen + STEP - 1) // STEP).astype(jnp.int32)

    coarse_rows = [
        lax.dynamic_slice(array, (tile_of * 64, 0), (64, 256)).reshape(64, 4, HEAD_SIZE)
        for array in (key_coarse, value_coarse)
    ]
    kvc = jnp.concatenate(
        [lax.dynamic_index_in_dim(rows, head_of, 1, keepdims=False) for rows in coarse_rows], axis=1
    )

    bias = jnp.where(coarse_scale[:, None] <= coarse_scale[None, :], 0.0, -1e9).astype(F32)
    packed = call(
        packet_kernel, (shape(1216, 256),) * 4, [pltpu.VMEM((4, 480, 256), BF16)], 1,
        flops=2**28, moved=2**22, exps=2**18,
    )(placed, query_coarse, key_coarse, value_coarse, bias, out_weight, grad_coarse.T)
    kv, qb, packed, onehot, kvc, steps, query_ids = lax.optimization_barrier(
        (kv, qb, packed, onehot, kvc, steps, query_ids)
    )

    half = [pltpu.VMEM((PIECES, PIECE, PIECE), BF16)]
    accum, stats, *prepared = call(
        forward_kernel,
        (shape(QUERY_BLOCKS, HEAD_SIZE, QUERY_BLOCK, dtype=F32), shape(2, 8, QUERY_BLOCK, dtype=F32))
        + (shape(PIECES, PIECE, PIECE),) * 4,
        [
            pltpu.VMEM((QUERY_BLOCKS, PIECE, QUERY_BLOCK), BF16),
            pltpu.VMEM((2, STEP * PIECE, QUERY_BLOCK), F32),
            pltpu.VMEM((QUERY_BLOCKS, 8, QUERY_BLOCK), F32),
        ],
        2,
    )(placed, steps, *kv, onehot, kvc, *qb, query_ids)
    packets = swap(packed, "head")
    stats, packets[1] = lax.optimization_barrier((stats, packets[1]))
    all_stats = swap([stats] * 4, KEY_TILES)
    parts = call(
        backward_kernel,
        (shape(4, PIECE, PIECE),) * 4 + (shape(4 * PIECE + 64, PIECE),) * 4,
        half
        + [
            pltpu.VMEM((PIECES, PIECE, PIECE), F32),
            pltpu.VMEM((64, PIECE), F32),
            pltpu.VMEM((4 * QUERY_BLOCKS, 8, QUERY_BLOCK), F32),
        ],
        2, 10 * 2048 * 2112 * 64, 2**22, 2048 * 2112,
    )(placed, steps, *prepared, kvc, query_ids, accum, *all_stats)

    parts, packets = lax.optimization_barrier((parts, packets))
    dkv = swap(parts[4:], QUERY_TILES)
    od = swap(parts[:4], KEY_TILES)
    attended = call(attended_kernel, shape(4, HEAD_SIZE, PIECE), moved=2**20)(*od)
    attended = swap([attended] * 4, "head")
    mixed_coarse, dq_coarse, dk_coarse, dv_coarse = call(
        coarse_kernel,
        (shape(480, 256), shape(256, 256), shape(256, 256, dtype=F32), shape(256, 256, dtype=F32)),
        flops=2**29, moved=2**22, exps=2**19,
    )(query_coarse, key_coarse, value_coarse, bias, *packets, *weights)
    dkv, dk_coarse = lax.optimization_barrier((dkv, dk_coarse))
    dkv = call(key_sums_kernel, shape(4 * PIECE + 64, PIECE), flops=2**33, moved=2**24)(*dkv)
    sums = call(
        sums_kernel, (shape(512, PIECE),) * 4, [pltpu.VMEM((4, 448, PIECE), BF16)], 1, moved=2**21
    )(placed, *attended, *od, dkv)
    attended, dq_fine, dk_fine, dv_fine, coarse_part = call(
        heads_kernel,
        (shape(4, 256, PIECE),) + (shape(PIECE, 256),) * 3 + (shape(4, 64, PIECE),),
        [pltpu.VMEM((256, PIECE), F32), pltpu.VMEM((4, PIECE, PIECE), BF16)], 1, moved=2**20,
    )(placed, *swap(sums, HEADS))
    coarse_parts = swap([coarse_part] * 4, KEY_TILES)
    mixed_fine = call(mix_kernel, shape(480, PIECE), flops=2**27, moved=2**20)(attended, *packets)
    coarse_parts, mixed_fine = lax.optimization_barrier((coarse_parts, mixed_fine))
    dk_coarse, dv_coarse = call(
        last_kernel, (shape(256, 256), shape(256, 256)), (), 1, moved=2**20
    )(placed, *coarse_parts, dk_coarse, dv_coarse)
    return (
        mixed_fine.T, mixed_coarse.T, dq_fine, dk_fine, dv_fine, dq_coarse, dk_coarse, dv_coarse,
    )


def solution(mesh):
    fine_mesh = Mesh(mesh.devices.reshape(2, 2, 2, 2, 2, 2, 4), SEQ + ("head",))
    in_specs = (
        P(SEQ, "head"), P(SEQ, "head"), P(SEQ, "head"),
        P(None, "head"), P(None, "head"), P(None, "head"),
        P("head", None), P(SEQ, "head"), P(None, "head"), P(), P(),
    )
    out_specs = (
        P(SEQ, "head"), P(None, "head"),
        P(SEQ, "head"), P(SEQ, "head"), P(SEQ, "head"),
        P(None, "head"), P(None, "head"), P(None, "head"),
    )
    return jax.shard_map(
        on_device, mesh=fine_mesh, in_specs=in_specs, out_specs=out_specs, check_vma=False
    )
```

```python
import jax
import jax.numpy as jnp
from jax import lax
from jax.experimental import pallas as pl
from jax.experimental.pallas import tpu as pltpu
from jax.sharding import Mesh
from jax.sharding import PartitionSpec as P

HEAD_SIZE = 64
SCALE = HEAD_SIZE ** (-0.5)
FSCALES = 3
HIDE = -30000.0
PIECE = 128
PIECES = 16
QUERY_BLOCKS = 4
QUERY_BLOCK = 512
STEP = 2
F32 = jnp.float32
BF16 = jnp.bfloat16

SEQ = ("xh", "yh", "yl", "zc", "zb", "za")
HEADS = ("xh", "za")
QUERY_TILES = ("zc", "zb")
KEY_TILES = ("yh", "yl")


def product(left, right):
    return jnp.dot(left, right, preferred_element_type=F32)


def product_nt(left, right):
    return lax.dot_general(left, right, (((1,), (1,)), ((), ())), preferred_element_type=F32)


def product_tn(left, right):
    return lax.dot_general(left, right, (((0,), (0,)), ((), ())), preferred_element_type=F32)


def call(kernel, outs, scratch=(), smem=0, flops=0, moved=0, exps=0):
    def run(*operands):
        return pl.pallas_call(
            kernel,
            out_shape=outs,
            in_specs=[pl.BlockSpec(memory_space=pltpu.SMEM)] * smem
            + [pl.BlockSpec(memory_space=pltpu.VMEM)] * (len(operands) - smem),
            out_specs=jax.tree.map(lambda _: pl.BlockSpec(memory_space=pltpu.VMEM), outs),
            scratch_shapes=list(scratch),
            compiler_params=pltpu.CompilerParams(vmem_limit_bytes=48 * 2**20),
            cost_estimate=pl.CostEstimate(
                flops=flops, bytes_accessed=moved, transcendentals=exps
            ),
        )(*operands)

    return run


def shape(*dims, dtype=BF16):
    return jax.ShapeDtypeStruct(dims, dtype)


def weight_blocks_kernel(place_ref, weight_ref, *refs):
    outs, held = refs[:4], refs[4]
    for part in range(4):
        held[part] = weight_ref[:, part * 480:(part + 1) * 480]
    for partner in range(4):
        outs[partner][...] = held[place_ref[2] ^ partner]


def pack_kernel(place_ref, query_ref, key_ref, value_ref, *refs):
    grads, weights, outs, held = refs[:4], refs[4:8], refs[8:12], refs[12]
    back = sum(product(weight[...], grad[...]) for weight, grad in zip(weights, grads)).astype(BF16)
    query = (query_ref[...].astype(F32) * SCALE).T.astype(BF16)
    for head in range(4):
        part = slice(head * HEAD_SIZE, (head + 1) * HEAD_SIZE)
        held[head, :HEAD_SIZE] = query[part]
        held[head, HEAD_SIZE:PIECE] = back[part]
        held[head, PIECE:] = jnp.concatenate([key_ref[:, part], value_ref[:, part]], axis=1)
    for partner in range(4):
        outs[partner][...] = held[place_ref[0] ^ partner]


def own_head_kernel(place_ref, *refs):
    parts, (qb_ref, kv_ref) = refs[:4], refs[4:]
    for partner, part in enumerate(parts):
        source = place_ref[0] ^ partner
        qb_ref[source] = part[:PIECE, :]
        kv_ref[source] = part[PIECE:, :]


def key_piece(place_ref, source, partner):
    return 8 * (source // 2) + 2 * (place_ref[3] ^ partner) + source % 2


def prepare_queries(qb_refs, held):
    for part, ref in enumerate(qb_refs):
        for source in range(4):
            held[8 * (source // 2) + 2 * part + source % 2] = ref[source]


def prepare_keys(place_ref, kv_refs, onehot_ref, masked_keys, plain, turned):
    lane = lax.broadcasted_iota(jnp.int32, (PIECE, PIECE), 1)
    for partner, ref in enumerate(kv_refs):
        for source in range(4):
            piece = key_piece(place_ref, source, partner)
            both = ref[source]
            masked_keys[piece] = jnp.where(lane < HEAD_SIZE, both, onehot_ref[piece])
            turned[piece] = both.astype(F32).T.astype(BF16)
            plain[piece] = both


def query_pieces(held, block):
    return jnp.concatenate([held[4 * block + part] for part in range(4)], axis=1)


def query_side(place_ref, held, ids_ref, block):
    both = query_pieces(held, block)
    own = 8 * (block // 2) if isinstance(block, int) else 8 * (block >> 1)
    first = own + 4 * ((place_ref[1] >> 1) ^ (block & 1))
    ids = jnp.concatenate(
        [ids_ref[first + 2 * ((place_ref[1] & 1) ^ (part // 2)) + part % 2] for part in range(4)], axis=1
    )
    row = lax.broadcasted_iota(jnp.int32, (HEAD_SIZE, QUERY_BLOCK), 0)
    hidden = (row > ids) & (row < FSCALES)
    penalty = jnp.where(hidden, HIDE, 0.0).astype(BF16)
    return both, jnp.concatenate([both[:HEAD_SIZE], penalty], axis=0)


def rows_of(ref, step, size=STEP):
    return ref[pl.ds(size * step, size)].reshape(size * PIECE, PIECE)


def turned_of(ref, step, first, size=STEP):
    return jnp.concatenate(
        [ref[size * step + part, first:first + HEAD_SIZE, :] for part in range(size)], axis=1
    )


def coarse_side(kvc_ref):
    both = kvc_ref[...]
    lane = lax.broadcasted_iota(jnp.int32, both.shape, 1)
    only_keys = jnp.where(lane < HEAD_SIZE, both, jnp.zeros_like(both))
    return both, only_keys, both.astype(F32).T.astype(BF16)


def forward_kernel(
    place_ref, steps_ref, kv0, kv1, kv2, kv3, onehot_ref, kvc_ref, qb0, qb1, qb2, qb3, ids_ref,
    out_ref, packed_ref, masked_keys, plain, turned, query_held, queries_held, scores_held, stats_ref,
):
    prepare_keys(place_ref, (kv0, kv1, kv2, kv3), onehot_ref, masked_keys, plain, turned)
    prepare_queries((qb0, qb1, qb2, qb3), query_held)
    _, coarse_keys, coarse_turned = coarse_side(kvc_ref)
    for block in range(QUERY_BLOCKS):
        _, queries = query_side(place_ref, query_held, ids_ref, block)
        queries_held[block] = queries
        scores = product(coarse_keys, queries)
        top = jnp.max(scores, axis=0, keepdims=True)
        probs = jnp.exp(scores - top)
        total = jnp.sum(probs, axis=0, keepdims=True)
        out_ref[block] = product(coarse_turned[HEAD_SIZE:], probs.astype(BF16))
        stats_ref[block] = jnp.concatenate([top, total, jnp.zeros((6, QUERY_BLOCK), F32)], axis=0)

    def one_block(block, _):
        queries = queries_held[block]
        steps = steps_ref[block ^ (place_ref[1] >> 1)]
        last = steps - 1
        scores_held[0] = product(rows_of(masked_keys, 0), queries)

        def one_step(step, carried):
            top, total, accum = carried
            slot = step & 1
            scores = scores_held[slot]
            scores_held[1 - slot] = product(rows_of(masked_keys, jnp.minimum(step + 1, last)), queries)
            new_top = jnp.maximum(top, jnp.max(scores, axis=0, keepdims=True))
            fade = jnp.exp(top - new_top)
            probs = jnp.exp(scores - new_top)
            total = total * fade + jnp.sum(probs, axis=0, keepdims=True)
            accum = accum * fade + product(turned_of(turned, step, HEAD_SIZE), probs.astype(BF16))
            return new_top, total, accum

        start = stats_ref[block]
        top, total, accum = lax.fori_loop(
            0, steps, one_step, (start[0:1], start[1:2], out_ref[block])
        )
        back = query_pieces(query_held, block)[HEAD_SIZE:]
        offset = jnp.sum(back.astype(F32) * accum, axis=0, keepdims=True)
        out_ref[block] = accum
        stats_ref[block] = jnp.concatenate(
            [top, total, offset, jnp.zeros((5, QUERY_BLOCK), F32)], axis=0
        )
        return 0

    lax.fori_loop(0, QUERY_BLOCKS, one_block, 0)
    for pair in range(2):
        packed_ref[pair] = jnp.concatenate([stats_ref[2 * pair, :4, :], stats_ref[2 * pair + 1, :4, :]], axis=0)


def backward_kernel(
    place_ref, steps_ref, masked_keys, plain, turned, query_held, kvc_ref, ids_ref, accum_ref,
    stats0, stats1, stats2, stats3, od0, od1, od2, od3, dkv0, dkv1, dkv2, dkv3,
    out_held, key_sums, coarse_sums, stats_held,
):
    for partner, ref in enumerate((stats0, stats1, stats2, stats3)):
        for block in range(QUERY_BLOCKS):
            rows = slice(4 * (block % 2), 4 * (block % 2) + 4)
            stats_held[4 * partner + block, :4, :] = ref[block // 2, rows, :]
    coarse_both, coarse_keys, coarse_turned = coarse_side(kvc_ref)
    key_sums[...] = jnp.zeros_like(key_sums)
    coarse_sums[...] = jnp.zeros_like(coarse_sums)

    def one_block(block, _):
        both, queries = query_side(place_ref, query_held, ids_ref, block)
        own = stats_held[block]
        stats = [own]
        for partner in (1, 2, 3):
            theirs = stats_held[4 * partner + (block ^ (partner // 2))]
            flip = 2 * (partner % 2)
            parts = [theirs[:, (part ^ flip) * PIECE:((part ^ flip) + 1) * PIECE] for part in range(4)]
            stats.append(jnp.concatenate(parts, axis=1))
        top = stats[0][0:1]
        for other in stats[1:]:
            top = jnp.maximum(top, other[0:1])
        total = jnp.zeros_like(top)
        offset = jnp.zeros_like(top)
        for other in stats:
            fade = jnp.exp(other[0:1] - top)
            total = total + fade * other[1:2]
            offset = offset + fade * other[2:3]
        offset = offset / total
        log_total = top + jnp.log(total)
        attended = accum_ref[block] * (jnp.exp(own[0:1] - top) / total)
        back = jnp.concatenate(
            [jnp.zeros((HEAD_SIZE, QUERY_BLOCK), BF16), both[HEAD_SIZE:]], axis=0
        )
        token_rows = both.astype(F32).T
        lane = lax.broadcasted_iota(jnp.int32, token_rows.shape, 1)
        query_rows = jnp.where(lane < HEAD_SIZE, token_rows, 0.0).astype(BF16)
        back_rows = jnp.where(lane < HEAD_SIZE, 0.0, token_rows).astype(BF16)

        def terms(only_keys, key_value, key_turned):
            probs = jnp.exp(product(only_keys, queries) - log_total)
            grad_probs = product(key_value, back)
            grad_scores = (probs * (grad_probs - offset)).astype(BF16)
            key_side = product(grad_scores, query_rows) + product(probs.astype(BF16), back_rows)
            return product(key_turned, grad_scores), key_side

        query_grad, coarse_term = terms(coarse_keys, coarse_both, coarse_turned[:HEAD_SIZE])
        coarse_sums[...] += coarse_term

        def one_step(step, query_grad):
            query_term, key_side = terms(
                rows_of(masked_keys, step, 4), rows_of(plain, step, 4), turned_of(turned, step, 0, 4)
            )
            key_sums[pl.ds(4 * step, 4)] += key_side.reshape(4, PIECE, PIECE)
            return query_grad + query_term

        steps = lax.div(steps_ref[block ^ (place_ref[1] >> 1)] + 1, 2)
        query_grad = lax.fori_loop(0, steps, one_step, query_grad)
        both_out = jnp.concatenate([attended, query_grad * SCALE], axis=0).astype(BF16)
        for part in range(4):
            out_held[4 * block + part] = both_out[:, part * PIECE:(part + 1) * PIECE]
        return 0

    lax.fori_loop(0, QUERY_BLOCKS, one_block, 0)
    for part, ref in enumerate((od0, od1, od2, od3)):
        for source in range(4):
            ref[source] = out_held[8 * (source // 2) + 2 * part + source % 2]
    coarse = coarse_sums[...].astype(BF16)
    for partner, ref in enumerate((dkv0, dkv1, dkv2, dkv3)):
        for source in range(4):
            piece = key_sums[key_piece(place_ref, source, partner)]
            ref[source * PIECE:(source + 1) * PIECE, :] = piece.astype(BF16)
        ref[4 * PIECE:, :] = coarse


def coarse_probs(query, key, bias):
    scores = product_nt(key, query) + bias
    top = jnp.max(scores, axis=0, keepdims=True)
    total = jnp.sum(jnp.exp(scores - top), axis=0, keepdims=True)
    return jnp.exp(scores - (top + jnp.log(total)))


def head_columns(ref, head):
    return ref[:, head * HEAD_SIZE:(head + 1) * HEAD_SIZE]


def packet_kernel(place_ref, query_ref, key_ref, value_ref, bias_ref, weight_ref, grad_ref, *refs):
    outs, held = refs[:4], refs[4]
    for part in range(4):
        held[part] = weight_ref[:, part * 480:(part + 1) * 480].astype(F32).T.astype(BF16)
    attended = []
    for head in range(4):
        query = (head_columns(query_ref, head).astype(F32) * SCALE).astype(BF16)
        probs = coarse_probs(query, head_columns(key_ref, head), bias_ref[...])
        attended.append(product_tn(head_columns(value_ref, head), probs.astype(BF16)).astype(BF16))
    attended = jnp.concatenate(attended, axis=0)
    for partner in range(4):
        outs[partner][:480, :] = held[place_ref[2] ^ partner]
        outs[partner][480:960, :] = grad_ref[...]
        outs[partner][960:, :] = attended


def coarse_kernel(query_ref, key_ref, value_ref, bias_ref, *refs):
    packets, weights, (mixed_ref, dq_ref, dk_ref, dv_ref) = refs[:4], refs[4:8], refs[8:]
    back_all = sum(
        product(weight[...], packet[480:960, :]) for weight, packet in zip(weights, packets)
    ).astype(BF16)
    mixed_ref[...] = sum(product(packet[:480, :], packet[960:, :]) for packet in packets).astype(BF16)
    query_grads, key_grads, value_grads = [], [], []
    for head in range(4):
        part = slice(head * HEAD_SIZE, (head + 1) * HEAD_SIZE)
        query = (query_ref[:, part].astype(F32) * SCALE).astype(BF16)
        key, value, back = key_ref[:, part], value_ref[:, part], back_all[part]
        probs = coarse_probs(query, key, bias_ref[...])
        rounded = probs.astype(BF16)
        attended = packets[0][960 + part.start:960 + part.stop, :]
        offset = jnp.sum(back.astype(F32) * attended.astype(F32), axis=0, keepdims=True)
        grad_scores = (probs * (product(value, back) - offset)).astype(BF16)
        query_grads.append(product_tn(key, grad_scores) * SCALE)
        key_grads.append(product(grad_scores, query))
        value_grads.append(product_nt(rounded, back))
    dq_ref[...] = jnp.concatenate(query_grads, axis=0).T.astype(BF16)
    dk_ref[...] = jnp.concatenate(key_grads, axis=1)
    dv_ref[...] = jnp.concatenate(value_grads, axis=1)


def attended_kernel(*refs):
    parts, out_ref = refs[:4], refs[4]
    for source in range(4):
        total = sum(part[source, :HEAD_SIZE, :].astype(F32) for part in parts)
        out_ref[source] = total.astype(BF16)


def key_sums_kernel(*refs):
    refs[4][...] = sum(part[...].astype(F32) for part in refs[:4]).astype(BF16)


def sums_kernel(place_ref, *refs):
    attended, od, dkv, outs, held = refs[:4], refs[4:8], refs[8], refs[9:13], refs[13]
    for source in range(4):
        rows = slice(source * PIECE, (source + 1) * PIECE)
        for part in range(4):
            held[source, part * HEAD_SIZE:(part + 1) * HEAD_SIZE] = attended[part][source]
        held[source, 256:320] = sum(part[source, HEAD_SIZE:, :].astype(F32) for part in od).astype(BF16)
        held[source, 320:] = dkv[rows, :]
    coarse = dkv[4 * PIECE:, :]
    for partner in range(4):
        outs[partner][:448, :] = held[place_ref[0] ^ partner]
        outs[partner][448:, :] = coarse


def heads_kernel(place_ref, *refs):
    parts, (att_ref, dq_ref, dk_ref, dv_ref, coarse_ref, query_held, key_held) = refs[:4], refs[4:]
    for partner, part in enumerate(parts):
        head = place_ref[0] ^ partner
        rows = pl.ds(pl.multiple_of(head * HEAD_SIZE, HEAD_SIZE), HEAD_SIZE)
        for group in range(4):
            att_ref[group, rows, :] = part[group * HEAD_SIZE:(group + 1) * HEAD_SIZE, :]
        query_held[rows, :] = part[256:320, :].astype(F32)
        key_held[head] = part[320:448, :]
        coarse_ref[head] = part[448:, :]
    dq_ref[...] = query_held[...].T.astype(BF16)
    dk_ref[...] = jnp.concatenate([key_held[head, :, :HEAD_SIZE] for head in range(4)], axis=1)
    dv_ref[...] = jnp.concatenate([key_held[head, :, HEAD_SIZE:] for head in range(4)], axis=1)


def mix_kernel(att_ref, *refs):
    packets, mixed_ref = refs[:4], refs[4]
    mixed_ref[...] = sum(
        product(packet[:480, :], att_ref[group]) for group, packet in enumerate(packets)
    ).astype(BF16)


def last_kernel(place_ref, *refs):
    received, (dk_ref, dv_ref, dk_out, dv_out) = refs[:4], refs[4:]
    for partner, ref in enumerate(received):
        rows = pl.ds(pl.multiple_of((place_ref[1] ^ partner) * 64, 64), 64)
        parts = [ref[head].astype(F32) for head in range(4)]
        keys = jnp.concatenate([part[:, :HEAD_SIZE] for part in parts], axis=1)
        values = jnp.concatenate([part[:, HEAD_SIZE:] for part in parts], axis=1)
        dk_out[rows, :] = (dk_ref[rows, :] + keys).astype(BF16)
        dv_out[rows, :] = (dv_ref[rows, :] + values).astype(BF16)


def swap(arrays, axes):
    out = [arrays[0]]
    sent = {
        partner: lax.ppermute(arrays[partner], axes, [(i, i ^ partner) for i in range(4)])
        for partner in (1, 3, 2)
    }
    return out + [sent[1], sent[2], sent[3]]


def on_device(
    query_fine, key_fine, value_fine, query_coarse, key_coarse, value_coarse,
    out_weight, grad_fine, grad_coarse, fine_scale, coarse_scale,
):
    place = {name: lax.axis_index(name) for name in SEQ}
    head_of = place["xh"] * 2 + place["za"]
    tile_of = place["yh"] * 2 + place["yl"]
    placed = jnp.stack(
        [head_of, tile_of, lax.axis_index("head"), place["zc"] * 2 + place["zb"]]
    ).astype(jnp.int32)

    grads = swap([grad_fine.T] * 4, "head")
    weights = call(
        weight_blocks_kernel, (shape(256, 480),) * 4, [pltpu.VMEM((4, 256, 480), BF16)], 1, moved=2**21
    )(placed, out_weight)
    packed = call(
        pack_kernel, (shape(2 * PIECE, PIECE),) * 4, [pltpu.VMEM((4, 2 * PIECE, PIECE), BF16)], 1,
        flops=2 * 128 * 256 * 1920, moved=2**21,
    )(placed, query_fine, key_fine, value_fine, *grads, *weights)
    own_qb, own_kv = call(own_head_kernel, (shape(4, PIECE, PIECE),) * 2, (), 1, moved=2**19)(
        placed, *swap(packed, HEADS)
    )
    kv = swap([own_kv] * 4, QUERY_TILES)
    qb = swap([own_qb] * 4, KEY_TILES)

    ids = fine_scale.reshape(2, 2, 2, 2, 2, 2, PIECE)
    query_ids = lax.dynamic_index_in_dim(ids, place["zc"], 3, keepdims=False)
    query_ids = lax.dynamic_index_in_dim(query_ids, place["zb"], 3, keepdims=False)
    query_ids = query_ids.reshape(PIECES, 1, PIECE)
    key_ids = lax.dynamic_index_in_dim(ids, place["yh"], 1, keepdims=False)
    key_ids = lax.dynamic_index_in_dim(key_ids, place["yl"], 1, keepdims=False)
    key_ids = key_ids.reshape(PIECES, PIECE)
    lane = lax.broadcasted_iota(jnp.int32, (PIECES, PIECE, PIECE), 2)
    onehot = (lane - HEAD_SIZE == key_ids[:, :, None]).astype(BF16)
    seen = jnp.sum(key_ids[None, :, 0] <= query_ids[3::4, 0, -1:], axis=1)
    steps = ((seen + STEP - 1) // STEP).astype(jnp.int32)

    coarse_rows = [
        lax.dynamic_slice(array, (tile_of * 64, 0), (64, 256)).reshape(64, 4, HEAD_SIZE)
        for array in (key_coarse, value_coarse)
    ]
    kvc = jnp.concatenate(
        [lax.dynamic_index_in_dim(rows, head_of, 1, keepdims=False) for rows in coarse_rows], axis=1
    )

    bias = jnp.where(coarse_scale[:, None] <= coarse_scale[None, :], 0.0, -1e9).astype(F32)
    packed = call(
        packet_kernel, (shape(1216, 256),) * 4, [pltpu.VMEM((4, 480, 256), BF16)], 1,
        flops=2**28, moved=2**22, exps=2**18,
    )(placed, query_coarse, key_coarse, value_coarse, bias, out_weight, grad_coarse.T)
    kv = [kv[0], kv[1], kv[3], kv[2]]
    kv, qb, packed, onehot, kvc, steps, query_ids = lax.optimization_barrier(
        (kv, qb, packed, onehot, kvc, steps, query_ids)
    )
    kv = [kv[0], kv[1], kv[3], kv[2]]

    half = [pltpu.VMEM((PIECES, PIECE, PIECE), BF16)]
    accum, stats, *prepared = call(
        forward_kernel,
        (shape(QUERY_BLOCKS, HEAD_SIZE, QUERY_BLOCK, dtype=F32), shape(2, 8, QUERY_BLOCK, dtype=F32))
        + (shape(PIECES, PIECE, PIECE),) * 4,
        [
            pltpu.VMEM((QUERY_BLOCKS, PIECE, QUERY_BLOCK), BF16),
            pltpu.VMEM((2, STEP * PIECE, QUERY_BLOCK), F32),
            pltpu.VMEM((QUERY_BLOCKS, 8, QUERY_BLOCK), F32),
        ],
        2,
    )(placed, steps, *kv, onehot, kvc, *qb, query_ids)
    packets = swap(packed, "head")
    stats, packets[1] = lax.optimization_barrier((stats, packets[1]))
    all_stats = swap([stats] * 4, KEY_TILES)
    parts = call(
        backward_kernel,
        (shape(4, PIECE, PIECE),) * 4 + (shape(4 * PIECE + 64, PIECE),) * 4,
        half
        + [
            pltpu.VMEM((PIECES, PIECE, PIECE), F32),
            pltpu.VMEM((64, PIECE), F32),
            pltpu.VMEM((4 * QUERY_BLOCKS, 8, QUERY_BLOCK), F32),
        ],
        2, 10 * 2048 * 2112 * 64, 2**22, 2048 * 2112,
    )(placed, steps, *prepared, kvc, query_ids, accum, *all_stats)

    parts, packets = lax.optimization_barrier((parts, packets))
    dkv = swap(parts[4:], QUERY_TILES)
    dkv = [dkv[0], dkv[2], dkv[3], dkv[1]]
    od = swap(parts[:4], KEY_TILES)
    attended = call(attended_kernel, shape(4, HEAD_SIZE, PIECE), moved=2**20)(*od)
    attended = swap([attended] * 4, "head")
    mixed_coarse, dq_coarse, dk_coarse, dv_coarse = call(
        coarse_kernel,
        (shape(480, 256), shape(256, 256), shape(256, 256, dtype=F32), shape(256, 256, dtype=F32)),
        flops=2**29, moved=2**22, exps=2**19,
    )(query_coarse, key_coarse, value_coarse, bias, *packets, *weights)
    dkv, dk_coarse = lax.optimization_barrier((dkv, dk_coarse))
    dkv = call(key_sums_kernel, shape(4 * PIECE + 64, PIECE), flops=2**33, moved=2**24)(*dkv)
    sums = call(
        sums_kernel, (shape(512, PIECE),) * 4, [pltpu.VMEM((4, 448, PIECE), BF16)], 1, moved=2**21
    )(placed, *attended, *od, dkv)
    attended, dq_fine, dk_fine, dv_fine, coarse_part = call(
        heads_kernel,
        (shape(4, 256, PIECE),) + (shape(PIECE, 256),) * 3 + (shape(4, 64, PIECE),),
        [pltpu.VMEM((256, PIECE), F32), pltpu.VMEM((4, PIECE, PIECE), BF16)], 1, moved=2**20,
    )(placed, *swap(sums, HEADS))
    coarse_parts = swap([coarse_part] * 4, KEY_TILES)
    mixed_fine = call(mix_kernel, shape(480, PIECE), flops=2**27, moved=2**20)(attended, *packets)
    coarse_parts, mixed_fine = lax.optimization_barrier((coarse_parts, mixed_fine))
    dk_coarse, dv_coarse = call(
        last_kernel, (shape(256, 256), shape(256, 256)), (), 1, moved=2**20
    )(placed, *coarse_parts, dk_coarse, dv_coarse)
    return (
        mixed_fine.T, mixed_coarse.T, dq_fine, dk_fine, dv_fine, dq_coarse, dk_coarse, dv_coarse,
    )


def solution(mesh):
    fine_mesh = Mesh(mesh.devices.reshape(2, 2, 2, 2, 2, 2, 4), SEQ + ("head",))
    in_specs = (
        P(SEQ, "head"), P(SEQ, "head"), P(SEQ, "head"),
        P(None, "head"), P(None, "head"), P(None, "head"),
        P("head", None), P(SEQ, "head"), P(None, "head"), P(), P(),
    )
    out_specs = (
        P(SEQ, "head"), P(None, "head"),
        P(SEQ, "head"), P(SEQ, "head"), P(SEQ, "head"),
        P(None, "head"), P(None, "head"), P(None, "head"),
    )
    return jax.shard_map(
        on_device, mesh=fine_mesh, in_specs=in_specs, out_specs=out_specs, check_vma=False
    )
```
